32 devices in a mesh: seq: 8 (over y, x, core), tp: 4 (over z).
Axes of the slice: x: 2, y: 2, z: 4, core: 2. Of those that a mesh axis runs over, the one named last changes fastest.
Arguments:
- stream: bfloat16 [2048, 1600], P(('seq', 'tp')), may hold values from -6 to 6
- cotangent: bfloat16 [2048, 1600], P(('seq', 'tp')), may hold values from -6 to 6
- segments: int32 [2048], replicated, may hold values from 0 to 4, as said below
- mixer_gain: float32 [1600], replicated, may hold values from 0.5 to 1.5
- query_weight: bfloat16 [1600, 1600], P(None, 'tp'), may hold values from -0.15625 to 0.15625
- key_weight: bfloat16 [1600, 320], P(None, 'tp'), may hold values from -0.15625 to 0.15625
- value_weight: bfloat16 [1600, 320], P(None, 'tp'), may hold values from -0.15625 to 0.15625
- output_weight: bfloat16 [1600, 1600], P(None, 'tp'), may hold values from -0.15625 to 0.15625
- attn_gain: float32 [1600], replicated, may hold values from 0.5 to 1.5
- mamba_gain: float32 [1600], replicated, may hold values from 0.5 to 1.5
- inner_proj: bfloat16 [1600, 3200], P('seq', 'tp'), may hold values from -0.15625 to 0.15625
- inner_gate: bfloat16 [1600, 3200], P('seq', 'tp'), may hold values from -0.15625 to 0.15625
- conv_kernel: float32 [4, 3200], P(None, 'tp'), may hold values from -3 to 3
- conv_bias: float32 [3200], P('tp'), may hold values from -0.5 to 0.5
- select_weight: bfloat16 [3200, 132], P('tp'), may hold values from -0.109375 to 0.109375
- step_weight: float32 [100, 3200], P(None, 'tp'), may hold values from -0.625 to 0.625
- step_bias: float32 [3200], P('tp'), may hold values from -9 to -2
- decay_log: float32 [3200, 16], P('tp'), may hold values from 0 to 2.8
- skip_scale: float32 [3200], P('tp'), may hold values from 0.5 to 1.5
- mamba_out: bfloat16 [1600, 3200], P('seq', 'tp'), may hold values from -0.109375 to 0.109375
- ffn_gain: float32 [1600], replicated, may hold values from 0.5 to 1.5
- ffn_gate: bfloat16 [1600, 5504], P('seq', 'tp'), may hold values from -0.15625 to 0.15625
- ffn_up: bfloat16 [1600, 5504], P('seq', 'tp'), may hold values from -0.15625 to 0.15625
- ffn_down: bfloat16 [1600, 5504], P('seq', 'tp'), may hold values from -0.078125 to 0.078125
Outputs:
- layer_out: bfloat16 [2048, 1600], P(('seq', 'tp'))
- stream_grad: bfloat16 [2048, 1600], P(('seq', 'tp'))
- mixer_gain_grad: float32 [1600], replicated
- query_weight_grad: float32 [1600, 1600], P(None, 'tp')
- key_weight_grad: float32 [1600, 320], P(None, 'tp')
- value_weight_grad: float32 [1600, 320], P(None, 'tp')
- output_weight_grad: float32 [1600, 1600], P(None, 'tp')
- attn_gain_grad: float32 [1600], replicated
- mamba_gain_grad: float32 [1600], replicated
- inner_proj_grad: float32 [1600, 3200], P('seq', 'tp')
- inner_gate_grad: float32 [1600, 3200], P('seq', 'tp')
- conv_kernel_grad: float32 [4, 3200], P(None, 'tp')
- conv_bias_grad: float32 [3200], P('tp')
- select_weight_grad: float32 [3200, 132], P('tp')
- step_weight_grad: float32 [100, 3200], P(None, 'tp')
- step_bias_grad: float32 [3200], P('tp')
- decay_log_grad: float32 [3200, 16], P('tp')
- skip_scale_grad: float32 [3200], P('tp')
- mamba_out_grad: float32 [1600, 3200], P('seq', 'tp')
- ffn_gain_grad: float32 [1600], replicated
- ffn_gate_grad: float32 [1600, 5504], P('seq', 'tp')
- ffn_up_grad: float32 [1600, 5504], P('seq', 'tp')
- ffn_down_grad: float32 [1600, 5504], P('seq', 'tp')
The draws below stay inside these ranges and needn't reach their ends.
Inputs may be any that keep to these rules, and one draw needn't show every extreme that they name: `segments`: segment numbers start at 0, never fall, and rise by one at each document start. The stream holds five documents. Counting positions from 0, the middle one (number 2) begins at a position from 2 to 128, and its last token is at a position from 1919 to 2045.
All inputs are finite; a program needn't handle non-finite values.
Results may differ from the reference program's by a relative error of at most 0.018.
Values may be sent and summed in bfloat16 or wider, within the bound.
No kernel may reach another device: no remote copies, remote signals or barrier semaphores. Data moves between devices by JAX's collectives and lax.ppermute only.
A program may use at most 256 MiB of HBM per device.

```python
import math
from functools import partial
import jax
import jax.numpy as jnp
from jax import lax

D = 1600
HEADS = 25
KV_HEADS = 5
HEAD_DIM = 64
INNER = 3200
STATE = 16
CONV = 4
STEP_RANK = 100
FF = 5504
WINDOW = 1024
SCAN_BLOCK = 64
TOK_DEV = 256
TOKENS = 2048


def draw_segments(key, part):
    key = jax.random.fold_in(key, 11)
    keys = jax.random.split(key, 4)
    half = TOK_DEV // 2
    head = jax.random.randint(keys[0], (), 2, half + 1)
    first_cut = jax.random.randint(keys[1], (), 1, head)
    tail = jax.random.randint(keys[2], (), 2, half + 1)
    finish = TOKENS - tail
    second_cut = finish + jax.random.randint(keys[3], (), 1, tail)
    place = jnp.arange(TOKENS, dtype=jnp.int32)
    marks = (place >= first_cut).astype(jnp.int32) + (place >= head).astype(jnp.int32)
    marks = marks + (place >= finish).astype(jnp.int32) + (place >= second_cut).astype(jnp.int32)
    return marks.astype(jnp.int32)


def level_of(stream_key, shape, cuts, low, largest):
    loudness, own = 1.0, jax.random.fold_in(stream_key, 6)
    for position, parts in cuts:
        heights = jnp.exp(jax.random.uniform(jax.random.fold_in(own, position), (parts,), jnp.float32, low / len(cuts), largest / len(cuts)))
        loudness = loudness * jnp.repeat(heights, shape[position] // parts).reshape([-1 if axis == position else 1 for axis in range(len(shape))])
    return loudness


def bell_draw(rng, dims, scale, reach, cuts=(), held_as=jnp.bfloat16):
    values = jax.random.normal(rng, dims, jnp.float32) * scale
    if len(cuts) > 0:
        values = level_of(rng, dims, cuts, -0.22, 0.18) * values
    return jnp.clip(values, min=-reach, max=reach).astype(held_as)


def setup_inputs(seed: int = 0) -> dict:
    key_of = jax.random.split(jax.random.key(seed), 25)
    stream = bell_draw(key_of[0], (TOKENS, D), 1.0, 6.0, ((0, 32),))
    cotangent = bell_draw(key_of[1], (TOKENS, D), 1.0, 6.0, ((0, 32),))
    segments = draw_segments(jax.random.fold_in(key_of[24], 71), 0)
    mixer_gain = jnp.clip(1.0 + 0.1 * jax.random.normal(key_of[3], (D,), jnp.float32), 0.5, 1.5)
    query_weight = bell_draw(key_of[4], (D, HEADS * HEAD_DIM), D ** -0.5, 0.15625, ((1, 4),))
    key_weight = bell_draw(key_of[5], (D, KV_HEADS * HEAD_DIM), D ** -0.5, 0.15625, ((1, 4),))
    value_weight = bell_draw(key_of[6], (D, KV_HEADS * HEAD_DIM), D ** -0.5, 0.15625, ((1, 4),))
    output_weight = bell_draw(key_of[7], (D, HEADS * HEAD_DIM), (HEADS * HEAD_DIM) ** -0.5, 0.15625, ((1, 4),))
    attn_gain = jnp.clip(1.0 + 0.1 * jax.random.normal(key_of[8], (D,), jnp.float32), 0.5, 1.5)
    mamba_gain = jnp.clip(1.0 + 0.1 * jax.random.normal(key_of[9], (D,), jnp.float32), 0.5, 1.5)
    inner_proj = bell_draw(key_of[10], (D, INNER), D ** -0.5, 0.15625, ((0, 8), (1, 4)))
    inner_gate = bell_draw(key_of[11], (D, INNER), D ** -0.5, 0.15625, ((0, 8), (1, 4)))
    conv_kernel = bell_draw(key_of[12], (CONV, INNER), CONV ** -0.5, 3.0, ((1, 4),), jnp.float32)
    conv_bias = jnp.clip(jax.random.uniform(key_of[13], (INNER,), jnp.float32, -0.5, 0.5) * level_of(key_of[13], (INNER,), ((0, 4),), -0.4, 0.0), -0.5, 0.5)
    select_weight = bell_draw(key_of[14], (INNER, STEP_RANK + 2 * STATE), INNER ** -0.5, 0.109375, ((0, 4),))
    step_weight = bell_draw(key_of[15], (STEP_RANK, INNER), STEP_RANK ** -0.5, 0.625, ((1, 4),), jnp.float32)
    step_bias = jnp.clip(-9.0 + 7.0 * jax.random.uniform(key_of[16], (INNER,), jnp.float32) ** level_of(key_of[16], (INNER,), ((0, 4),), -0.2, 0.2), -9.0, -2.0)
    decay_log = jnp.clip(2.8 * jax.random.uniform(key_of[17], (INNER, STATE), jnp.float32) ** level_of(key_of[17], (INNER, STATE), ((0, 4),), -0.2, 0.2), 0.0, 2.8)
    skip_scale = jnp.clip(0.5 + 1.0 * jax.random.uniform(key_of[18], (INNER,), jnp.float32) ** level_of(key_of[18], (INNER,), ((0, 4),), -0.2, 0.2), 0.5, 1.5)
    mamba_out = bell_draw(key_of[19], (D, INNER), INNER ** -0.5, 0.109375, ((0, 8), (1, 4)))
    ffn_gain = jnp.clip(1.0 + 0.1 * jax.random.normal(key_of[20], (D,), jnp.float32), 0.5, 1.5)
    ffn_gate = bell_draw(key_of[21], (D, FF), D ** -0.5, 0.15625, ((0, 8), (1, 4)))
    ffn_up = bell_draw(key_of[22], (D, FF), D ** -0.5, 0.15625, ((0, 8), (1, 4)))
    ffn_down = bell_draw(key_of[23], (D, FF), FF ** -0.5, 0.078125, ((0, 8), (1, 4)))
    return dict(stream=stream, cotangent=cotangent, segments=segments, mixer_gain=mixer_gain, query_weight=query_weight, key_weight=key_weight, value_weight=value_weight, output_weight=output_weight, attn_gain=attn_gain, mamba_gain=mamba_gain, inner_proj=inner_proj, inner_gate=inner_gate, conv_kernel=conv_kernel, conv_bias=conv_bias, select_weight=select_weight, step_weight=step_weight, step_bias=step_bias, decay_log=decay_log, skip_scale=skip_scale, mamba_out=mamba_out, ffn_gain=ffn_gain, ffn_gate=ffn_gate, ffn_up=ffn_up, ffn_down=ffn_down)


@jax.custom_vjp
def low(v):
    return lax.optimization_barrier(v.astype(jnp.bfloat16)).astype(jnp.float32)

@jax.custom_vjp
def low_back(v):
    return v

def low_keep(v):
    return (low(v), None)

def low_pass(kept, grad):
    return (grad,)

def back_keep(v):
    return (v, None)

def back_low(kept, grad):
    return (low(grad),)
low.defvjp(low_keep, low_pass)
low_back.defvjp(back_keep, back_low)
EPS = 1e-06
HIGH = lax.Precision.HIGHEST

def rounded(value):
    return low_back(low(value))

def matmul(left, right):
    return jnp.dot(left, right, precision=HIGH)

def matmul_t(left, right):
    return jnp.dot(left, right.T, precision=HIGH)

def normed(value):
    return value * lax.rsqrt(lax.optimization_barrier(jnp.mean(value * value, -1, keepdims=True)) + EPS)

def link(earlier, later):
    return (earlier[0] * later[0], later[0] * earlier[1] + later[1])

def selective(state, step_size, inputs, entry, readout, alive, decay, block):
    total = step_size.shape[0]
    count = total // block
    width = step_size.shape[1]

    def advance(carry, pieces):
        step_blk, input_blk, entry_blk, read_blk, alive_blk = pieces
        factor = jnp.exp(step_blk[:, :, None] * decay[None]) * alive_blk[:, None, None]
        source = (step_blk * input_blk)[:, :, None] * entry_blk[:, None, :]
        cumulative, states = lax.associative_scan(link, (factor, source), axis=0)
        states = states + cumulative * carry[None]
        output = jnp.einsum('ten,tn->te', states, read_blk, precision=HIGH)
        return (states[-1], output)
    pieces = (step_size.reshape(count, block, width), inputs.reshape(count, block, width), entry.reshape(count, block, -1), readout.reshape(count, block, -1), alive.reshape(count, block))
    last, outputs = lax.scan(jax.checkpoint(advance), state, pieces)
    return (outputs.reshape(total, width), last)

def attention(queries, keys, values, segments):
    total = queries.shape[0]
    block = math.gcd(512, total)
    groups = HEADS // KV_HEADS
    key_width = KV_HEADS * HEAD_DIM
    key_pad = jnp.concatenate([jnp.zeros((WINDOW, key_width), jnp.float32), keys], 0)
    value_pad = jnp.concatenate([jnp.zeros((WINDOW, key_width), jnp.float32), values], 0)
    seg_pad = jnp.concatenate([jnp.full((WINDOW,), -1, jnp.int32), segments])

    def one_block(start):
        query_heads = lax.dynamic_slice_in_dim(queries, start, block, 0).reshape(block, KV_HEADS, groups, HEAD_DIM)
        key_heads = lax.dynamic_slice_in_dim(key_pad, start, block + WINDOW, 0).reshape(block + WINDOW, KV_HEADS, HEAD_DIM)
        value_heads = lax.dynamic_slice_in_dim(value_pad, start, block + WINDOW, 0).reshape(block + WINDOW, KV_HEADS, HEAD_DIM)
        query_seg = lax.dynamic_slice_in_dim(segments, start, block, 0)
        key_seg = lax.dynamic_slice_in_dim(seg_pad, start, block + WINDOW, 0)
        query_pos = start + jnp.arange(block, dtype=jnp.int32)
        key_pos = start - WINDOW + jnp.arange(block + WINDOW, dtype=jnp.int32)
        distance = query_pos[:, None] - key_pos[None, :]
        allowed = (key_pos[None, :] >= 0) & (distance >= 0) & (distance < WINDOW) & (query_seg[:, None] == key_seg[None, :])
        scores = low_back(jnp.einsum('qhgd,khd->hgqk', query_heads, key_heads, precision=HIGH) * HEAD_DIM ** (-0.5))
        scores = jnp.where(allowed[None, None], scores, -1e+30)
        top = lax.optimization_barrier(jnp.max(scores, -1, keepdims=True))
        raised = jnp.exp(scores - top)
        weights = low(raised / lax.optimization_barrier(jnp.sum(raised, -1, keepdims=True)))
        return jnp.einsum('hgqk,khd->qhgd', weights, value_heads, precision=HIGH).reshape(block, HEADS * HEAD_DIM)
    starts = jnp.arange(total // block, dtype=jnp.int32) * block
    return lax.map(jax.checkpoint(one_block), starts).reshape(total, HEADS * HEAD_DIM)

def layer(segments, stream, mixer_gain, query_weight, key_weight, value_weight, output_weight, attn_gain, mamba_gain, inner_proj, inner_gate, conv_kernel, conv_bias, select_weight, step_weight, step_bias, decay_log, skip_scale, mamba_out, ffn_gain, ffn_gate, ffn_up, ffn_down):
    total = stream.shape[0]
    mixer_in = low(normed(stream) * mixer_gain)
    queries = rounded(matmul(mixer_in, query_weight))
    keys = rounded(matmul(mixer_in, key_weight))
    values = rounded(matmul(mixer_in, value_weight))
    heads = rounded(attention(queries, keys, values, segments))
    attn = low_back(matmul_t(heads, output_weight))
    inner = rounded(matmul(mixer_in, inner_proj))
    zgate_in = low_back(matmul(mixer_in, inner_gate))
    seg_pad = jnp.concatenate([jnp.full((CONV - 1,), -1, jnp.int32), segments])
    inner_pad = jnp.concatenate([jnp.zeros((CONV - 1, INNER), jnp.float32), inner], 0)
    conv_pre = conv_bias
    for tap in range(CONV):
        same = (seg_pad[tap:tap + total] == segments).astype(jnp.float32)[:, None]
        conv_pre = conv_pre + conv_kernel[tap] * inner_pad[tap:tap + total] * same
    mixed_in = jax.nn.silu(conv_pre)
    selected = low_back(matmul(low(mixed_in), select_weight))
    step_low = selected[:, :STEP_RANK]
    entry = selected[:, STEP_RANK:STEP_RANK + STATE]
    readout = selected[:, STEP_RANK + STATE:]
    step_size = jax.nn.softplus(matmul(step_low, step_weight) + step_bias)
    alive = (seg_pad[CONV - 2:CONV - 2 + total] == segments).astype(jnp.float32)
    decay = -jnp.exp(decay_log)
    scanned, last = selective(jnp.zeros((INNER, STATE), jnp.float32), step_size, mixed_in, entry, readout, alive, decay, SCAN_BLOCK)
    gated = rounded((scanned + skip_scale * mixed_in) * jax.nn.silu(zgate_in))
    mamba = low_back(matmul_t(gated, mamba_out))
    resid = stream + 0.5 * (normed(attn) * attn_gain + normed(mamba) * mamba_gain)
    ffn_in = low(normed(resid) * ffn_gain)
    gate = low_back(matmul(ffn_in, ffn_gate))
    up = low_back(matmul(ffn_in, ffn_up))
    activated = rounded(jax.nn.silu(gate) * up)
    return resid + matmul_t(activated, ffn_down)

def reference(stream, cotangent, segments, mixer_gain, query_weight, key_weight, value_weight, output_weight, attn_gain, mamba_gain, inner_proj, inner_gate, conv_kernel, conv_bias, select_weight, step_weight, step_bias, decay_log, skip_scale, mamba_out, ffn_gain, ffn_gate, ffn_up, ffn_down):
    inputs = (stream, mixer_gain, query_weight, key_weight, value_weight, output_weight, attn_gain, mamba_gain, inner_proj, inner_gate, conv_kernel, conv_bias, select_weight, step_weight, step_bias, decay_log, skip_scale, mamba_out, ffn_gain, ffn_gate, ffn_up, ffn_down)
    floats = tuple((item.astype(jnp.float32) for item in inputs))
    result, pull = jax.vjp(partial(layer, segments), *floats)
    grads = pull(cotangent.astype(jnp.float32))
    return (result.astype(jnp.bfloat16), grads[0].astype(jnp.bfloat16), grads[1], grads[2], grads[3], grads[4], grads[5], grads[6], grads[7], grads[8], grads[9], grads[10], grads[11], grads[12], grads[13], grads[14], grads[15], grads[16], grads[17], grads[18], grads[19], grads[20], grads[21])
```

```python
import jax
import jax.numpy as jnp
from jax import lax
from jax.experimental import pallas as pl
from jax.experimental.pallas import tpu as pltpu
from jax.sharding import PartitionSpec as P
from functools import partial

D = 1600
HEADS = 25
KV_HEADS = 5
HEAD_DIM = 64
STATE = 16
CONV = 4
STEP_RANK = 100
WINDOW = 1024
TOK_DEV = 256
EPS = 1e-06
HIGH = lax.Precision.HIGHEST
NT = (((1,), (1,)), ((), ()))
LANES = 128
HALF = 8
CHUNK = 16
LOG2E = 1.4426950408889634
LN2 = 0.6931471805599453
FAR = 1e6
VMEM_LIMIT = 48 * 1024 * 1024


def lane_groups(width):
    return [(start, min(LANES, width - start)) for start in range(0, width, LANES)]


def tiles(width):
    return [(s, w, n) for s, w in lane_groups(width) for n in range(0, STATE, HALF)]


def spread_row(ref, row):
    return ref[pl.ds(row, 1), :]


def widened(width):
    return -(-width // LANES) * LANES


def end_kernel(reverse, size_in, drive_in, vec_ref, rate_ref, out_ref, size_ref, drive_ref):
    total, width = size_in.shape
    parts = tiles(width)
    size_ref[:, :width] = size_in[...]
    drive_ref[:, :width] = drive_in[...]

    def chunk_step(chunk, held):
        held = list(held)
        at = total // CHUNK - 1 - chunk if reverse else chunk
        for k in range(CHUNK - 1, -1, -1) if reverse else range(CHUNK):
            t = at * CHUNK + k
            sizes = spread_row(size_ref, t)
            drives = spread_row(drive_ref, t)
            for i, (s, w, n) in enumerate(parts):
                size, drive = sizes[:, s : s + w], drives[:, s : s + w]
                factor = jnp.exp2(size * rate_ref[n : n + HALF, s : s + w])
                push = drive * vec_ref[t, n : n + HALF, :w]
                held[i] = factor * (held[i] + push) if reverse else factor * held[i] + push
        return tuple(held)

    held = lax.fori_loop(
        0,
        total // CHUNK,
        chunk_step,
        tuple(jnp.zeros((HALF, w), jnp.float32) for _, w, _ in parts),
    )
    for i, (s, w, n) in enumerate(parts):
        out_ref[n : n + HALF, s : s + w] = held[i]
    out_ref[STATE:, :] = jnp.broadcast_to(
        jnp.sum(size_in[...], 0, keepdims=True), (out_ref.shape[0] - STATE, width)
    )


def entering(reverse, place_ref, ends_ref, rate_ref, into_ref):
    count = ends_ref.shape[0]
    into_ref[...] = jnp.zeros(into_ref.shape, jnp.float32)

    def one(step, carry):
        at = count - 1 - step if reverse else step
        decay = jnp.exp2(rate_ref[...] * ends_ref[at, STATE : STATE + 1, :])
        into_ref[...] = decay * into_ref[...] + ends_ref[at, 0:STATE, :]
        return carry

    lax.fori_loop(0, count - 1 - place_ref[0] if reverse else place_ref[0], one, 0)


def block_mask():
    span = CHUNK * STATE
    row = lax.broadcasted_iota(jnp.int32, (CHUNK, span), 0)
    col = lax.broadcasted_iota(jnp.int32, (CHUNK, span), 1)
    return (col >= row * STATE) & (col < (row + 1) * STATE)


def repeat_matrix():
    span = CHUNK * STATE
    row = lax.broadcasted_iota(jnp.int32, (STATE, span), 0)
    col = lax.broadcasted_iota(jnp.int32, (STATE, span), 1)
    return (lax.rem(col, STATE) == row).astype(jnp.bfloat16)


def picked(vec, mine, repeat):
    wide = jnp.dot(vec.astype(jnp.bfloat16), repeat, preferred_element_type=jnp.float32)
    return jnp.where(mine, wide, 0.0).astype(jnp.bfloat16)


def scan_kernel(
    place_ref, ends_ref, size_in, drive_in, vec_ref, rate_ref, pick_ref,
    y_ref, states_ref, into_ref, size_ref, drive_ref,
):
    total, width = size_in.shape
    parts = tiles(width)
    size_ref[:, :width] = size_in[...]
    drive_ref[:, :width] = drive_in[...]
    entering(False, place_ref, ends_ref, rate_ref, into_ref)
    states_ref[0:STATE, :] = into_ref[...].astype(jnp.bfloat16)
    mine = block_mask()
    repeat = repeat_matrix()

    def chunk_step(chunk, held):
        held = list(held)
        base = chunk * (CHUNK * STATE) + STATE
        for k in range(CHUNK):
            t = chunk * CHUNK + k
            sizes = spread_row(size_ref, t)
            drives = spread_row(drive_ref, t)
            for i, (s, w, n) in enumerate(parts):
                size, drive = sizes[:, s : s + w], drives[:, s : s + w]
                factor = jnp.exp2(size * rate_ref[n : n + HALF, s : s + w])
                held[i] = factor * held[i] + drive * vec_ref[t, n : n + HALF, :w]
                if n == HALF:
                    states_ref[pl.ds(pl.multiple_of(base + k * STATE, STATE), STATE), s : s + w] = (
                        jnp.concatenate([held[i - 1], held[i]], 0).astype(jnp.bfloat16)
                    )
        rows = pl.ds(pl.multiple_of(base, STATE), CHUNK * STATE)
        y_ref[pl.ds(pl.multiple_of(chunk * CHUNK, CHUNK), CHUNK), :] = jnp.dot(
            picked(pick_ref[pl.ds(pl.multiple_of(chunk * CHUNK, CHUNK), CHUNK), :], mine, repeat),
            states_ref[rows, :],
            preferred_element_type=jnp.float32,
        )
        return tuple(held)

    lax.fori_loop(
        0,
        total // CHUNK,
        chunk_step,
        tuple(into_ref[n : n + HALF, s : s + w] for s, w, n in parts),
    )


def back_kernel(
    place_ref, ends_ref, size_in, drive_ref, grad_in, vec_ref, rate_ref, pick_ref, states_ref,
    gdrive_ref, gsize_ref, gentry_ref, gread_ref, grate_ref,
    into_ref, adj_ref, slope_ref, size_ref, grad_ref,
):
    total, width = size_in.shape
    parts = tiles(width)
    size_ref[:, :width] = size_in[...]
    grad_ref[:, :width] = grad_in[...]
    span = CHUNK * STATE
    entering(True, place_ref, ends_ref, rate_ref, into_ref)
    own = block_mask()
    repeat = repeat_matrix()
    mine = own.astype(jnp.float32)
    ones = mine.astype(jnp.bfloat16)
    grate_ref[...] = jnp.zeros(grate_ref.shape, jnp.float32)

    def chunk_step(step, held):
        held = list(held)
        chunk = total // CHUNK - 1 - step
        rates = [jnp.zeros((HALF, w), jnp.float32) for _, w, _ in parts]
        for k in range(CHUNK - 1, -1, -1):
            t = chunk * CHUNK + k
            sizes = spread_row(size_ref, t)
            grads = spread_row(grad_ref, t)
            for i, (s, w, n) in enumerate(parts):
                if n != 0:
                    continue
                size, grad = sizes[:, s : s + w], grads[:, s : s + w]
                before = states_ref[pl.ds(pl.multiple_of(t * STATE, STATE), STATE), s : s + w].astype(
                    jnp.float32
                )
                adjs, slopes = [], []
                for j in range(2):
                    n0 = j * HALF
                    rate = rate_ref[n0 : n0 + HALF, s : s + w]
                    adj = grad * vec_ref[t, n0 : n0 + HALF, :w] + held[i + j]
                    held[i + j] = jnp.exp2(size * rate) * adj
                    moved = held[i + j] * before[n0 : n0 + HALF]
                    rates[i + j] = rates[i + j] + moved * size
                    adjs.append(adj)
                    slopes.append(moved * rate)
                at = slice(k * STATE, (k + 1) * STATE)
                adj_ref[at, s : s + w] = jnp.concatenate(adjs, 0).astype(jnp.bfloat16)
                slope_ref[at, s : s + w] = jnp.concatenate(slopes, 0).astype(jnp.bfloat16)
        for i, (s, w, n) in enumerate(parts):
            grate_ref[n : n + HALF, s : s + w] += rates[i]
        here = pl.ds(pl.multiple_of(chunk * CHUNK, CHUNK), CHUNK)
        gdrive_ref[here, :] = jnp.dot(
            picked(pick_ref[here, :], own, repeat), adj_ref[...], preferred_element_type=jnp.float32
        )
        gsize_ref[here, :] = (
            jnp.dot(ones, slope_ref[...], preferred_element_type=jnp.float32) * LN2
        )
        nt = (((1,), (1,)), ((), ()))
        gentry_ref[pl.ds(chunk, 1), :] = jnp.sum(
            mine
            * lax.dot_general(
                drive_ref[here, :].astype(jnp.bfloat16), adj_ref[...], nt,
                preferred_element_type=jnp.float32,
            ),
            0, keepdims=True,
        )
        rows = pl.ds(pl.multiple_of(chunk * span + STATE, STATE), span)
        gread_ref[pl.ds(chunk, 1), :] = jnp.sum(
            mine
            * lax.dot_general(
                grad_in[here, :].astype(jnp.bfloat16), states_ref[rows, :], nt,
                preferred_element_type=jnp.float32,
            ),
            0, keepdims=True,
        )
        return tuple(held)

    lax.fori_loop(
        0,
        total // CHUNK,
        chunk_step,
        tuple(into_ref[n : n + HALF, s : s + w] for s, w, n in parts),
    )


def cost(total, width, flops, exps, extra):
    cells = total * width * STATE
    return pl.CostEstimate(
        flops=cells * flops, transcendentals=cells * exps, bytes_accessed=total * width * 12 + extra
    )


def rows_scratch(total, width):
    return [pltpu.VMEM((total, widened(width)), jnp.float32)] * 2


def kernel_call(body, outs, scratch, smem, args, estimate):
    vmem = pl.BlockSpec(memory_space=pltpu.VMEM)
    return pl.pallas_call(
        body,
        out_shape=outs,
        in_specs=[pl.BlockSpec(memory_space=pltpu.SMEM)] * smem + [vmem] * (len(args) - smem),
        out_specs=jax.tree.map(lambda _: vmem, outs),
        scratch_shapes=scratch,
        compiler_params=pltpu.CompilerParams(vmem_limit_bytes=VMEM_LIMIT),
        cost_estimate=estimate,
    )(*args)


def block_end(reverse, size, drive, vec, rate):
    total, width = size.shape
    return kernel_call(
        partial(end_kernel, reverse),
        jax.ShapeDtypeStruct((STATE + HALF, width), jnp.float32),
        rows_scratch(total, width), 0, (size, drive, vec, rate),
        cost(total, width, 5, 1, 0),
    )


def scan_forward(place, ends, size, drive, vec, rate, pick):
    total, width = size.shape
    return kernel_call(
        scan_kernel,
        (
            jax.ShapeDtypeStruct((total, width), jnp.float32),
            jax.ShapeDtypeStruct(((total + 1) * STATE, width), jnp.bfloat16),
        ),
        [pltpu.VMEM((STATE, width), jnp.float32)] + rows_scratch(total, width),
        1, (place, ends, size, drive, vec, rate, pick),
        cost(total, width, 6, 1, total * width * 32),
    )


def scan_backward(place, ends, size, drive, grad, vec, rate, pick, states):
    total, width = size.shape
    span = CHUNK * STATE
    return kernel_call(
        back_kernel,
        (
            jax.ShapeDtypeStruct((total, width), jnp.float32),
            jax.ShapeDtypeStruct((total, width), jnp.float32),
            jax.ShapeDtypeStruct((total // CHUNK, span), jnp.float32),
            jax.ShapeDtypeStruct((total // CHUNK, span), jnp.float32),
            jax.ShapeDtypeStruct((STATE, width), jnp.float32),
        ),
        [
            pltpu.VMEM((STATE, width), jnp.float32),
            pltpu.VMEM((span, width), jnp.bfloat16),
            pltpu.VMEM((span, width), jnp.bfloat16),
        ]
        + rows_scratch(total, width),
        1, (place, ends, size, drive, grad, vec, rate, pick, states),
        cost(total, width, 12, 1, total * width * 32),
    )


def lanes_of(vec):
    return jnp.broadcast_to(vec[:, :, None], vec.shape + (LANES,))


def piece_of(head, cols):
    first = lax.div(head * HEAD_DIM, cols)
    last = lax.div(head * HEAD_DIM + HEAD_DIM - 1, cols)
    return first, last, jnp.where(last > first, 1.0, 0.0).astype(jnp.bfloat16)


def pick_head(head, piece, cols, start, width):
    row = lax.broadcasted_iota(jnp.int32, (2 * cols, width), 0)
    lane = lax.broadcasted_iota(jnp.int32, (2 * cols, width), 1)
    source = piece * cols + row
    key = (row < cols) & (lane < HEAD_DIM) & (source == head * HEAD_DIM + lane)
    value = (
        (row >= cols)
        & (lane >= HEAD_DIM)
        & (source - cols == head * HEAD_DIM + lane - HEAD_DIM)
    )
    return (key | value).astype(jnp.bfloat16)


def head_pairs(head, pieces, pair_ref):
    cols = pieces[0].shape[2] // 2
    rows = pieces[0].shape[1]
    first, last, two = piece_of(head, cols)
    pick_first = pick_head(head, first, cols, 0, 2 * HEAD_DIM)
    pick_last = pick_head(head, last, cols, 0, 2 * HEAD_DIM) * two
    for block, ref in enumerate(pieces):
        pair = jnp.dot(ref[first], pick_first, preferred_element_type=jnp.float32) + jnp.dot(
            ref[last], pick_last, preferred_element_type=jnp.float32
        )
        pair_ref[block * rows : (block + 1) * rows, :] = pair.astype(jnp.bfloat16)


def attend_kernel(count, *refs):
    pieces = refs[:count]
    offset_ref, query_seg_ref, key_seg_ref, query_ref, probs_ref, heads_ref = refs[count : count + 6]
    pair_ref, score_ref = refs[count + 6 :]
    head = pl.program_id(0)
    head_pairs(head, pieces, pair_ref)
    quarter = query_seg_ref.shape[0]
    span = key_seg_ref.shape[1]
    row = lax.broadcasted_iota(jnp.int32, (quarter, span), 0)
    col = lax.broadcasted_iota(jnp.int32, (quarter, span), 1)
    distance = row + offset_ref[0] - col
    allowed = (
        (distance >= 0) & (distance < WINDOW) & (query_seg_ref[...] == key_seg_ref[...])
    )
    score_ref[...] = lax.dot_general(
        query_ref[0], pair_ref[:, :HEAD_DIM], NT, preferred_element_type=jnp.float32
    )
    for group in range(query_ref.shape[1] // quarter):
        at = slice(group * quarter, (group + 1) * quarter)
        scores = jnp.where(allowed, score_ref[at, :] * HEAD_DIM ** (-0.5), -1e30)
        raised = jnp.exp(scores - jnp.max(scores, -1, keepdims=True))
        share = 1.0 / jnp.sum(raised, -1, keepdims=True)
        probs_ref[0, at, :] = (raised * share).astype(jnp.bfloat16)
    heads_ref[0] = jnp.dot(
        probs_ref[0], pair_ref[:, HEAD_DIM:], preferred_element_type=jnp.float32
    ).astype(jnp.bfloat16)


def attend_back_kernel(count, *refs):
    pieces = refs[:count]
    query_ref, probs_ref, grad_ref, gquery_ref, gwindow_ref = refs[count : count + 5]
    pair_ref, gprob_ref, gscore_ref = refs[count + 5 :]
    head = pl.program_id(0)
    cols = pieces[0].shape[2] // 2
    first, last, two = piece_of(head, cols)
    head_pairs(head, pieces, pair_ref)
    gprob_ref[...] = lax.dot_general(
        grad_ref[0], pair_ref[:, HEAD_DIM:], NT, preferred_element_type=jnp.float32
    )
    step = HEAD_DIM
    for at in range(0, gprob_ref.shape[0], step):
        probs = probs_ref[0, at : at + step, :].astype(jnp.float32)
        both = probs * gprob_ref[at : at + step, :]
        gscore_ref[at : at + step, :] = (
            both - probs * jnp.sum(both, -1, keepdims=True)
        ).astype(jnp.bfloat16)
    scale = HEAD_DIM ** (-0.5)
    gquery_ref[0] = (
        jnp.dot(gscore_ref[...], pair_ref[:, :HEAD_DIM], preferred_element_type=jnp.float32) * scale
    ).astype(jnp.bfloat16)
    row = lax.broadcasted_iota(jnp.int32, (HEAD_DIM, HEAD_DIM), 0)
    lane = lax.broadcasted_iota(jnp.int32, (HEAD_DIM, HEAD_DIM), 1)
    unit = (row == lane).astype(jnp.bfloat16)

    def turned(value):
        return lax.dot_general(unit, value, NT, preferred_element_type=jnp.float32).astype(
            jnp.bfloat16
        )

    gkey = jnp.dot(turned(query_ref[0]), gscore_ref[...], preferred_element_type=jnp.float32)
    gvalue = jnp.dot(turned(grad_ref[0]), probs_ref[0], preferred_element_type=jnp.float32)
    gpair = jnp.concatenate([gkey * scale, gvalue], 0).astype(jnp.bfloat16)

    @pl.when(head == 0)
    def _():
        gwindow_ref[...] = jnp.zeros(gwindow_ref.shape, jnp.bfloat16)

    def add(piece, weight):
        pick = pick_head(head, piece, cols, 0, 2 * HEAD_DIM) * weight
        part = jnp.dot(pick, gpair, preferred_element_type=jnp.float32)
        gwindow_ref[piece] = (gwindow_ref[piece].astype(jnp.float32) + part).astype(jnp.bfloat16)

    add(first, jnp.ones((), jnp.bfloat16))
    add(last, two)


def whole(shape):
    return pl.BlockSpec(shape, lambda head: (0,) * len(shape))


def of_head(shape):
    return pl.BlockSpec((1,) + shape[1:], lambda head: (head,) + (0,) * (len(shape) - 1))


def attend(pieces, offset, query_seg, key_seg, queries):
    heads, rows, dim = queries.shape
    span = key_seg.shape[1]
    outs = (
        jax.ShapeDtypeStruct((heads, rows, span), jnp.bfloat16),
        jax.ShapeDtypeStruct(queries.shape, jnp.bfloat16),
    )
    return pl.pallas_call(
        partial(attend_kernel, len(pieces)),
        grid=(heads,),
        out_shape=outs,
        in_specs=[whole(p.shape) for p in pieces]
        + [pl.BlockSpec(memory_space=pltpu.SMEM), whole(query_seg.shape), whole(key_seg.shape)]
        + [of_head(queries.shape)],
        out_specs=tuple(of_head(o.shape) for o in outs),
        scratch_shapes=[
            pltpu.VMEM((span, 2 * dim), jnp.bfloat16),
            pltpu.VMEM((rows, span), jnp.float32),
        ],
        compiler_params=pltpu.CompilerParams(vmem_limit_bytes=VMEM_LIMIT),
        cost_estimate=pl.CostEstimate(
            flops=4 * heads * rows * span * dim,
            transcendentals=heads * rows * span,
            bytes_accessed=2 * heads * rows * span + 4 * queries.size,
        ),
    )(*pieces, offset, query_seg, key_seg, queries)


def attend_back(pieces, queries, probs, grads):
    heads, rows, dim = queries.shape
    span = probs.shape[2]
    outs = (
        jax.ShapeDtypeStruct(queries.shape, jnp.bfloat16),
        jax.ShapeDtypeStruct((pieces[0].shape[0], pieces[0].shape[2], span), jnp.bfloat16),
    )
    return pl.pallas_call(
        partial(attend_back_kernel, len(pieces)),
        grid=(heads,),
        out_shape=outs,
        in_specs=[whole(p.shape) for p in pieces]
        + [of_head(queries.shape), of_head(probs.shape), of_head(grads.shape)],
        out_specs=(of_head(outs[0].shape), whole(outs[1].shape)),
        scratch_shapes=[
            pltpu.VMEM((span, 2 * dim), jnp.bfloat16),
            pltpu.VMEM((rows, span), jnp.float32),
            pltpu.VMEM((rows, span), jnp.bfloat16),
        ],
        compiler_params=pltpu.CompilerParams(vmem_limit_bytes=VMEM_LIMIT),
        cost_estimate=pl.CostEstimate(
            flops=8 * heads * rows * span * dim,
            transcendentals=0,
            bytes_accessed=4 * heads * rows * span,
        ),
    )(*pieces, queries, probs, grads)


def passed_along(value, axis, steps):
    count = lax.axis_size(axis)
    first, last = (max(0, -steps), min(count, count - steps))
    return lax.ppermute(value, axis, [(source, source + steps) for source in range(first, last)])


def after(value, *others):
    return lax.optimization_barrier((value, *others))[0]


def partner(value, axis, bit, when=None):
    count = lax.axis_size(axis)
    got = lax.ppermute(value, axis, [(s, s ^ (1 << bit)) for s in range(count)])
    return got if when is None else after(got, when)


def all_sum(value, axes, kind, whens=()):
    whens = list(whens)
    for axis in axes:
        count = lax.axis_size(axis)
        bits = count.bit_length() - 1
        if count != 1 << bits:
            value = lax.psum(value, axis)
            continue
        for bit in range(bits):
            low = value.astype(kind)
            got = partner(low, axis, bit, whens.pop(0) if whens else None)
            value = low.astype(jnp.float32) + got.astype(jnp.float32)
    return value


class Halving:
    def __init__(self, value, order):
        self.order = list(order)
        self.left = sorted(order, reverse=True)
        self.split(value.astype(jnp.bfloat16).reshape([2] * len(self.left) + [-1, value.shape[1]]))

    def split(self, held):
        self.bit = self.order.pop(0)
        axis = self.left.index(self.bit)
        self.left.remove(self.bit)
        mine = (lax.axis_index("seq") >> self.bit) & 1
        self.sent = lax.dynamic_index_in_dim(held, 1 - mine, axis, False)
        self.kept = lax.dynamic_index_in_dim(held, mine, axis, False)

    def step(self, when=None):
        got = partner(self.sent, "seq", self.bit, when)
        total = self.kept.astype(jnp.float32) + got.astype(jnp.float32)
        if self.order:
            self.split(total.astype(jnp.bfloat16))
        return total

    def finish(self, when=None):
        while self.order:
            self.step(when)
        return self.step(when)


def chip_bits():
    return list(range(1, lax.axis_size("seq").bit_length() - 1))


def row_sides(value):
    blocks = lax.axis_size("seq")
    turned = value.T.reshape(blocks // 2, 2, -1, value.shape[0])
    mine = lax.axis_index("seq") & 1
    return [
        lax.dynamic_index_in_dim(turned, side, 1, False).reshape(-1, value.shape[0])
        for side in (mine, 1 - mine)
    ]


def core_send(left_sib, right):
    return matmul(left_sib, right).astype(jnp.bfloat16)


def core_sum(left_own, right, send, when=None):
    got = partner(send, "seq", 0, when)
    return (matmul(left_own, right) + got.astype(jnp.float32)).astype(jnp.bfloat16)


def first_core():
    return (lax.axis_index("seq") & 1) == 0


def core_order(mine, other):
    first = first_core()
    return jnp.where(first, mine, other), jnp.where(first, other, mine)


def chip_groups():
    count = lax.axis_size("seq")
    return [[c for c in range(count) if c % 2 == p] for p in range(2)]


def core_columns(weights, padded_to):
    pad = [(0, 0), (0, padded_to - weights[0].shape[1] // 2)]
    low = jnp.concatenate([jnp.pad(w[:, : w.shape[1] // 2], pad) for w in weights], 1)
    high = jnp.concatenate([jnp.pad(w[:, w.shape[1] // 2 :], pad) for w in weights], 1)
    first = first_core()
    mine, other = jnp.where(first, low, high), jnp.where(first, high, low)
    return jnp.concatenate(core_order(mine, partner(other, "seq", 0)), 0)


def core_rows_back(held, count, width, when):
    mine = lax.axis_index("seq") & 1
    both = held.reshape(2, -1, held.shape[-1])
    kept = lax.dynamic_index_in_dim(both, mine, 0, False)
    sent = lax.dynamic_index_in_dim(both, 1 - mine, 0, False).astype(jnp.bfloat16)
    low, high = core_order(kept, partner(sent, "seq", 0, when).astype(jnp.float32))
    step = held.shape[-1] // count
    return [
        jnp.concatenate([low[:, at : at + width], high[:, at : at + width]], 1)
        for at in range(0, count * step, step)
    ]


def received(pieces, axis):
    count = lax.axis_size(axis)
    place = lax.axis_index(axis)
    held = []
    for shift in range(count):
        sent = lax.dynamic_index_in_dim(pieces, (place + shift) % count, 0, False)
        held.append(
            lax.ppermute(sent, axis, [(s, (s + shift) % count) for s in range(count)])
            if shift
            else sent
        )
    return held


def by_source(held, axis):
    count = lax.axis_size(axis)
    place = lax.axis_index(axis)
    held = jnp.stack(held)
    return jnp.stack(
        [
            lax.dynamic_index_in_dim(held, (place - source) % count, 0, False)
            for source in range(count)
        ]
    )


def exchange(pieces, axis):
    return lax.all_to_all(pieces, axis, 0, 0, tiled=True)


def spread_direct(value, axis, when):
    count = lax.axis_size(axis)
    held = [value]
    for shift in range(1, count):
        got = lax.ppermute(value, axis, [(s, (s + shift) % count) for s in range(count)])
        held.append(after(got, when))
    return by_source(held, axis)


def inverse_rms(value):
    return lax.rsqrt(jnp.mean(value * value, -1, keepdims=True) + EPS)


def rms_back(grad_normed, normed, scale):
    return scale * (grad_normed - normed * jnp.mean(grad_normed * normed, -1, keepdims=True))


def silu_slope(value):
    sigma = jax.nn.sigmoid(value)
    return sigma * (1.0 + value * (1.0 - sigma))


def matmul(left, right):
    return jnp.dot(left, right, preferred_element_type=jnp.float32)


def matmul_nt(left, right):
    return lax.dot_general(
        left, right, (((1,), (1,)), ((), ())), preferred_element_type=jnp.float32
    )


def matmul_tn(left, right):
    return lax.dot_general(
        left, right, (((0,), (0,)), ((), ())), preferred_element_type=jnp.float32
    )


def on_device(
    stream,
    cotangent,
    segments,
    mixer_gain,
    query_weight,
    key_weight,
    value_weight,
    output_weight,
    attn_gain,
    mamba_gain,
    inner_proj,
    inner_gate,
    conv_kernel,
    conv_bias,
    select_weight,
    step_weight,
    step_bias,
    decay_log,
    skip_scale,
    mamba_out,
    ffn_gain,
    ffn_gate,
    ffn_up,
    ffn_down,
):
    seq_count = lax.axis_size("seq")
    tp_count = lax.axis_size("tp")
    seq_index = lax.axis_index("seq")
    tp_index = lax.axis_index("tp")
    quarter = stream.shape[0]
    rows = TOK_DEV
    hops = (WINDOW + TOK_DEV - 1) // TOK_DEV
    span = (hops + 1) * rows
    key_width = KV_HEADS * HEAD_DIM
    groups = HEADS // KV_HEADS
    head_cols = query_weight.shape[1]
    pair_cols = key_weight.shape[1]

    def spread(value):
        return lax.all_gather(value, "tp", axis=0, tiled=True)

    def spread_later(value, when):
        return spread_direct(value, "tp", when).reshape(rows, -1)

    def token_sums(value, when=None):
        pieces = received(value.astype(jnp.bfloat16).reshape(tp_count, quarter, -1), "tp")
        if when is not None:
            pieces = [after(piece, when) for piece in pieces]
        return sum(piece.astype(jnp.float32) for piece in pieces)

    def token_sums_late(value):
        pieces = exchange(value.astype(jnp.bfloat16).reshape(tp_count, quarter, -1), "tp")
        return jnp.sum(pieces.astype(jnp.float32), 0)

    def earlier(value, hop):
        return passed_along(value, "seq", hop)

    def later(value, hop):
        return passed_along(value, "seq", -hop)

    def whole_rows(weight):
        return lax.all_gather(weight, "seq", axis=0, tiled=True)

    def from_chips(value):
        return lax.all_gather(
            value, "seq", axis=0, tiled=True, axis_index_groups=chip_groups()
        )

    def over_chips(value):
        return lax.psum_scatter(
            value, "seq", scatter_dimension=0, tiled=True, axis_index_groups=chip_groups()
        ).astype(jnp.float32)

    def own_cols(value):
        return value.reshape(quarter, tp_count, -1).transpose(1, 0, 2)

    proj = whole_rows(inner_proj)
    wide_cols = -(-inner_gate.shape[1] // LANES) * LANES
    pad_cols = ((0, 0), (0, wide_cols - inner_gate.shape[1]))
    ssm_pair = whole_rows(
        jnp.concatenate([jnp.pad(inner_gate, pad_cols), jnp.pad(mamba_out, pad_cols)], 1)
    )
    zproj = ssm_pair[:, : inner_gate.shape[1]]
    mout = ssm_pair[:, wide_cols : wide_cols + mamba_out.shape[1]]
    block_stream = spread(stream)
    (
        block_stream, stream, cotangent, segments, key_weight, value_weight, conv_kernel,
        conv_bias, decay_log, ffn_gate, ffn_up, ffn_down,
    ) = lax.optimization_barrier(
        (
            block_stream, stream, cotangent, segments, key_weight, value_weight, conv_kernel,
            conv_bias, decay_log, ffn_gate, ffn_up, ffn_down,
        )
    )
    block_stream = block_stream.astype(jnp.float32)
    half = ffn_gate.shape[1] // 2
    wide = -(-half // 256) * 256
    ffn_here = core_columns([ffn_gate, ffn_up, ffn_down], wide)
    ffn_here = ffn_here[:, : 2 * wide], ffn_here[:, 2 * wide :]
    base = seq_index * rows
    first_row = base + tp_index * quarter
    stream_f = stream.astype(jnp.float32)
    scale_one = inverse_rms(stream_f)
    normed_one = stream_f * scale_one
    block_normed = block_stream * inverse_rms(block_stream)
    block_in = (block_normed * mixer_gain).astype(jnp.bfloat16)
    gate_up_w = from_chips(ffn_here[0])
    down_w = from_chips(ffn_here[1])
    pair_weight = jnp.concatenate([key_weight, value_weight], 1)
    query_cols = matmul(block_in, query_weight).astype(jnp.bfloat16)
    pair_part = matmul(block_in, pair_weight).astype(jnp.bfloat16)
    block_late = after(block_in, query_cols, pair_part)
    inner = matmul(block_late, proj).astype(jnp.bfloat16)
    block_pairs = spread_direct(pair_part, "tp", inner)
    edge = earlier(inner[rows - (CONV - 1) :], 1)
    seg_conv = lax.dynamic_slice_in_dim(
        jnp.concatenate([jnp.full((CONV - 1,), -1, jnp.int32), segments]), base, rows + CONV - 1, 0
    )
    own_seg = seg_conv[CONV - 1 :]
    taps = [
        (seg_conv[tap : tap + rows] == own_seg).astype(jnp.float32)[:, None] for tap in range(CONV)
    ]
    padded = jnp.concatenate([edge, inner], 0).astype(jnp.float32)
    conv_pre = conv_bias + sum(
        (conv_kernel[tap] * padded[tap : tap + rows] * taps[tap] for tap in range(CONV))
    )
    alive = (seg_conv[CONV - 2 : CONV - 2 + rows] == own_seg)[:, None]
    mixed_in = jax.nn.silu(conv_pre)
    mixed_low = mixed_in.astype(jnp.bfloat16)
    selected = all_sum(matmul(mixed_low, select_weight), ("tp",), jnp.bfloat16)

    selected = after(selected, block_pairs, *ffn_here)
    step_low = selected[:, :STEP_RANK]
    entry = selected[:, STEP_RANK : STEP_RANK + STATE]
    readout = selected[:, STEP_RANK + STATE :]
    step_pre = jnp.dot(step_low, step_weight, precision=HIGH) + step_bias
    step_size = jax.nn.softplus(step_pre)
    decay = -jnp.exp(decay_log).T
    rate = decay * LOG2E
    size = jnp.where(alive, step_size, FAR)
    drive = step_size * mixed_in
    entry_wide = lanes_of(entry)
    readout_wide = lanes_of(readout)
    ends = block_end(False, size, after(drive, ssm_pair), entry_wide, rate)
    place = seq_index.astype(jnp.int32).reshape(1)
    block_ends = lax.all_gather(ends, "seq")
    scanned, states = scan_forward(
        place, block_ends, size, drive, entry_wide, rate, readout
    )
    zgate_in = matmul(after(block_in, ends), zproj)
    ssm = scanned + skip_scale * mixed_in
    zgate = jax.nn.silu(zgate_in)
    gated = (ssm * zgate).astype(jnp.bfloat16)
    mamba_part = matmul_nt(gated, mout).astype(jnp.bfloat16)
    mamba = token_sums(mamba_part)
    seg_ext = jnp.concatenate([jnp.full((hops * rows,), -1, jnp.int32), segments])
    query_seg = lax.dynamic_slice_in_dim(segments, first_row, quarter, 0)[:, None]
    key_seg = lax.dynamic_slice_in_dim(seg_ext, base, span, 0)[None]
    offset = (hops * rows + tp_index * quarter).astype(jnp.int32).reshape(1)

    def by_head(pieces):
        value = pieces.transpose(1, 0, 2).reshape(quarter, KV_HEADS, groups, HEAD_DIM)
        return value.transpose(1, 2, 0, 3).reshape(KV_HEADS, groups * quarter, HEAD_DIM)

    def by_column(value):
        value = value.reshape(KV_HEADS, groups, quarter, HEAD_DIM).transpose(2, 0, 1, 3)
        return value.reshape(quarter, tp_count, head_cols).transpose(1, 0, 2)

    pieces = [after(earlier(block_pairs, hop), gated) for hop in range(hops, 0, -1)]
    pieces.append(block_pairs)
    queries = by_head(
        after(exchange(query_cols.reshape(tp_count, quarter, head_cols), "tp"), mamba_part)
    )
    probs, heads_out = attend(pieces, offset, query_seg, key_seg, queries)
    heads_cols = exchange(by_column(heads_out), "tp").reshape(rows, head_cols)
    attn_part = matmul_nt(after(heads_cols, mamba), output_weight).astype(jnp.bfloat16)
    mamba = after(mamba, attn_part, gate_up_w)
    attn = token_sums_late(attn_part)

    grad_rows = spread_later(cotangent, mamba)
    scale_attn = inverse_rms(attn)
    normed_attn = attn * scale_attn
    scale_mamba = inverse_rms(mamba)
    normed_mamba = mamba * scale_mamba
    resid = stream_f + 0.5 * (normed_attn * attn_gain + normed_mamba * mamba_gain)
    scale_two = inverse_rms(resid)
    normed_two = resid * scale_two
    ffn_in = (normed_two * ffn_gain).astype(jnp.bfloat16)
    ffn_rows = spread(after(ffn_in, down_w))
    ffn_two = jnp.concatenate([ffn_rows, partner(ffn_rows, "seq", 0)], 0)
    grad_two = jnp.concatenate([grad_rows, partner(grad_rows, "seq", 0, gated)], 0)
    gate_up = matmul(ffn_two, gate_up_w)
    gate, up = gate_up[:, :wide], gate_up[:, wide:]
    activated = (jax.nn.silu(gate) * up).astype(jnp.bfloat16)

    grad_out = cotangent.astype(jnp.float32)
    grad_act_low = matmul(grad_two, down_w).astype(jnp.bfloat16)
    grad_gate = (grad_act_low * up * silu_slope(gate)).astype(jnp.bfloat16)
    grad_up = (grad_act_low * jax.nn.silu(gate)).astype(jnp.bfloat16)
    grad_gate_up = jnp.concatenate([grad_gate, grad_up], 1)

    def chip_tokens(value, weight):
        got = partner(matmul_nt(value[rows:], weight).astype(jnp.bfloat16), "seq", 0)
        return (matmul_nt(value[:rows], weight) + got.astype(jnp.float32)).astype(jnp.bfloat16)

    grad_ffn_part = chip_tokens(grad_gate_up, gate_up_w)
    grad_ffn_in = token_sums(grad_ffn_part)
    gate_up_late, activated_late = lax.optimization_barrier(
        (grad_gate_up, activated, grad_ffn_part)
    )[:2]
    gate_up_grads = matmul_tn(ffn_two, gate_up_late).astype(jnp.bfloat16)
    down_grads = matmul_tn(grad_two, activated_late).astype(jnp.bfloat16)
    bits = chip_bits()
    gate_up_sum = over_chips(gate_up_grads)
    down_x = Halving(down_grads, bits[::-1])
    grad_ffn_in = after(grad_ffn_in, gate_up_grads, down_x.sent)
    grad_ffn_gain = jnp.sum(grad_ffn_in * normed_two, 0)
    grad_resid = grad_out + rms_back(grad_ffn_in * ffn_gain, normed_two, scale_two)
    grad_attn_gain = 0.5 * jnp.sum(grad_resid * normed_attn, 0)
    grad_mamba_gain = 0.5 * jnp.sum(grad_resid * normed_mamba, 0)
    grad_attn = rms_back(0.5 * grad_resid * attn_gain, normed_attn, scale_attn).astype(jnp.bfloat16)
    grad_mamba = rms_back(0.5 * grad_resid * mamba_gain, normed_mamba, scale_mamba).astype(
        jnp.bfloat16
    )
    grad_mrows = spread(grad_mamba)
    grad_arows = exchange(
        jnp.broadcast_to(after(grad_attn, grad_mrows), (tp_count,) + grad_attn.shape), "tp"
    ).reshape(rows, -1)
    grad_gated = matmul(grad_mrows, mout).astype(jnp.bfloat16)
    grad_ssm = grad_gated * zgate
    grad_zgate = (grad_gated * ssm * silu_slope(zgate_in)).astype(jnp.bfloat16)
    grad_skip = jnp.sum(grad_ssm * mixed_in, 0)
    down_x.step(grad_mrows)
    backlog = block_end(True, size, grad_ssm, readout_wide, rate)
    block_backlogs = lax.all_gather(backlog, "seq")

    grad_head_cols = matmul(grad_arows, output_weight).astype(jnp.bfloat16)
    grad_heads = by_head(
        exchange(grad_head_cols.reshape(tp_count, quarter, head_cols), "tp")
    )
    grad_heads = after(grad_heads, down_x.sent)
    mrows_own, mrows_sib = row_sides(after(grad_mrows, grad_ssm))
    block_own, block_sib = row_sides(block_in)
    mout_send = core_send(mrows_sib, gated)
    zgate_send = core_send(block_sib, grad_zgate)
    grad_query, grad_window = attend_back(pieces, queries, probs, grad_heads)
    mout_held = core_sum(mrows_own, gated, mout_send, backlog)
    zgate_held = core_sum(block_own, grad_zgate, zgate_send, backlog)
    window_grad = lax.psum_scatter(after(grad_window, gate_up_sum), "tp", scatter_dimension=0, tiled=False)
    grad_query_cols = exchange(by_column(grad_query), "tp").reshape(rows, head_cols)
    head_grads = jnp.concatenate(
        [matmul_tn(grad_query_cols, block_in), matmul_tn(heads_cols, grad_arows)], 0
    )
    head_grads = head_grads.astype(jnp.bfloat16)
    head_sums = lax.psum(head_grads, "seq")
    mout_x = Halving(mout_held, bits[::-1])
    zgate_x = Halving(zgate_held, bits)
    before_scan = after(
        grad_ssm, mout_x.sent, zgate_x.sent
    )
    grad_drive, grad_size, grad_entry, grad_read, grad_rates = scan_backward(
        place, block_backlogs, size, drive, before_scan, readout_wide, rate, entry, states
    )
    grad_step = grad_size + grad_drive * mixed_in
    grad_inputs = grad_drive * step_size + grad_ssm * skip_scale
    grad_pre = grad_step * jax.nn.sigmoid(step_pre)
    grad_low = jnp.dot(grad_pre, step_weight.T, precision=HIGH)
    grad_low = jnp.concatenate(
        [grad_low, grad_entry.reshape(rows, STATE), grad_read.reshape(rows, STATE)], 1
    )
    grad_decay_log = grad_rates * decay
    grad_step_bias = jnp.sum(grad_pre, 0)
    grad_skip = jnp.sum(grad_ssm * mixed_in, 0)
    grad_step_weight = jnp.dot(step_low.T, grad_pre, precision=HIGH)
    grad_selected = all_sum(grad_low, ("tp",), jnp.bfloat16).astype(jnp.bfloat16)
    moved = [
        later(after(window_grad, grad_low)[:, (hops - hop) * rows : (hops - hop + 1) * rows], hop)
        for hop in range(1, hops + 1)
    ]
    grad_selected = after(grad_selected, window_grad)
    grad_inputs = grad_inputs + matmul_nt(grad_selected, select_weight)
    grad_conv = grad_inputs * silu_slope(conv_pre)
    grad_padded = sum(
        (
            jnp.pad(conv_kernel[tap] * grad_conv * taps[tap], ((tap, CONV - 1 - tap), (0, 0)))
            for tap in range(CONV)
        )
    )
    returned = later(grad_padded[: CONV - 1].astype(jnp.bfloat16), 1).astype(jnp.float32)
    grad_inner = (
        grad_padded[CONV - 1 :] + jnp.pad(returned, ((rows - (CONV - 1), 0), (0, 0)))
    ).astype(jnp.bfloat16)
    down_sum = down_x.finish(grad_selected)
    mout_x.step(grad_selected)
    zgate_x.step(grad_selected)
    layer_sums = token_sums_late(chip_tokens(after(activated, grad_selected), down_w))
    layer_out = (resid + layer_sums).astype(jnp.bfloat16)
    grad_pairs = window_grad[:, hops * rows :].astype(jnp.float32)
    for part in moved:
        grad_pairs = grad_pairs + after(part, grad_conv).astype(jnp.float32)
    grad_pair_low = grad_pairs.astype(jnp.bfloat16)
    pair_grads = matmul(grad_pair_low, block_in)
    grad_inner = after(grad_inner, mout_x.sent, zgate_x.sent, pair_grads)
    proj_send = core_send(block_sib, grad_inner)
    pair_grads = all_sum(pair_grads, ("seq",), jnp.bfloat16, [proj_send] * (len(bits) + 1))
    proj_x = Halving(core_sum(block_own, grad_inner, proj_send), bits[::-1])
    tail = proj_x.sent
    grad_block_rest = (
        matmul_nt(grad_zgate, zproj)
        + matmul_nt(grad_query_cols, query_weight)
        + lax.dot_general(
            grad_pair_low,
            pair_weight,
            (((0,), (1,)), ((), ())),
            preferred_element_type=jnp.float32,
        )
    )
    grad_block_in = matmul_nt(after(grad_inner, proj_send), proj) + grad_block_rest
    block_in_pieces = received(
        grad_block_in.astype(jnp.bfloat16).reshape(tp_count, quarter, -1), "tp"
    )
    proj_sum = proj_x.finish()
    grad_mixer_in = sum(
        after(piece, tail).astype(jnp.float32) for piece in block_in_pieces
    )
    stream_grad = (grad_resid + rms_back(grad_mixer_in * mixer_gain, normed_one, scale_one)).astype(
        jnp.bfloat16
    )
    grad_mixer_gain = jnp.sum(after(grad_block_in, tail) * block_normed, 0)
    gain_parts = jnp.stack([grad_mixer_gain, grad_attn_gain, grad_mamba_gain, grad_ffn_gain])
    gain_parts = all_sum(gain_parts, ("tp",), jnp.float32)
    grad_select = matmul_tn(grad_selected, mixed_low)
    grad_conv_bias = jnp.sum(grad_conv, 0)
    grad_kernel = jnp.stack(
        [jnp.sum(grad_conv * padded[tap : tap + rows] * taps[tap], 0) for tap in range(CONV)]
    )
    width = grad_skip.shape[0]
    gain_rows = -(-gain_parts.size // width)
    gain_flat = jnp.pad(gain_parts.reshape(-1), (0, gain_rows * width - gain_parts.size))
    aligned = [
        gain_flat.reshape(gain_rows, width),
        grad_kernel,
        jnp.stack([grad_conv_bias, grad_step_bias, grad_skip, jnp.zeros_like(grad_skip)]),
        grad_decay_log,
        jnp.pad(grad_select, ((0, -grad_select.shape[0] % HALF), (0, 0))),
        jnp.pad(grad_step_weight, ((0, -STEP_RANK % HALF), (0, 0))),
    ]
    small = jnp.concatenate(aligned, 0).astype(jnp.bfloat16)
    small = all_sum(after(small, tail), ("seq",), jnp.bfloat16)
    mout_sum = mout_x.finish(proj_send)
    zgate_sum = zgate_x.finish(proj_send)
    gate_grad, up_grad = core_rows_back(gate_up_sum, 2, half, proj_send)
    (down_grad,) = core_rows_back(down_sum, 1, half, proj_send)
    head_sums = after(head_sums, proj_sum).astype(jnp.float32)
    ranks = STEP_RANK + 2 * STATE
    starts = [0]
    for part in aligned:
        starts.append(starts[-1] + part.shape[0])
    gain_totals = small[: starts[1]].reshape(-1)[: gain_parts.size].reshape(gain_parts.shape)
    conv_at, lone_at, decay_at, select_at, step_at = starts[1:6]
    return (
        layer_out,
        stream_grad,
        gain_totals[0],
        head_sums[:head_cols].T,
        pair_grads[:pair_cols].T,
        pair_grads[pair_cols:].T,
        head_sums[head_cols:].T,
        gain_totals[1],
        gain_totals[2],
        proj_sum,
        zgate_sum,
        small[conv_at : conv_at + CONV],
        small[lone_at],
        small[select_at : select_at + ranks].T,
        small[step_at : step_at + STEP_RANK],
        small[lone_at + 1],
        small[decay_at : decay_at + STATE].T,
        small[lone_at + 2],
        mout_sum,
        gain_totals[3],
        gate_grad,
        up_grad,
        down_grad,
    )


def solution(mesh):
    return jax.shard_map(
        on_device,
        mesh=mesh,
        in_specs=(
            P(("seq", "tp"), None),
            P(("seq", "tp"), None),
            P(),
            P(),
            P(None, "tp"),
            P(None, "tp"),
            P(None, "tp"),
            P(None, "tp"),
            P(),
            P(),
            P("seq", "tp"),
            P("seq", "tp"),
            P(None, "tp"),
            P("tp"),
            P("tp", None),
            P(None, "tp"),
            P("tp"),
            P("tp", None),
            P("tp"),
            P("seq", "tp"),
            P(),
            P("seq", "tp"),
            P("seq", "tp"),
            P("seq", "tp"),
        ),
        out_specs=(
            P(("seq", "tp"), None),
            P(("seq", "tp"), None),
            P(),
            P(None, "tp"),
            P(None, "tp"),
            P(None, "tp"),
            P(None, "tp"),
            P(),
            P(),
            P("seq", "tp"),
            P("seq", "tp"),
            P(None, "tp"),
            P("tp"),
            P("tp", None),
            P(None, "tp"),
            P("tp"),
            P("tp", None),
            P("tp"),
            P("seq", "tp"),
            P(),
            P("seq", "tp"),
            P("seq", "tp"),
            P("seq", "tp"),
        ),
        check_vma=False,
    )
```

```python
import jax
import jax.numpy as jnp
from jax import lax
from jax.experimental import pallas as pl
from jax.experimental.layout import Layout, with_layout_constraint
from jax.experimental.pallas import tpu as pltpu
from jax.sharding import PartitionSpec as P
from functools import partial

D = 1600
HEADS = 25
KV_HEADS = 5
HEAD_DIM = 64
STATE = 16
CONV = 4
STEP_RANK = 100
WINDOW = 1024
TOK_DEV = 256
EPS = 1e-06
HIGH = lax.Precision.HIGHEST
NT = (((1,), (1,)), ((), ()))
LANES = 128
HALF = 8
CHUNK = 16
LOG2E = 1.4426950408889634
LN2 = 0.6931471805599453
FAR = 1e6
VMEM_LIMIT = 48 * 1024 * 1024


def lane_groups(width):
    return [(start, min(LANES, width - start)) for start in range(0, width, LANES)]


def tiles(width):
    return [(s, w, n) for s, w in lane_groups(width) for n in range(0, STATE, HALF)]


def spread_row(ref, row):
    return ref[pl.ds(row, 1), :]


def widened(width):
    return -(-width // LANES) * LANES


def end_kernel(reverse, size_in, drive_in, vec_ref, rate_ref, out_ref, size_ref, drive_ref):
    total, width = size_in.shape
    parts = tiles(width)
    size_ref[:, :width] = size_in[...]
    drive_ref[:, :width] = drive_in[...]

    def chunk_step(chunk, held):
        held = list(held)
        at = total // CHUNK - 1 - chunk if reverse else chunk
        for k in range(CHUNK - 1, -1, -1) if reverse else range(CHUNK):
            t = at * CHUNK + k
            sizes = spread_row(size_ref, t)
            drives = spread_row(drive_ref, t)
            for i, (s, w, n) in enumerate(parts):
                size, drive = sizes[:, s : s + w], drives[:, s : s + w]
                factor = jnp.exp2(size * rate_ref[n : n + HALF, s : s + w])
                push = drive * vec_ref[t, n : n + HALF, :w]
                held[i] = factor * (held[i] + push) if reverse else factor * held[i] + push
        return tuple(held)

    held = lax.fori_loop(
        0,
        total // CHUNK,
        chunk_step,
        tuple(jnp.zeros((HALF, w), jnp.float32) for _, w, _ in parts),
    )
    for i, (s, w, n) in enumerate(parts):
        out_ref[n : n + HALF, s : s + w] = held[i]
    out_ref[STATE:, :] = jnp.broadcast_to(
        jnp.sum(size_in[...], 0, keepdims=True), (out_ref.shape[0] - STATE, width)
    )


def entering(reverse, place_ref, ends_ref, rate_ref, into_ref):
    count = ends_ref.shape[0]
    into_ref[...] = jnp.zeros(into_ref.shape, jnp.float32)

    def one(step, carry):
        at = count - 1 - step if reverse else step
        decay = jnp.exp2(rate_ref[...] * ends_ref[at, STATE : STATE + 1, :])
        into_ref[...] = decay * into_ref[...] + ends_ref[at, 0:STATE, :]
        return carry

    lax.fori_loop(0, count - 1 - place_ref[0] if reverse else place_ref[0], one, 0)


def block_mask():
    span = CHUNK * STATE
    row = lax.broadcasted_iota(jnp.int32, (CHUNK, span), 0)
    col = lax.broadcasted_iota(jnp.int32, (CHUNK, span), 1)
    return (col >= row * STATE) & (col < (row + 1) * STATE)


def repeat_matrix():
    span = CHUNK * STATE
    row = lax.broadcasted_iota(jnp.int32, (STATE, span), 0)
    col = lax.broadcasted_iota(jnp.int32, (STATE, span), 1)
    return (lax.rem(col, STATE) == row).astype(jnp.bfloat16)


def picked(vec, mine, repeat):
    wide = jnp.dot(vec.astype(jnp.bfloat16), repeat, preferred_element_type=jnp.float32)
    return jnp.where(mine, wide, 0.0).astype(jnp.bfloat16)


def scan_kernel(
    place_ref, ends_ref, size_in, drive_in, vec_ref, rate_ref, pick_ref,
    y_ref, states_ref, into_ref, size_ref, drive_ref,
):
    total, width = size_in.shape
    parts = tiles(width)
    size_ref[:, :width] = size_in[...]
    drive_ref[:, :width] = drive_in[...]
    entering(False, place_ref, ends_ref, rate_ref, into_ref)
    states_ref[0:STATE, :] = into_ref[...].astype(jnp.bfloat16)
    mine = block_mask()
    repeat = repeat_matrix()

    def chunk_step(chunk, held):
        held = list(held)
        base = chunk * (CHUNK * STATE) + STATE
        for k in range(CHUNK):
            t = chunk * CHUNK + k
            sizes = spread_row(size_ref, t)
            drives = spread_row(drive_ref, t)
            for i, (s, w, n) in enumerate(parts):
                size, drive = sizes[:, s : s + w], drives[:, s : s + w]
                factor = jnp.exp2(size * rate_ref[n : n + HALF, s : s + w])
                held[i] = factor * held[i] + drive * vec_ref[t, n : n + HALF, :w]
                if n == HALF:
                    states_ref[pl.ds(pl.multiple_of(base + k * STATE, STATE), STATE), s : s + w] = (
                        jnp.concatenate([held[i - 1], held[i]], 0).astype(jnp.bfloat16)
                    )
        rows = pl.ds(pl.multiple_of(base, STATE), CHUNK * STATE)
        y_ref[pl.ds(pl.multiple_of(chunk * CHUNK, CHUNK), CHUNK), :] = jnp.dot(
            picked(pick_ref[pl.ds(pl.multiple_of(chunk * CHUNK, CHUNK), CHUNK), :], mine, repeat),
            states_ref[rows, :],
            preferred_element_type=jnp.float32,
        )
        return tuple(held)

    lax.fori_loop(
        0,
        total // CHUNK,
        chunk_step,
        tuple(into_ref[n : n + HALF, s : s + w] for s, w, n in parts),
    )


def back_kernel(
    place_ref, ends_ref, size_in, drive_ref, grad_in, vec_ref, rate_ref, pick_ref, states_ref,
    gdrive_ref, gsize_ref, gentry_ref, gread_ref, grate_ref,
    into_ref, adj_ref, slope_ref, size_ref, grad_ref,
):
    total, width = size_in.shape
    parts = tiles(width)
    size_ref[:, :width] = size_in[...]
    grad_ref[:, :width] = grad_in[...]
    span = CHUNK * STATE
    entering(True, place_ref, ends_ref, rate_ref, into_ref)
    own = block_mask()
    repeat = repeat_matrix()
    mine = own.astype(jnp.float32)
    ones = mine.astype(jnp.bfloat16)
    grate_ref[...] = jnp.zeros(grate_ref.shape, jnp.float32)

    def chunk_step(step, held):
        held = list(held)
        chunk = total // CHUNK - 1 - step
        rates = [jnp.zeros((HALF, w), jnp.float32) for _, w, _ in parts]
        for k in range(CHUNK - 1, -1, -1):
            t = chunk * CHUNK + k
            sizes = spread_row(size_ref, t)
            grads = spread_row(grad_ref, t)
            for i, (s, w, n) in enumerate(parts):
                if n != 0:
                    continue
                size, grad = sizes[:, s : s + w], grads[:, s : s + w]
                before = states_ref[pl.ds(pl.multiple_of(t * STATE, STATE), STATE), s : s + w].astype(
                    jnp.float32
                )
                adjs, slopes = [], []
                for j in range(2):
                    n0 = j * HALF
                    rate = rate_ref[n0 : n0 + HALF, s : s + w]
                    adj = grad * vec_ref[t, n0 : n0 + HALF, :w] + held[i + j]
                    held[i + j] = jnp.exp2(size * rate) * adj
                    moved = held[i + j] * before[n0 : n0 + HALF]
                    rates[i + j] = rates[i + j] + moved * size
                    adjs.append(adj)
                    slopes.append(moved * rate)
                at = slice(k * STATE, (k + 1) * STATE)
                adj_ref[at, s : s + w] = jnp.concatenate(adjs, 0).astype(jnp.bfloat16)
                slope_ref[at, s : s + w] = jnp.concatenate(slopes, 0).astype(jnp.bfloat16)
        for i, (s, w, n) in enumerate(parts):
            grate_ref[n : n + HALF, s : s + w] += rates[i]
        here = pl.ds(pl.multiple_of(chunk * CHUNK, CHUNK), CHUNK)
        gdrive_ref[here, :] = jnp.dot(
            picked(pick_ref[here, :], own, repeat), adj_ref[...], preferred_element_type=jnp.float32
        )
        gsize_ref[here, :] = (
            jnp.dot(ones, slope_ref[...], preferred_element_type=jnp.float32) * LN2
        )
        nt = (((1,), (1,)), ((), ()))
        gentry_ref[pl.ds(chunk, 1), :] = jnp.sum(
            mine
            * lax.dot_general(
                drive_ref[here, :].astype(jnp.bfloat16), adj_ref[...], nt,
                preferred_element_type=jnp.float32,
            ),
            0, keepdims=True,
        )
        rows = pl.ds(pl.multiple_of(chunk * span + STATE, STATE), span)
        gread_ref[pl.ds(chunk, 1), :] = jnp.sum(
            mine
            * lax.dot_general(
                grad_in[here, :].astype(jnp.bfloat16), states_ref[rows, :], nt,
                preferred_element_type=jnp.float32,
            ),
            0, keepdims=True,
        )
        return tuple(held)

    lax.fori_loop(
        0,
        total // CHUNK,
        chunk_step,
        tuple(into_ref[n : n + HALF, s : s + w] for s, w, n in parts),
    )


def cost(total, width, flops, exps, extra):
    cells = total * width * STATE
    return pl.CostEstimate(
        flops=cells * flops, transcendentals=cells * exps, bytes_accessed=total * width * 12 + extra
    )


def rows_scratch(total, width):
    return [pltpu.VMEM((total, widened(width)), jnp.float32)] * 2


def kernel_call(body, outs, scratch, smem, args, estimate):
    vmem = pl.BlockSpec(memory_space=pltpu.VMEM)
    return pl.pallas_call(
        body,
        out_shape=outs,
        in_specs=[pl.BlockSpec(memory_space=pltpu.SMEM)] * smem + [vmem] * (len(args) - smem),
        out_specs=jax.tree.map(lambda _: vmem, outs),
        scratch_shapes=scratch,
        compiler_params=pltpu.CompilerParams(vmem_limit_bytes=VMEM_LIMIT),
        cost_estimate=estimate,
    )(*args)


def block_end(reverse, size, drive, vec, rate):
    total, width = size.shape
    return kernel_call(
        partial(end_kernel, reverse),
        jax.ShapeDtypeStruct((STATE + HALF, width), jnp.float32),
        rows_scratch(total, width), 0, (size, drive, vec, rate),
        cost(total, width, 5, 1, 0),
    )


def scan_forward(place, ends, size, drive, vec, rate, pick):
    total, width = size.shape
    return kernel_call(
        scan_kernel,
        (
            jax.ShapeDtypeStruct((total, width), jnp.float32),
            jax.ShapeDtypeStruct(((total + 1) * STATE, width), jnp.bfloat16),
        ),
        [pltpu.VMEM((STATE, width), jnp.float32)] + rows_scratch(total, width),
        1, (place, ends, size, drive, vec, rate, pick),
        cost(total, width, 6, 1, total * width * 32),
    )


def scan_backward(place, ends, size, drive, grad, vec, rate, pick, states):
    total, width = size.shape
    span = CHUNK * STATE
    return kernel_call(
        back_kernel,
        (
            jax.ShapeDtypeStruct((total, width), jnp.float32),
            jax.ShapeDtypeStruct((total, width), jnp.float32),
            jax.ShapeDtypeStruct((total // CHUNK, span), jnp.float32),
            jax.ShapeDtypeStruct((total // CHUNK, span), jnp.float32),
            jax.ShapeDtypeStruct((STATE, width), jnp.float32),
        ),
        [
            pltpu.VMEM((STATE, width), jnp.float32),
            pltpu.VMEM((span, width), jnp.bfloat16),
            pltpu.VMEM((span, width), jnp.bfloat16),
        ]
        + rows_scratch(total, width),
        1, (place, ends, size, drive, grad, vec, rate, pick, states),
        cost(total, width, 12, 1, total * width * 32),
    )


def lanes_of(vec):
    return jnp.broadcast_to(vec[:, :, None], vec.shape + (LANES,))


def piece_of(head, cols):
    first = lax.div(head * HEAD_DIM, cols)
    last = lax.div(head * HEAD_DIM + HEAD_DIM - 1, cols)
    return first, last, jnp.where(last > first, 1.0, 0.0).astype(jnp.bfloat16)


def pick_head(head, piece, cols, start, width):
    row = lax.broadcasted_iota(jnp.int32, (2 * cols, width), 0)
    lane = lax.broadcasted_iota(jnp.int32, (2 * cols, width), 1)
    source = piece * cols + row
    key = (row < cols) & (lane < HEAD_DIM) & (source == head * HEAD_DIM + lane)
    value = (
        (row >= cols)
        & (lane >= HEAD_DIM)
        & (source - cols == head * HEAD_DIM + lane - HEAD_DIM)
    )
    return (key | value).astype(jnp.bfloat16)


def head_pairs(head, pieces, pair_ref):
    cols = pieces[0].shape[2] // 2
    rows = pieces[0].shape[1]
    first, last, two = piece_of(head, cols)
    pick_first = pick_head(head, first, cols, 0, 2 * HEAD_DIM)
    pick_last = pick_head(head, last, cols, 0, 2 * HEAD_DIM) * two
    for block, ref in enumerate(pieces):
        pair = jnp.dot(ref[first], pick_first, preferred_element_type=jnp.float32) + jnp.dot(
            ref[last], pick_last, preferred_element_type=jnp.float32
        )
        pair_ref[block * rows : (block + 1) * rows, :] = pair.astype(jnp.bfloat16)


def attend_kernel(count, *refs):
    pieces = refs[:count]
    offset_ref, query_seg_ref, key_seg_ref, query_ref, probs_ref, heads_ref = refs[count : count + 6]
    pair_ref, score_ref = refs[count + 6 :]
    head = pl.program_id(0)
    head_pairs(head, pieces, pair_ref)
    quarter = query_seg_ref.shape[0]
    span = key_seg_ref.shape[1]
    row = lax.broadcasted_iota(jnp.int32, (quarter, span), 0)
    col = lax.broadcasted_iota(jnp.int32, (quarter, span), 1)
    distance = row + offset_ref[0] - col
    allowed = (
        (distance >= 0) & (distance < WINDOW) & (query_seg_ref[...] == key_seg_ref[...])
    )
    score_ref[...] = lax.dot_general(
        query_ref[0], pair_ref[:, :HEAD_DIM], NT, preferred_element_type=jnp.float32
    )
    for group in range(query_ref.shape[1] // quarter):
        at = slice(group * quarter, (group + 1) * quarter)
        scores = jnp.where(allowed, score_ref[at, :] * HEAD_DIM ** (-0.5), -1e30)
        raised = jnp.exp(scores - jnp.max(scores, -1, keepdims=True))
        share = 1.0 / jnp.sum(raised, -1, keepdims=True)
        probs_ref[0, at, :] = (raised * share).astype(jnp.bfloat16)
    heads_ref[0] = jnp.dot(
        probs_ref[0], pair_ref[:, HEAD_DIM:], preferred_element_type=jnp.float32
    ).astype(jnp.bfloat16)


def attend_back_kernel(count, *refs):
    pieces = refs[:count]
    query_ref, probs_ref, grad_ref, gquery_ref, gwindow_ref = refs[count : count + 5]
    pair_ref, gprob_ref, gscore_ref = refs[count + 5 :]
    head = pl.program_id(0)
    cols = pieces[0].shape[2] // 2
    first, last, two = piece_of(head, cols)
    head_pairs(head, pieces, pair_ref)
    gprob_ref[...] = lax.dot_general(
        grad_ref[0], pair_ref[:, HEAD_DIM:], NT, preferred_element_type=jnp.float32
    )
    step = HEAD_DIM
    for at in range(0, gprob_ref.shape[0], step):
        probs = probs_ref[0, at : at + step, :].astype(jnp.float32)
        both = probs * gprob_ref[at : at + step, :]
        gscore_ref[at : at + step, :] = (
            both - probs * jnp.sum(both, -1, keepdims=True)
        ).astype(jnp.bfloat16)
    scale = HEAD_DIM ** (-0.5)
    gquery_ref[0] = (
        jnp.dot(gscore_ref[...], pair_ref[:, :HEAD_DIM], preferred_element_type=jnp.float32) * scale
    ).astype(jnp.bfloat16)
    row = lax.broadcasted_iota(jnp.int32, (HEAD_DIM, HEAD_DIM), 0)
    lane = lax.broadcasted_iota(jnp.int32, (HEAD_DIM, HEAD_DIM), 1)
    unit = (row == lane).astype(jnp.bfloat16)

    def turned(value):
        return lax.dot_general(unit, value, NT, preferred_element_type=jnp.float32).astype(
            jnp.bfloat16
        )

    gkey = jnp.dot(turned(query_ref[0]), gscore_ref[...], preferred_element_type=jnp.float32)
    gvalue = jnp.dot(turned(grad_ref[0]), probs_ref[0], preferred_element_type=jnp.float32)
    gpair = jnp.concatenate([gkey * scale, gvalue], 0).astype(jnp.bfloat16)

    @pl.when(head == 0)
    def _():
        gwindow_ref[...] = jnp.zeros(gwindow_ref.shape, jnp.bfloat16)

    def add(piece, weight):
        pick = pick_head(head, piece, cols, 0, 2 * HEAD_DIM) * weight
        part = jnp.dot(pick, gpair, preferred_element_type=jnp.float32)
        gwindow_ref[piece] = (gwindow_ref[piece].astype(jnp.float32) + part).astype(jnp.bfloat16)

    add(first, jnp.ones((), jnp.bfloat16))
    add(last, two)


def whole(shape):
    return pl.BlockSpec(shape, lambda head: (0,) * len(shape))


def of_head(shape):
    return pl.BlockSpec((1,) + shape[1:], lambda head: (head,) + (0,) * (len(shape) - 1))


def attend(pieces, offset, query_seg, key_seg, queries):
    heads, rows, dim = queries.shape
    span = key_seg.shape[1]
    outs = (
        jax.ShapeDtypeStruct((heads, rows, span), jnp.bfloat16),
        jax.ShapeDtypeStruct(queries.shape, jnp.bfloat16),
    )
    return pl.pallas_call(
        partial(attend_kernel, len(pieces)),
        grid=(heads,),
        out_shape=outs,
        in_specs=[whole(p.shape) for p in pieces]
        + [pl.BlockSpec(memory_space=pltpu.SMEM), whole(query_seg.shape), whole(key_seg.shape)]
        + [of_head(queries.shape)],
        out_specs=tuple(of_head(o.shape) for o in outs),
        scratch_shapes=[
            pltpu.VMEM((span, 2 * dim), jnp.bfloat16),
            pltpu.VMEM((rows, span), jnp.float32),
        ],
        compiler_params=pltpu.CompilerParams(vmem_limit_bytes=VMEM_LIMIT),
        cost_estimate=pl.CostEstimate(
            flops=4 * heads * rows * span * dim,
            transcendentals=heads * rows * span,
            bytes_accessed=2 * heads * rows * span + 4 * queries.size,
        ),
    )(*pieces, offset, query_seg, key_seg, queries)


def attend_back(pieces, queries, probs, grads):
    heads, rows, dim = queries.shape
    span = probs.shape[2]
    outs = (
        jax.ShapeDtypeStruct(queries.shape, jnp.bfloat16),
        jax.ShapeDtypeStruct((pieces[0].shape[0], pieces[0].shape[2], span), jnp.bfloat16),
    )
    return pl.pallas_call(
        partial(attend_back_kernel, len(pieces)),
        grid=(heads,),
        out_shape=outs,
        in_specs=[whole(p.shape) for p in pieces]
        + [of_head(queries.shape), of_head(probs.shape), of_head(grads.shape)],
        out_specs=(of_head(outs[0].shape), whole(outs[1].shape)),
        scratch_shapes=[
            pltpu.VMEM((span, 2 * dim), jnp.bfloat16),
            pltpu.VMEM((rows, span), jnp.float32),
            pltpu.VMEM((rows, span), jnp.bfloat16),
        ],
        compiler_params=pltpu.CompilerParams(vmem_limit_bytes=VMEM_LIMIT),
        cost_estimate=pl.CostEstimate(
            flops=8 * heads * rows * span * dim,
            transcendentals=0,
            bytes_accessed=4 * heads * rows * span,
        ),
    )(*pieces, queries, probs, grads)


def passed_along(value, axis, steps):
    count = lax.axis_size(axis)
    first, last = (max(0, -steps), min(count, count - steps))
    return lax.ppermute(value, axis, [(source, source + steps) for source in range(first, last)])


def after(value, *others):
    return lax.optimization_barrier((value, *others))[0]


def partner(value, axis, bit, when=None):
    count = lax.axis_size(axis)
    got = lax.ppermute(value, axis, [(s, s ^ (1 << bit)) for s in range(count)])
    return got if when is None else after(got, when)


def all_sum(value, axes, kind, whens=()):
    whens = list(whens)
    for axis in axes:
        count = lax.axis_size(axis)
        bits = count.bit_length() - 1
        if count != 1 << bits:
            value = lax.psum(value, axis)
            continue
        for bit in range(bits):
            low = value.astype(kind)
            got = partner(low, axis, bit, whens.pop(0) if whens else None)
            value = low.astype(jnp.float32) + got.astype(jnp.float32)
    return value


class Halving:
    def __init__(self, value, order):
        self.order = list(order)
        self.left = sorted(order, reverse=True)
        self.split(value.astype(jnp.bfloat16).reshape([2] * len(self.left) + [-1, value.shape[1]]))

    def split(self, held):
        self.bit = self.order.pop(0)
        axis = self.left.index(self.bit)
        self.left.remove(self.bit)
        mine = (lax.axis_index("seq") >> self.bit) & 1
        self.sent = lax.dynamic_index_in_dim(held, 1 - mine, axis, False)
        self.kept = lax.dynamic_index_in_dim(held, mine, axis, False)

    def step(self, when=None):
        got = partner(self.sent, "seq", self.bit, when)
        total = self.kept.astype(jnp.float32) + got.astype(jnp.float32)
        if self.order:
            self.split(total.astype(jnp.bfloat16))
        return total

    def finish(self, when=None):
        while self.order:
            self.step(when)
        return self.step(when)


def chip_bits():
    return list(range(1, lax.axis_size("seq").bit_length() - 1))


def row_sides(value):
    blocks = lax.axis_size("seq")
    turned = value.T.reshape(blocks // 2, 2, -1, value.shape[0])
    mine = lax.axis_index("seq") & 1
    return [
        lax.dynamic_index_in_dim(turned, side, 1, False).reshape(-1, value.shape[0])
        for side in (mine, 1 - mine)
    ]


def core_send(left_sib, right):
    return matmul(left_sib, right).astype(jnp.bfloat16)


def core_sum(left_own, right, send, when=None):
    got = partner(send, "seq", 0, when)
    return (matmul(left_own, right) + got.astype(jnp.float32)).astype(jnp.bfloat16)


def first_core():
    return (lax.axis_index("seq") & 1) == 0


def core_order(mine, other):
    first = first_core()
    return jnp.where(first, mine, other), jnp.where(first, other, mine)


def chip_groups():
    count = lax.axis_size("seq")
    return [[c for c in range(count) if c % 2 == p] for p in range(2)]


def core_columns(weights, padded_to):
    pad = [(0, 0), (0, padded_to - weights[0].shape[1] // 2)]
    low = jnp.concatenate([jnp.pad(w[:, : w.shape[1] // 2], pad) for w in weights], 1)
    high = jnp.concatenate([jnp.pad(w[:, w.shape[1] // 2 :], pad) for w in weights], 1)
    first = first_core()
    mine, other = jnp.where(first, low, high), jnp.where(first, high, low)
    return jnp.concatenate(core_order(mine, partner(other, "seq", 0)), 0)


def core_rows_back(held, count, width, when):
    mine = lax.axis_index("seq") & 1
    both = held.reshape(2, -1, held.shape[-1])
    kept = lax.dynamic_index_in_dim(both, mine, 0, False)
    sent = lax.dynamic_index_in_dim(both, 1 - mine, 0, False).astype(jnp.bfloat16)
    low, high = core_order(kept, partner(sent, "seq", 0, when).astype(kept.dtype))
    step = held.shape[-1] // count
    return [
        jnp.concatenate([low[:, at : at + width], high[:, at : at + width]], 1).astype(jnp.float32)
        for at in range(0, count * step, step)
    ]


def received(pieces, axis):
    count = lax.axis_size(axis)
    place = lax.axis_index(axis)
    held = []
    for shift in range(count):
        sent = row_major(lax.dynamic_index_in_dim(pieces, (place + shift) % count, 0, False))
        held.append(
            lax.ppermute(sent, axis, [(s, (s + shift) % count) for s in range(count)])
            if shift
            else sent
        )
    return held


def by_source(held, axis):
    count = lax.axis_size(axis)
    place = lax.axis_index(axis)
    held = jnp.stack(held)
    return jnp.stack(
        [
            lax.dynamic_index_in_dim(held, (place - source) % count, 0, False)
            for source in range(count)
        ]
    )


def exchange(pieces, axis):
    return lax.all_to_all(pieces, axis, 0, 0, tiled=True)


def spread_direct(value, axis, when):
    count = lax.axis_size(axis)
    value = row_major(value)
    held = [value]
    for shift in range(1, count):
        got = lax.ppermute(value, axis, [(s, (s + shift) % count) for s in range(count)])
        held.append(after(got, when))
    return by_source(held, axis)


def inverse_rms(value):
    return lax.rsqrt(jnp.mean(value * value, -1, keepdims=True) + EPS)


def rms_back(grad_normed, normed, scale):
    return scale * (grad_normed - normed * jnp.mean(grad_normed * normed, -1, keepdims=True))


def silu_slope(value):
    sigma = jax.nn.sigmoid(value)
    return sigma * (1.0 + value * (1.0 - sigma))


def matmul(left, right):
    return jnp.dot(left, right, preferred_element_type=jnp.float32)


def matmul_nt(left, right):
    return lax.dot_general(
        left, right, (((1,), (1,)), ((), ())), preferred_element_type=jnp.float32
    )


def row_major(value):
    order = tuple(range(value.ndim))
    return with_layout_constraint(value, Layout(major_to_minor=order))


def matmul_tn(left, right):
    return lax.dot_general(
        left, right, (((0,), (0,)), ((), ())), preferred_element_type=jnp.float32
    )


def on_device(
    stream,
    cotangent,
    segments,
    mixer_gain,
    query_weight,
    key_weight,
    value_weight,
    output_weight,
    attn_gain,
    mamba_gain,
    inner_proj,
    inner_gate,
    conv_kernel,
    conv_bias,
    select_weight,
    step_weight,
    step_bias,
    decay_log,
    skip_scale,
    mamba_out,
    ffn_gain,
    ffn_gate,
    ffn_up,
    ffn_down,
):
    seq_count = lax.axis_size("seq")
    tp_count = lax.axis_size("tp")
    seq_index = lax.axis_index("seq")
    tp_index = lax.axis_index("tp")
    quarter = stream.shape[0]
    rows = TOK_DEV
    hops = (WINDOW + TOK_DEV - 1) // TOK_DEV
    span = (hops + 1) * rows
    key_width = KV_HEADS * HEAD_DIM
    groups = HEADS // KV_HEADS
    head_cols = query_weight.shape[1]
    pair_cols = key_weight.shape[1]

    def spread(value):
        return lax.all_gather(value, "tp", axis=0, tiled=True)

    def spread_later(value, when):
        return spread_direct(value, "tp", when).reshape(rows, -1)

    def token_sums(value, when=None):
        value = row_major(value.astype(jnp.bfloat16))
        pieces = received(value.reshape(tp_count, quarter, -1), "tp")
        if when is not None:
            pieces = [after(piece, when) for piece in pieces]
        return sum(piece.astype(jnp.float32) for piece in pieces)

    def token_sums_late(value):
        pieces = exchange(value.astype(jnp.bfloat16).reshape(tp_count, quarter, -1), "tp")
        return jnp.sum(pieces.astype(jnp.float32), 0)

    def earlier(value, hop):
        return passed_along(value, "seq", hop)

    def later(value, hop):
        return passed_along(value, "seq", -hop)

    def whole_rows(weight):
        return lax.all_gather(weight, "seq", axis=0, tiled=True)

    def from_chips(value):
        return lax.all_gather(
            value, "seq", axis=0, tiled=True, axis_index_groups=chip_groups()
        )

    def over_chips(value):
        return lax.psum_scatter(
            value, "seq", scatter_dimension=0, tiled=True, axis_index_groups=chip_groups()
        )

    def own_cols(value):
        return value.reshape(quarter, tp_count, -1).transpose(1, 0, 2)

    proj = whole_rows(inner_proj)
    wide_cols = -(-inner_gate.shape[1] // LANES) * LANES
    pad_cols = ((0, 0), (0, wide_cols - inner_gate.shape[1]))
    ssm_pair = whole_rows(
        jnp.concatenate([jnp.pad(inner_gate, pad_cols), jnp.pad(mamba_out, pad_cols)], 1)
    )
    zproj = ssm_pair[:, : inner_gate.shape[1]]
    mout = ssm_pair[:, wide_cols : wide_cols + mamba_out.shape[1]]
    block_stream = spread(stream)
    (
        block_stream, stream, cotangent, segments, key_weight, value_weight, conv_kernel,
        conv_bias, decay_log, ffn_gate, ffn_up, ffn_down,
    ) = lax.optimization_barrier(
        (
            block_stream, stream, cotangent, segments, key_weight, value_weight, conv_kernel,
            conv_bias, decay_log, ffn_gate, ffn_up, ffn_down,
        )
    )
    block_stream = block_stream.astype(jnp.float32)
    base = seq_index * rows
    first_row = base + tp_index * quarter
    stream_f = stream.astype(jnp.float32)
    scale_one = inverse_rms(stream_f)
    normed_one = stream_f * scale_one
    block_normed = block_stream * inverse_rms(block_stream)
    block_in = (block_normed * mixer_gain).astype(jnp.bfloat16)
    pair_weight = jnp.concatenate([key_weight, value_weight], 1)
    query_cols = matmul(block_in, query_weight).astype(jnp.bfloat16)
    pair_part = matmul(block_in, pair_weight).astype(jnp.bfloat16)
    block_late = after(block_in, query_cols, pair_part)
    inner = matmul(block_late, proj).astype(jnp.bfloat16)
    half = ffn_gate.shape[1] // 2
    wide = -(-half // 256) * 256
    ffn_here = core_columns([after(ffn_gate, inner), ffn_up, ffn_down], wide)
    ffn_here = ffn_here[:, : 2 * wide], ffn_here[:, 2 * wide :]
    gate_up_w = from_chips(ffn_here[0])
    down_w = from_chips(ffn_here[1])
    block_pairs = spread_direct(pair_part, "tp", inner)
    edge = earlier(inner[rows - (CONV - 1) :], 1)
    seg_conv = lax.dynamic_slice_in_dim(
        jnp.concatenate([jnp.full((CONV - 1,), -1, jnp.int32), segments]), base, rows + CONV - 1, 0
    )
    own_seg = seg_conv[CONV - 1 :]
    taps = [
        (seg_conv[tap : tap + rows] == own_seg).astype(jnp.float32)[:, None] for tap in range(CONV)
    ]
    padded = jnp.concatenate([edge, inner], 0).astype(jnp.float32)
    conv_pre = conv_bias + sum(
        (conv_kernel[tap] * padded[tap : tap + rows] * taps[tap] for tap in range(CONV))
    )
    alive = (seg_conv[CONV - 2 : CONV - 2 + rows] == own_seg)[:, None]
    mixed_in = jax.nn.silu(conv_pre)
    mixed_low = mixed_in.astype(jnp.bfloat16)
    selected = all_sum(matmul(mixed_low, select_weight), ("tp",), jnp.bfloat16)

    selected = after(selected, block_pairs, *ffn_here)
    step_low = selected[:, :STEP_RANK]
    entry = selected[:, STEP_RANK : STEP_RANK + STATE]
    readout = selected[:, STEP_RANK + STATE :]
    step_pre = jnp.dot(step_low, step_weight, precision=HIGH) + step_bias
    step_size = jax.nn.softplus(step_pre)
    decay = -jnp.exp(decay_log).T
    rate = decay * LOG2E
    size = jnp.where(alive, step_size, FAR)
    drive = step_size * mixed_in
    entry_wide = lanes_of(entry)
    readout_wide = lanes_of(readout)
    ends = block_end(False, size, after(drive, ssm_pair), entry_wide, rate)
    place = seq_index.astype(jnp.int32).reshape(1)
    block_ends = lax.all_gather(ends, "seq")
    scanned, states = scan_forward(
        place, block_ends, size, drive, entry_wide, rate, readout
    )
    zgate_in = matmul(after(block_in, ends), zproj)
    ssm = scanned + skip_scale * mixed_in
    zgate = jax.nn.silu(zgate_in)
    gated = (ssm * zgate).astype(jnp.bfloat16)
    mamba_part = matmul_nt(gated, mout).astype(jnp.bfloat16)
    mamba = token_sums(mamba_part)
    seg_ext = jnp.concatenate([jnp.full((hops * rows,), -1, jnp.int32), segments])
    query_seg = lax.dynamic_slice_in_dim(segments, first_row, quarter, 0)[:, None]
    key_seg = lax.dynamic_slice_in_dim(seg_ext, base, span, 0)[None]
    offset = (hops * rows + tp_index * quarter).astype(jnp.int32).reshape(1)

    def by_head(pieces):
        value = pieces.transpose(1, 0, 2).reshape(quarter, KV_HEADS, groups, HEAD_DIM)
        return value.transpose(1, 2, 0, 3).reshape(KV_HEADS, groups * quarter, HEAD_DIM)

    def by_column(value):
        value = value.reshape(KV_HEADS, groups, quarter, HEAD_DIM).transpose(2, 0, 1, 3)
        return value.reshape(quarter, tp_count, head_cols).transpose(1, 0, 2)

    sent_pairs = after(block_pairs, block_ends)
    pieces = [after(earlier(sent_pairs, hop), gated) for hop in range(hops, 0, -1)]
    pieces.append(block_pairs)
    queries = by_head(
        after(exchange(query_cols.reshape(tp_count, quarter, head_cols), "tp"), mamba_part)
    )
    probs, heads_out = attend(pieces, offset, query_seg, key_seg, queries)
    heads_held = received(by_column(heads_out), "tp")
    heads_back = jnp.concatenate(heads_held, 0)
    attn_part = row_major(
        matmul_nt(after(heads_back, mamba), output_weight).astype(jnp.bfloat16)
    )
    mamba = after(mamba, attn_part, gate_up_w)
    attn = attn_part[:quarter].astype(jnp.float32)
    for shift in range(1, tp_count):
        back = [(s, (s - shift) % tp_count) for s in range(tp_count)]
        part = row_major(attn_part[shift * quarter : (shift + 1) * quarter])
        attn = attn + lax.ppermute(part, "tp", back).astype(jnp.float32)
    heads_cols = by_source([after(held, attn_part) for held in heads_held], "tp")
    heads_cols = heads_cols.reshape(rows, head_cols)

    grad_rows = spread_later(cotangent, mamba)
    scale_attn = inverse_rms(attn)
    normed_attn = attn * scale_attn
    scale_mamba = inverse_rms(mamba)
    normed_mamba = mamba * scale_mamba
    resid = stream_f + 0.5 * (normed_attn * attn_gain + normed_mamba * mamba_gain)
    scale_two = inverse_rms(resid)
    normed_two = resid * scale_two
    ffn_in = (normed_two * ffn_gain).astype(jnp.bfloat16)
    ffn_rows = spread(after(ffn_in, down_w))
    ffn_two = jnp.concatenate([ffn_rows, partner(ffn_rows, "seq", 0)], 0)
    grad_two = jnp.concatenate([grad_rows, partner(grad_rows, "seq", 0, gated)], 0)
    gate_up = matmul(ffn_two, gate_up_w)
    gate, up = gate_up[:, :wide], gate_up[:, wide:]
    activated = (jax.nn.silu(gate) * up).astype(jnp.bfloat16)

    grad_out = cotangent.astype(jnp.float32)
    grad_act_low = matmul(grad_two, down_w).astype(jnp.bfloat16)
    grad_gate = (grad_act_low * up * silu_slope(gate)).astype(jnp.bfloat16)
    grad_up = (grad_act_low * jax.nn.silu(gate)).astype(jnp.bfloat16)
    grad_gate_up = jnp.concatenate([grad_gate, grad_up], 1)

    def chip_tokens(value, weight):
        got = partner(matmul_nt(value[rows:], weight).astype(jnp.bfloat16), "seq", 0)
        return (matmul_nt(value[:rows], weight) + got.astype(jnp.float32)).astype(jnp.bfloat16)

    grad_ffn_part = chip_tokens(grad_gate_up, gate_up_w)
    grad_ffn_in = token_sums(grad_ffn_part)
    gate_up_late, activated_late = lax.optimization_barrier(
        (grad_gate_up, activated, grad_ffn_part)
    )[:2]
    gate_up_grads = matmul_tn(ffn_two, gate_up_late).astype(jnp.bfloat16)
    down_grads = matmul_tn(grad_two, activated_late).astype(jnp.bfloat16)
    bits = chip_bits()
    gate_up_sum = over_chips(gate_up_grads)
    down_x = Halving(down_grads, bits[::-1])
    layer_part = chip_tokens(activated_late, down_w)
    grad_ffn_in = after(grad_ffn_in, gate_up_grads, down_x.sent, layer_part)
    grad_ffn_gain = jnp.sum(grad_ffn_in * normed_two, 0)
    grad_resid = grad_out + rms_back(grad_ffn_in * ffn_gain, normed_two, scale_two)
    grad_attn_gain = 0.5 * jnp.sum(grad_resid * normed_attn, 0)
    grad_mamba_gain = 0.5 * jnp.sum(grad_resid * normed_mamba, 0)
    grad_attn = rms_back(0.5 * grad_resid * attn_gain, normed_attn, scale_attn).astype(jnp.bfloat16)
    grad_mamba = rms_back(0.5 * grad_resid * mamba_gain, normed_mamba, scale_mamba).astype(
        jnp.bfloat16
    )
    grad_mrows = spread(grad_mamba)
    grad_arows = exchange(
        jnp.broadcast_to(after(grad_attn, grad_mrows), (tp_count,) + grad_attn.shape), "tp"
    ).reshape(rows, -1)
    grad_gated = matmul(grad_mrows, mout).astype(jnp.bfloat16)
    grad_ssm = grad_gated * zgate
    grad_zgate = (grad_gated * ssm * silu_slope(zgate_in)).astype(jnp.bfloat16)
    grad_skip = jnp.sum(grad_ssm * mixed_in, 0)
    down_x.step(grad_mrows)
    backlog = block_end(True, size, grad_ssm, readout_wide, rate)
    block_backlogs = lax.all_gather(backlog, "seq")

    grad_head_cols = matmul(grad_arows, output_weight).astype(jnp.bfloat16)
    grad_heads = by_head(
        exchange(grad_head_cols.reshape(tp_count, quarter, head_cols), "tp")
    )
    grad_heads = after(grad_heads, down_x.sent)
    mrows_own, mrows_sib = row_sides(after(grad_mrows, grad_ssm))
    block_own, block_sib = row_sides(block_in)
    mout_send = core_send(mrows_sib, gated)
    zgate_send = core_send(block_sib, grad_zgate)
    grad_query, grad_window = attend_back(pieces, queries, probs, grad_heads)
    mout_held = core_sum(mrows_own, gated, mout_send, backlog)
    zgate_held = core_sum(block_own, grad_zgate, zgate_send, backlog)
    window_grad = lax.psum_scatter(after(grad_window, gate_up_sum), "tp", scatter_dimension=0, tiled=False)
    grad_query_cols = exchange(by_column(grad_query), "tp").reshape(rows, head_cols)
    head_grads = jnp.concatenate(
        [matmul_tn(grad_query_cols, block_in), matmul_tn(heads_cols, grad_arows)], 0
    )
    head_grads = head_grads.astype(jnp.bfloat16)
    head_sums = lax.psum(head_grads, "seq")
    mout_x = Halving(mout_held, bits[::-1])
    zgate_x = Halving(zgate_held, bits)
    before_scan = after(
        grad_ssm, mout_x.sent, zgate_x.sent
    )
    grad_drive, grad_size, grad_entry, grad_read, grad_rates = scan_backward(
        place, block_backlogs, size, drive, before_scan, readout_wide, rate, entry, states
    )
    grad_step = grad_size + grad_drive * mixed_in
    grad_inputs = grad_drive * step_size + grad_ssm * skip_scale
    grad_pre = grad_step * jax.nn.sigmoid(step_pre)
    grad_low = jnp.dot(grad_pre, step_weight.T, precision=HIGH)
    grad_low = jnp.concatenate(
        [grad_low, grad_entry.reshape(rows, STATE), grad_read.reshape(rows, STATE)], 1
    )
    grad_decay_log = grad_rates * decay
    grad_step_bias = jnp.sum(grad_pre, 0)
    grad_skip = jnp.sum(grad_ssm * mixed_in, 0)
    grad_step_weight = jnp.dot(step_low.T, grad_pre, precision=HIGH)
    grad_selected = all_sum(grad_low, ("tp",), jnp.bfloat16).astype(jnp.bfloat16)
    moved = [
        later(after(window_grad, grad_low)[:, (hops - hop) * rows : (hops - hop + 1) * rows], hop)
        for hop in range(1, hops + 1)
    ]
    grad_selected = after(grad_selected, window_grad)
    grad_inputs = grad_inputs + matmul_nt(grad_selected, select_weight)
    grad_conv = grad_inputs * silu_slope(conv_pre)
    grad_padded = sum(
        (
            jnp.pad(conv_kernel[tap] * grad_conv * taps[tap], ((tap, CONV - 1 - tap), (0, 0)))
            for tap in range(CONV)
        )
    )
    returned = later(grad_padded[: CONV - 1].astype(jnp.bfloat16), 1).astype(jnp.float32)
    grad_inner = (
        grad_padded[CONV - 1 :] + jnp.pad(returned, ((rows - (CONV - 1), 0), (0, 0)))
    ).astype(jnp.bfloat16)
    down_sum = down_x.finish(grad_selected)
    mout_x.step(grad_selected)
    zgate_x.step(grad_selected)
    layer_sums = token_sums(after(layer_part, grad_gated), grad_low)
    layer_out = (resid + layer_sums).astype(jnp.bfloat16)
    grad_pairs = window_grad[:, hops * rows :].astype(jnp.float32)
    for part in moved:
        grad_pairs = grad_pairs + after(part, grad_conv).astype(jnp.float32)
    grad_pair_low = grad_pairs.astype(jnp.bfloat16)
    pair_grads = matmul(grad_pair_low, block_in)
    grad_inner = after(grad_inner, mout_x.sent, zgate_x.sent, pair_grads)
    proj_send = core_send(block_sib, grad_inner)
    proj_x = Halving(core_sum(block_own, grad_inner, proj_send), bits[::-1])
    tail = proj_x.sent
    pair_grads = all_sum(pair_grads, ("seq",), jnp.bfloat16, [tail] * (len(bits) + 1))
    grad_block_rest = (
        matmul_nt(grad_zgate, zproj)
        + matmul_nt(grad_query_cols, query_weight)
        + lax.dot_general(
            grad_pair_low,
            pair_weight,
            (((0,), (1,)), ((), ())),
            preferred_element_type=jnp.float32,
        )
    )
    grad_block_in = matmul_nt(after(grad_inner, proj_send), proj) + grad_block_rest
    block_in_low = row_major(grad_block_in.astype(jnp.bfloat16))
    block_in_pieces = received(block_in_low.reshape(tp_count, quarter, -1), "tp")
    proj_sum = proj_x.finish()
    grad_mixer_in = sum(
        after(piece, tail).astype(jnp.float32) for piece in block_in_pieces
    )
    stream_grad = (grad_resid + rms_back(grad_mixer_in * mixer_gain, normed_one, scale_one)).astype(
        jnp.bfloat16
    )
    grad_mixer_gain = jnp.sum(after(grad_block_in, tail) * block_normed, 0)
    gain_parts = jnp.stack([grad_mixer_gain, grad_attn_gain, grad_mamba_gain, grad_ffn_gain])
    gain_parts = all_sum(gain_parts, ("tp",), jnp.float32)
    grad_select = matmul_tn(grad_selected, mixed_low)
    grad_conv_bias = jnp.sum(grad_conv, 0)
    grad_kernel = jnp.stack(
        [jnp.sum(grad_conv * padded[tap : tap + rows] * taps[tap], 0) for tap in range(CONV)]
    )
    width = grad_skip.shape[0]
    gain_rows = -(-gain_parts.size // width)
    gain_flat = jnp.pad(gain_parts.reshape(-1), (0, gain_rows * width - gain_parts.size))
    aligned = [
        gain_flat.reshape(gain_rows, width),
        grad_kernel,
        jnp.stack([grad_conv_bias, grad_step_bias, grad_skip, jnp.zeros_like(grad_skip)]),
        grad_decay_log,
        jnp.pad(grad_select, ((0, -grad_select.shape[0] % HALF), (0, 0))),
        jnp.pad(grad_step_weight, ((0, -STEP_RANK % HALF), (0, 0))),
    ]
    small = jnp.concatenate(aligned, 0).astype(jnp.bfloat16)
    small = all_sum(after(small, tail), ("seq",), jnp.bfloat16)
    mout_sum = mout_x.finish(tail)
    zgate_sum = zgate_x.finish(tail)
    gate_grad, up_grad = core_rows_back(gate_up_sum, 2, half, tail)
    (down_grad,) = core_rows_back(down_sum, 1, half, tail)
    head_sums = after(head_sums, proj_sum).astype(jnp.float32)
    ranks = STEP_RANK + 2 * STATE
    starts = [0]
    for part in aligned:
        starts.append(starts[-1] + part.shape[0])
    gain_totals = small[: starts[1]].reshape(-1)[: gain_parts.size].reshape(gain_parts.shape)
    conv_at, lone_at, decay_at, select_at, step_at = starts[1:6]
    return (
        layer_out,
        stream_grad,
        gain_totals[0],
        head_sums[:head_cols].T,
        pair_grads[:pair_cols].T,
        pair_grads[pair_cols:].T,
        head_sums[head_cols:].T,
        gain_totals[1],
        gain_totals[2],
        proj_sum,
        zgate_sum,
        small[conv_at : conv_at + CONV],
        small[lone_at],
        small[select_at : select_at + ranks].T,
        small[step_at : step_at + STEP_RANK],
        small[lone_at + 1],
        small[decay_at : decay_at + STATE].T,
        small[lone_at + 2],
        mout_sum,
        gain_totals[3],
        gate_grad,
        up_grad,
        down_grad,
    )


def solution(mesh):
    return jax.shard_map(
        on_device,
        mesh=mesh,
        in_specs=(
            P(("seq", "tp"), None),
            P(("seq", "tp"), None),
            P(),
            P(),
            P(None, "tp"),
            P(None, "tp"),
            P(None, "tp"),
            P(None, "tp"),
            P(),
            P(),
            P("seq", "tp"),
            P("seq", "tp"),
            P(None, "tp"),
            P("tp"),
            P("tp", None),
            P(None, "tp"),
            P("tp"),
            P("tp", None),
            P("tp"),
            P("seq", "tp"),
            P(),
            P("seq", "tp"),
            P("seq", "tp"),
            P("seq", "tp"),
        ),
        out_specs=(
            P(("seq", "tp"), None),
            P(("seq", "tp"), None),
            P(),
            P(None, "tp"),
            P(None, "tp"),
            P(None, "tp"),
            P(None, "tp"),
            P(),
            P(),
            P("seq", "tp"),
            P("seq", "tp"),
            P(None, "tp"),
            P("tp"),
            P("tp", None),
            P(None, "tp"),
            P("tp"),
            P("tp", None),
            P("tp"),
            P("seq", "tp"),
            P(),
            P("seq", "tp"),
            P("seq", "tp"),
            P("seq", "tp"),
        ),
        check_vma=False,
    )
```

```python
import jax
import jax.numpy as jnp
from jax import lax
from jax.experimental import pallas as pl
from jax.experimental.layout import Layout, with_layout_constraint
from jax.experimental.pallas import tpu as pltpu
from jax.sharding import PartitionSpec as P
from functools import partial

D = 1600
HEADS = 25
KV_HEADS = 5
HEAD_DIM = 64
STATE = 16
CONV = 4
STEP_RANK = 100
WINDOW = 1024
TOK_DEV = 256
EPS = 1e-06
HIGH = lax.Precision.HIGHEST
NT = (((1,), (1,)), ((), ()))
LANES = 128
HALF = 8
CHUNK = 16
LOG2E = 1.4426950408889634
LN2 = 0.6931471805599453
FAR = 1e6
VMEM_LIMIT = 48 * 1024 * 1024


def lane_groups(width):
    return [(start, min(LANES, width - start)) for start in range(0, width, LANES)]


def tiles(width):
    return [(s, w, n) for s, w in lane_groups(width) for n in range(0, STATE, HALF)]


def spread_row(ref, row):
    return ref[pl.ds(row, 1), :]


def widened(width):
    return -(-width // LANES) * LANES


def end_kernel(reverse, size_in, drive_in, vec_ref, rate_ref, out_ref, size_ref, drive_ref):
    total, width = size_in.shape
    parts = tiles(width)
    size_ref[:, :width] = size_in[...]
    drive_ref[:, :width] = drive_in[...]

    def chunk_step(chunk, held):
        held = list(held)
        at = total // CHUNK - 1 - chunk if reverse else chunk
        for k in range(CHUNK - 1, -1, -1) if reverse else range(CHUNK):
            t = at * CHUNK + k
            sizes = spread_row(size_ref, t)
            drives = spread_row(drive_ref, t)
            for i, (s, w, n) in enumerate(parts):
                size, drive = sizes[:, s : s + w], drives[:, s : s + w]
                factor = jnp.exp2(size * rate_ref[n : n + HALF, s : s + w])
                push = drive * vec_ref[t, n : n + HALF, :w]
                held[i] = factor * (held[i] + push) if reverse else factor * held[i] + push
        return tuple(held)

    held = lax.fori_loop(
        0,
        total // CHUNK,
        chunk_step,
        tuple(jnp.zeros((HALF, w), jnp.float32) for _, w, _ in parts),
    )
    for i, (s, w, n) in enumerate(parts):
        out_ref[n : n + HALF, s : s + w] = held[i]
    out_ref[STATE:, :] = jnp.broadcast_to(
        jnp.sum(size_in[...], 0, keepdims=True), (out_ref.shape[0] - STATE, width)
    )


def entering(reverse, place_ref, ends_ref, rate_ref, into_ref):
    count = ends_ref.shape[0]
    into_ref[...] = jnp.zeros(into_ref.shape, jnp.float32)

    def one(step, carry):
        at = count - 1 - step if reverse else step
        decay = jnp.exp2(rate_ref[...] * ends_ref[at, STATE : STATE + 1, :])
        into_ref[...] = decay * into_ref[...] + ends_ref[at, 0:STATE, :]
        return carry

    lax.fori_loop(0, count - 1 - place_ref[0] if reverse else place_ref[0], one, 0)


def block_mask():
    span = CHUNK * STATE
    row = lax.broadcasted_iota(jnp.int32, (CHUNK, span), 0)
    col = lax.broadcasted_iota(jnp.int32, (CHUNK, span), 1)
    return (col >= row * STATE) & (col < (row + 1) * STATE)


def repeat_matrix():
    span = CHUNK * STATE
    row = lax.broadcasted_iota(jnp.int32, (STATE, span), 0)
    col = lax.broadcasted_iota(jnp.int32, (STATE, span), 1)
    return (lax.rem(col, STATE) == row).astype(jnp.bfloat16)


def picked(vec, mine, repeat):
    wide = jnp.dot(vec.astype(jnp.bfloat16), repeat, preferred_element_type=jnp.float32)
    return jnp.where(mine, wide, 0.0).astype(jnp.bfloat16)


def scan_kernel(
    place_ref, ends_ref, size_in, drive_in, vec_ref, rate_ref, pick_ref,
    y_ref, states_ref, into_ref, size_ref, drive_ref,
):
    total, width = size_in.shape
    parts = tiles(width)
    size_ref[:, :width] = size_in[...]
    drive_ref[:, :width] = drive_in[...]
    entering(False, place_ref, ends_ref, rate_ref, into_ref)
    states_ref[0:STATE, :] = into_ref[...].astype(jnp.bfloat16)
    mine = block_mask()
    repeat = repeat_matrix()

    def chunk_step(chunk, held):
        held = list(held)
        base = chunk * (CHUNK * STATE) + STATE
        for k in range(CHUNK):
            t = chunk * CHUNK + k
            sizes = spread_row(size_ref, t)
            drives = spread_row(drive_ref, t)
            for i, (s, w, n) in enumerate(parts):
                size, drive = sizes[:, s : s + w], drives[:, s : s + w]
                factor = jnp.exp2(size * rate_ref[n : n + HALF, s : s + w])
                held[i] = factor * held[i] + drive * vec_ref[t, n : n + HALF, :w]
                if n == HALF:
                    states_ref[pl.ds(pl.multiple_of(base + k * STATE, STATE), STATE), s : s + w] = (
                        jnp.concatenate([held[i - 1], held[i]], 0).astype(jnp.bfloat16)
                    )
        rows = pl.ds(pl.multiple_of(base, STATE), CHUNK * STATE)
        y_ref[pl.ds(pl.multiple_of(chunk * CHUNK, CHUNK), CHUNK), :] = jnp.dot(
            picked(pick_ref[pl.ds(pl.multiple_of(chunk * CHUNK, CHUNK), CHUNK), :], mine, repeat),
            states_ref[rows, :],
            preferred_element_type=jnp.float32,
        )
        return tuple(held)

    lax.fori_loop(
        0,
        total // CHUNK,
        chunk_step,
        tuple(into_ref[n : n + HALF, s : s + w] for s, w, n in parts),
    )


def back_kernel(
    place_ref, ends_ref, size_in, drive_ref, grad_in, vec_ref, rate_ref, pick_ref, states_ref,
    gdrive_ref, gsize_ref, gentry_ref, gread_ref, grate_ref,
    into_ref, adj_ref, slope_ref, size_ref, grad_ref,
):
    total, width = size_in.shape
    parts = tiles(width)
    size_ref[:, :width] = size_in[...]
    grad_ref[:, :width] = grad_in[...]
    span = CHUNK * STATE
    entering(True, place_ref, ends_ref, rate_ref, into_ref)
    own = block_mask()
    repeat = repeat_matrix()
    mine = own.astype(jnp.float32)
    ones = mine.astype(jnp.bfloat16)
    grate_ref[...] = jnp.zeros(grate_ref.shape, jnp.float32)

    def chunk_step(step, held):
        held = list(held)
        chunk = total // CHUNK - 1 - step
        rates = [jnp.zeros((HALF, w), jnp.float32) for _, w, _ in parts]
        for k in range(CHUNK - 1, -1, -1):
            t = chunk * CHUNK + k
            sizes = spread_row(size_ref, t)
            grads = spread_row(grad_ref, t)
            for i, (s, w, n) in enumerate(parts):
                if n != 0:
                    continue
                size, grad = sizes[:, s : s + w], grads[:, s : s + w]
                before = states_ref[pl.ds(pl.multiple_of(t * STATE, STATE), STATE), s : s + w].astype(
                    jnp.float32
                )
                adjs, slopes = [], []
                for j in range(2):
                    n0 = j * HALF
                    rate = rate_ref[n0 : n0 + HALF, s : s + w]
                    adj = grad * vec_ref[t, n0 : n0 + HALF, :w] + held[i + j]
                    held[i + j] = jnp.exp2(size * rate) * adj
                    moved = held[i + j] * before[n0 : n0 + HALF]
                    rates[i + j] = rates[i + j] + moved * size
                    adjs.append(adj)
                    slopes.append(moved * rate)
                at = slice(k * STATE, (k + 1) * STATE)
                adj_ref[at, s : s + w] = jnp.concatenate(adjs, 0).astype(jnp.bfloat16)
                slope_ref[at, s : s + w] = jnp.concatenate(slopes, 0).astype(jnp.bfloat16)
        for i, (s, w, n) in enumerate(parts):
            grate_ref[n : n + HALF, s : s + w] += rates[i]
        here = pl.ds(pl.multiple_of(chunk * CHUNK, CHUNK), CHUNK)
        gdrive_ref[here, :] = jnp.dot(
            picked(pick_ref[here, :], own, repeat), adj_ref[...], preferred_element_type=jnp.float32
        )
        gsize_ref[here, :] = (
            jnp.dot(ones, slope_ref[...], preferred_element_type=jnp.float32) * LN2
        )
        nt = (((1,), (1,)), ((), ()))
        gentry_ref[pl.ds(chunk, 1), :] = jnp.sum(
            mine
            * lax.dot_general(
                drive_ref[here, :].astype(jnp.bfloat16), adj_ref[...], nt,
                preferred_element_type=jnp.float32,
            ),
            0, keepdims=True,
        )
        rows = pl.ds(pl.multiple_of(chunk * span + STATE, STATE), span)
        gread_ref[pl.ds(chunk, 1), :] = jnp.sum(
            mine
            * lax.dot_general(
                grad_in[here, :].astype(jnp.bfloat16), states_ref[rows, :], nt,
                preferred_element_type=jnp.float32,
            ),
            0, keepdims=True,
        )
        return tuple(held)

    lax.fori_loop(
        0,
        total // CHUNK,
        chunk_step,
        tuple(into_ref[n : n + HALF, s : s + w] for s, w, n in parts),
    )


def cost(total, width, flops, exps, extra):
    cells = total * width * STATE
    return pl.CostEstimate(
        flops=cells * flops, transcendentals=cells * exps, bytes_accessed=total * width * 12 + extra
    )


def rows_scratch(total, width):
    return [pltpu.VMEM((total, widened(width)), jnp.float32)] * 2


def kernel_call(body, outs, scratch, smem, args, estimate):
    vmem = pl.BlockSpec(memory_space=pltpu.VMEM)
    return pl.pallas_call(
        body,
        out_shape=outs,
        in_specs=[pl.BlockSpec(memory_space=pltpu.SMEM)] * smem + [vmem] * (len(args) - smem),
        out_specs=jax.tree.map(lambda _: vmem, outs),
        scratch_shapes=scratch,
        compiler_params=pltpu.CompilerParams(vmem_limit_bytes=VMEM_LIMIT),
        cost_estimate=estimate,
    )(*args)


def block_end(reverse, size, drive, vec, rate):
    total, width = size.shape
    return kernel_call(
        partial(end_kernel, reverse),
        jax.ShapeDtypeStruct((STATE + HALF, width), jnp.float32),
        rows_scratch(total, width), 0, (size, drive, vec, rate),
        cost(total, width, 5, 1, 0),
    )


def scan_forward(place, ends, size, drive, vec, rate, pick):
    total, width = size.shape
    return kernel_call(
        scan_kernel,
        (
            jax.ShapeDtypeStruct((total, width), jnp.float32),
            jax.ShapeDtypeStruct(((total + 1) * STATE, width), jnp.bfloat16),
        ),
        [pltpu.VMEM((STATE, width), jnp.float32)] + rows_scratch(total, width),
        1, (place, ends, size, drive, vec, rate, pick),
        cost(total, width, 6, 1, total * width * 32),
    )


def scan_backward(place, ends, size, drive, grad, vec, rate, pick, states):
    total, width = size.shape
    span = CHUNK * STATE
    return kernel_call(
        back_kernel,
        (
            jax.ShapeDtypeStruct((total, width), jnp.float32),
            jax.ShapeDtypeStruct((total, width), jnp.float32),
            jax.ShapeDtypeStruct((total // CHUNK, span), jnp.float32),
            jax.ShapeDtypeStruct((total // CHUNK, span), jnp.float32),
            jax.ShapeDtypeStruct((STATE, width), jnp.float32),
        ),
        [
            pltpu.VMEM((STATE, width), jnp.float32),
            pltpu.VMEM((span, width), jnp.bfloat16),
            pltpu.VMEM((span, width), jnp.bfloat16),
        ]
        + rows_scratch(total, width),
        1, (place, ends, size, drive, grad, vec, rate, pick, states),
        cost(total, width, 12, 1, total * width * 32),
    )


def lanes_of(vec):
    return jnp.broadcast_to(vec[:, :, None], vec.shape + (LANES,))


def piece_of(head, cols):
    first = lax.div(head * HEAD_DIM, cols)
    last = lax.div(head * HEAD_DIM + HEAD_DIM - 1, cols)
    return first, last, jnp.where(last > first, 1.0, 0.0).astype(jnp.bfloat16)


def pick_head(head, piece, cols, start, width):
    row = lax.broadcasted_iota(jnp.int32, (2 * cols, width), 0)
    lane = lax.broadcasted_iota(jnp.int32, (2 * cols, width), 1)
    source = piece * cols + row
    key = (row < cols) & (lane < HEAD_DIM) & (source == head * HEAD_DIM + lane)
    value = (
        (row >= cols)
        & (lane >= HEAD_DIM)
        & (source - cols == head * HEAD_DIM + lane - HEAD_DIM)
    )
    return (key | value).astype(jnp.bfloat16)


def head_pairs(head, pieces, pair_ref):
    cols = pieces[0].shape[2] // 2
    rows = pieces[0].shape[1]
    first, last, two = piece_of(head, cols)
    pick_first = pick_head(head, first, cols, 0, 2 * HEAD_DIM)
    pick_last = pick_head(head, last, cols, 0, 2 * HEAD_DIM) * two
    for block, ref in enumerate(pieces):
        pair = jnp.dot(ref[first], pick_first, preferred_element_type=jnp.float32) + jnp.dot(
            ref[last], pick_last, preferred_element_type=jnp.float32
        )
        pair_ref[block * rows : (block + 1) * rows, :] = pair.astype(jnp.bfloat16)


def attend_kernel(count, *refs):
    pieces = refs[:count]
    offset_ref, query_seg_ref, key_seg_ref, query_ref, probs_ref, heads_ref = refs[count : count + 6]
    pair_ref, score_ref = refs[count + 6 :]
    head = pl.program_id(0)
    head_pairs(head, pieces, pair_ref)
    quarter = query_seg_ref.shape[0]
    span = key_seg_ref.shape[1]
    row = lax.broadcasted_iota(jnp.int32, (quarter, span), 0)
    col = lax.broadcasted_iota(jnp.int32, (quarter, span), 1)
    distance = row + offset_ref[0] - col
    allowed = (
        (distance >= 0) & (distance < WINDOW) & (query_seg_ref[...] == key_seg_ref[...])
    )
    score_ref[...] = lax.dot_general(
        query_ref[0], pair_ref[:, :HEAD_DIM], NT, preferred_element_type=jnp.float32
    )
    for group in range(query_ref.shape[1] // quarter):
        at = slice(group * quarter, (group + 1) * quarter)
        scores = jnp.where(allowed, score_ref[at, :] * HEAD_DIM ** (-0.5), -1e30)
        raised = jnp.exp(scores - jnp.max(scores, -1, keepdims=True))
        share = 1.0 / jnp.sum(raised, -1, keepdims=True)
        probs_ref[0, at, :] = (raised * share).astype(jnp.bfloat16)
    heads_ref[0] = jnp.dot(
        probs_ref[0], pair_ref[:, HEAD_DIM:], preferred_element_type=jnp.float32
    ).astype(jnp.bfloat16)


def attend_back_kernel(count, *refs):
    pieces = refs[:count]
    query_ref, probs_ref, grad_ref, gquery_ref, gwindow_ref = refs[count : count + 5]
    pair_ref, gprob_ref, gscore_ref = refs[count + 5 :]
    head = pl.program_id(0)
    cols = pieces[0].shape[2] // 2
    first, last, two = piece_of(head, cols)
    head_pairs(head, pieces, pair_ref)
    gprob_ref[...] = lax.dot_general(
        grad_ref[0], pair_ref[:, HEAD_DIM:], NT, preferred_element_type=jnp.float32
    )
    step = HEAD_DIM
    for at in range(0, gprob_ref.shape[0], step):
        probs = probs_ref[0, at : at + step, :].astype(jnp.float32)
        both = probs * gprob_ref[at : at + step, :]
        gscore_ref[at : at + step, :] = (
            both - probs * jnp.sum(both, -1, keepdims=True)
        ).astype(jnp.bfloat16)
    scale = HEAD_DIM ** (-0.5)
    gquery_ref[0] = (
        jnp.dot(gscore_ref[...], pair_ref[:, :HEAD_DIM], preferred_element_type=jnp.float32) * scale
    ).astype(jnp.bfloat16)
    row = lax.broadcasted_iota(jnp.int32, (HEAD_DIM, HEAD_DIM), 0)
    lane = lax.broadcasted_iota(jnp.int32, (HEAD_DIM, HEAD_DIM), 1)
    unit = (row == lane).astype(jnp.bfloat16)

    def turned(value):
        return lax.dot_general(unit, value, NT, preferred_element_type=jnp.float32).astype(
            jnp.bfloat16
        )

    gkey = jnp.dot(turned(query_ref[0]), gscore_ref[...], preferred_element_type=jnp.float32)
    gvalue = jnp.dot(turned(grad_ref[0]), probs_ref[0], preferred_element_type=jnp.float32)
    gpair = jnp.concatenate([gkey * scale, gvalue], 0).astype(jnp.bfloat16)

    @pl.when(head == 0)
    def _():
        gwindow_ref[...] = jnp.zeros(gwindow_ref.shape, jnp.bfloat16)

    def add(piece, weight):
        pick = pick_head(head, piece, cols, 0, 2 * HEAD_DIM) * weight
        part = jnp.dot(pick, gpair, preferred_element_type=jnp.float32)
        gwindow_ref[piece] = (gwindow_ref[piece].astype(jnp.float32) + part).astype(jnp.bfloat16)

    add(first, jnp.ones((), jnp.bfloat16))
    add(last, two)


def whole(shape):
    return pl.BlockSpec(shape, lambda head: (0,) * len(shape))


def of_head(shape):
    return pl.BlockSpec((1,) + shape[1:], lambda head: (head,) + (0,) * (len(shape) - 1))


def attend(pieces, offset, query_seg, key_seg, queries):
    heads, rows, dim = queries.shape
    span = key_seg.shape[1]
    outs = (
        jax.ShapeDtypeStruct((heads, rows, span), jnp.bfloat16),
        jax.ShapeDtypeStruct(queries.shape, jnp.bfloat16),
    )
    return pl.pallas_call(
        partial(attend_kernel, len(pieces)),
        grid=(heads,),
        out_shape=outs,
        in_specs=[whole(p.shape) for p in pieces]
        + [pl.BlockSpec(memory_space=pltpu.SMEM), whole(query_seg.shape), whole(key_seg.shape)]
        + [of_head(queries.shape)],
        out_specs=tuple(of_head(o.shape) for o in outs),
        scratch_shapes=[
            pltpu.VMEM((span, 2 * dim), jnp.bfloat16),
            pltpu.VMEM((rows, span), jnp.float32),
        ],
        compiler_params=pltpu.CompilerParams(vmem_limit_bytes=VMEM_LIMIT),
        cost_estimate=pl.CostEstimate(
            flops=4 * heads * rows * span * dim,
            transcendentals=heads * rows * span,
            bytes_accessed=2 * heads * rows * span + 4 * queries.size,
        ),
    )(*pieces, offset, query_seg, key_seg, queries)


def attend_back(pieces, queries, probs, grads):
    heads, rows, dim = queries.shape
    span = probs.shape[2]
    outs = (
        jax.ShapeDtypeStruct(queries.shape, jnp.bfloat16),
        jax.ShapeDtypeStruct((pieces[0].shape[0], pieces[0].shape[2], span), jnp.bfloat16),
    )
    return pl.pallas_call(
        partial(attend_back_kernel, len(pieces)),
        grid=(heads,),
        out_shape=outs,
        in_specs=[whole(p.shape) for p in pieces]
        + [of_head(queries.shape), of_head(probs.shape), of_head(grads.shape)],
        out_specs=(of_head(outs[0].shape), whole(outs[1].shape)),
        scratch_shapes=[
            pltpu.VMEM((span, 2 * dim), jnp.bfloat16),
            pltpu.VMEM((rows, span), jnp.float32),
            pltpu.VMEM((rows, span), jnp.bfloat16),
        ],
        compiler_params=pltpu.CompilerParams(vmem_limit_bytes=VMEM_LIMIT),
        cost_estimate=pl.CostEstimate(
            flops=8 * heads * rows * span * dim,
            transcendentals=0,
            bytes_accessed=4 * heads * rows * span,
        ),
    )(*pieces, queries, probs, grads)


def passed_along(value, axis, steps):
    count = lax.axis_size(axis)
    first, last = (max(0, -steps), min(count, count - steps))
    return lax.ppermute(value, axis, [(source, source + steps) for source in range(first, last)])


def after(value, *others):
    return lax.optimization_barrier((value, *others))[0]


def partner(value, axis, bit, when=None):
    count = lax.axis_size(axis)
    got = lax.ppermute(value, axis, [(s, s ^ (1 << bit)) for s in range(count)])
    return got if when is None else after(got, when)


def all_sum(value, axes, kind, whens=()):
    whens = list(whens)
    for axis in axes:
        count = lax.axis_size(axis)
        bits = count.bit_length() - 1
        if count != 1 << bits:
            value = lax.psum(value, axis)
            continue
        for bit in range(bits):
            low = value.astype(kind)
            got = partner(low, axis, bit, whens.pop(0) if whens else None)
            value = low.astype(jnp.float32) + got.astype(jnp.float32)
    return value


class Halving:
    def __init__(self, value, order):
        self.order = list(order)
        self.left = sorted(order, reverse=True)
        self.split(value.astype(jnp.bfloat16).reshape([2] * len(self.left) + [-1, value.shape[1]]))

    def split(self, held):
        self.bit = self.order.pop(0)
        axis = self.left.index(self.bit)
        self.left.remove(self.bit)
        mine = (lax.axis_index("seq") >> self.bit) & 1
        self.sent = lax.dynamic_index_in_dim(held, 1 - mine, axis, False)
        self.kept = lax.dynamic_index_in_dim(held, mine, axis, False)

    def step(self, when=None):
        got = partner(self.sent, "seq", self.bit, when)
        total = self.kept.astype(jnp.float32) + got.astype(jnp.float32)
        if self.order:
            self.split(total.astype(jnp.bfloat16))
        return total

    def finish(self, when=None):
        while self.order:
            self.step(when)
        return self.step(when)


def chip_bits():
    return list(range(1, lax.axis_size("seq").bit_length() - 1))


def row_sides(value):
    blocks = lax.axis_size("seq")
    turned = value.T.reshape(blocks // 2, 2, -1, value.shape[0])
    mine = lax.axis_index("seq") & 1
    return [
        lax.dynamic_index_in_dim(turned, side, 1, False).reshape(-1, value.shape[0])
        for side in (mine, 1 - mine)
    ]


def core_send(left_sib, right):
    return matmul(left_sib, right).astype(jnp.bfloat16)


def core_sum(left_own, right, send, when=None):
    got = partner(send, "seq", 0, when)
    return (matmul(left_own, right) + got.astype(jnp.float32)).astype(jnp.bfloat16)


def first_core():
    return (lax.axis_index("seq") & 1) == 0


def core_order(mine, other):
    first = first_core()
    return jnp.where(first, mine, other), jnp.where(first, other, mine)


def chip_groups():
    count = lax.axis_size("seq")
    return [[c for c in range(count) if c % 2 == p] for p in range(2)]


def core_columns(weights, padded_to):
    pad = [(0, 0), (0, padded_to - weights[0].shape[1] // 2)]
    low = jnp.concatenate([jnp.pad(w[:, : w.shape[1] // 2], pad) for w in weights], 1)
    high = jnp.concatenate([jnp.pad(w[:, w.shape[1] // 2 :], pad) for w in weights], 1)
    first = first_core()
    mine, other = jnp.where(first, low, high), jnp.where(first, high, low)
    return jnp.concatenate(core_order(mine, partner(other, "seq", 0)), 0)


def core_rows_back(held, count, width, when):
    mine = lax.axis_index("seq") & 1
    both = held.reshape(2, -1, held.shape[-1])
    kept = lax.dynamic_index_in_dim(both, mine, 0, False)
    sent = lax.dynamic_index_in_dim(both, 1 - mine, 0, False).astype(jnp.bfloat16)
    low, high = core_order(kept, partner(sent, "seq", 0, when).astype(kept.dtype))
    step = held.shape[-1] // count
    return [
        jnp.concatenate([low[:, at : at + width], high[:, at : at + width]], 1).astype(jnp.float32)
        for at in range(0, count * step, step)
    ]


def received(pieces, axis):
    count = lax.axis_size(axis)
    place = lax.axis_index(axis)
    held = []
    for shift in range(count):
        sent = row_major(lax.dynamic_index_in_dim(pieces, (place + shift) % count, 0, False))
        held.append(
            lax.ppermute(sent, axis, [(s, (s + shift) % count) for s in range(count)])
            if shift
            else sent
        )
    return held


def by_source(held, axis):
    count = lax.axis_size(axis)
    place = lax.axis_index(axis)
    held = jnp.stack(held)
    return jnp.stack(
        [
            lax.dynamic_index_in_dim(held, (place - source) % count, 0, False)
            for source in range(count)
        ]
    )


def exchange(pieces, axis):
    return lax.all_to_all(pieces, axis, 0, 0, tiled=True)


def spread_direct(value, axis, when):
    count = lax.axis_size(axis)
    value = row_major(value)
    held = [value]
    for shift in range(1, count):
        got = lax.ppermute(value, axis, [(s, (s + shift) % count) for s in range(count)])
        held.append(after(got, when))
    return by_source(held, axis)


def inverse_rms(value):
    return lax.rsqrt(jnp.mean(value * value, -1, keepdims=True) + EPS)


def rms_back(grad_normed, normed, scale):
    return scale * (grad_normed - normed * jnp.mean(grad_normed * normed, -1, keepdims=True))


def silu_slope(value):
    sigma = jax.nn.sigmoid(value)
    return sigma * (1.0 + value * (1.0 - sigma))


def matmul(left, right):
    return jnp.dot(left, right, preferred_element_type=jnp.float32)


def matmul_nt(left, right):
    return lax.dot_general(
        left, right, (((1,), (1,)), ((), ())), preferred_element_type=jnp.float32
    )


def row_major(value):
    order = tuple(range(value.ndim))
    return with_layout_constraint(value, Layout(major_to_minor=order))


def matmul_tn(left, right):
    return lax.dot_general(
        left, right, (((0,), (0,)), ((), ())), preferred_element_type=jnp.float32
    )


def on_device(
    stream,
    cotangent,
    segments,
    mixer_gain,
    query_weight,
    key_weight,
    value_weight,
    output_weight,
    attn_gain,
    mamba_gain,
    inner_proj,
    inner_gate,
    conv_kernel,
    conv_bias,
    select_weight,
    step_weight,
    step_bias,
    decay_log,
    skip_scale,
    mamba_out,
    ffn_gain,
    ffn_gate,
    ffn_up,
    ffn_down,
):
    seq_count = lax.axis_size("seq")
    tp_count = lax.axis_size("tp")
    seq_index = lax.axis_index("seq")
    tp_index = lax.axis_index("tp")
    quarter = stream.shape[0]
    rows = TOK_DEV
    hops = (WINDOW + TOK_DEV - 1) // TOK_DEV
    span = (hops + 1) * rows
    key_width = KV_HEADS * HEAD_DIM
    groups = HEADS // KV_HEADS
    head_cols = query_weight.shape[1]
    pair_cols = key_weight.shape[1]

    def spread(value):
        return lax.all_gather(value, "tp", axis=0, tiled=True)

    def spread_later(value, when):
        return spread_direct(value, "tp", when).reshape(rows, -1)

    def token_sums(value, when=None):
        value = row_major(value.astype(jnp.bfloat16))
        pieces = received(value.reshape(tp_count, quarter, -1), "tp")
        if when is not None:
            pieces = [after(piece, when) for piece in pieces]
        return sum(piece.astype(jnp.float32) for piece in pieces)

    def token_sums_late(value):
        pieces = exchange(value.astype(jnp.bfloat16).reshape(tp_count, quarter, -1), "tp")
        return jnp.sum(pieces.astype(jnp.float32), 0)

    def earlier(value, hop):
        return passed_along(value, "seq", hop)

    def later(value, hop):
        return passed_along(value, "seq", -hop)

    def whole_rows(weight):
        return lax.all_gather(weight, "seq", axis=0, tiled=True)

    def from_chips(value):
        return lax.all_gather(
            value, "seq", axis=0, tiled=True, axis_index_groups=chip_groups()
        )

    def over_chips(value):
        return lax.psum_scatter(
            value, "seq", scatter_dimension=0, tiled=True, axis_index_groups=chip_groups()
        )

    def own_cols(value):
        return value.reshape(quarter, tp_count, -1).transpose(1, 0, 2)

    proj = whole_rows(inner_proj)
    wide_cols = -(-inner_gate.shape[1] // LANES) * LANES
    pad_cols = ((0, 0), (0, wide_cols - inner_gate.shape[1]))
    ssm_pair = whole_rows(
        jnp.concatenate([jnp.pad(inner_gate, pad_cols), jnp.pad(mamba_out, pad_cols)], 1)
    )
    zproj = ssm_pair[:, : inner_gate.shape[1]]
    mout = ssm_pair[:, wide_cols : wide_cols + mamba_out.shape[1]]
    block_stream = spread(stream)
    (
        block_stream, stream, cotangent, segments, key_weight, value_weight, conv_kernel,
        conv_bias, decay_log, ffn_gate, ffn_up, ffn_down,
    ) = lax.optimization_barrier(
        (
            block_stream, stream, cotangent, segments, key_weight, value_weight, conv_kernel,
            conv_bias, decay_log, ffn_gate, ffn_up, ffn_down,
        )
    )
    block_stream = block_stream.astype(jnp.float32)
    base = seq_index * rows
    first_row = base + tp_index * quarter
    stream_f = stream.astype(jnp.float32)
    scale_one = inverse_rms(stream_f)
    normed_one = stream_f * scale_one
    block_normed = block_stream * inverse_rms(block_stream)
    block_in = (block_normed * mixer_gain).astype(jnp.bfloat16)
    pair_weight = jnp.concatenate([key_weight, value_weight], 1)
    query_cols = matmul(block_in, query_weight).astype(jnp.bfloat16)
    pair_part = matmul(block_in, pair_weight).astype(jnp.bfloat16)
    block_late = after(block_in, query_cols, pair_part)
    inner = matmul(block_late, proj).astype(jnp.bfloat16)
    half = ffn_gate.shape[1] // 2
    wide = -(-half // 256) * 256
    ffn_here = core_columns([after(ffn_gate, inner), ffn_up, ffn_down], wide)
    ffn_w = from_chips(ffn_here)
    gate_up_w, down_w = ffn_w[:, : 2 * wide], ffn_w[:, 2 * wide :]
    block_pairs = spread_direct(pair_part, "tp", inner)
    edge = earlier(inner[rows - (CONV - 1) :], 1)
    seg_conv = lax.dynamic_slice_in_dim(
        jnp.concatenate([jnp.full((CONV - 1,), -1, jnp.int32), segments]), base, rows + CONV - 1, 0
    )
    own_seg = seg_conv[CONV - 1 :]
    taps = [
        (seg_conv[tap : tap + rows] == own_seg).astype(jnp.float32)[:, None] for tap in range(CONV)
    ]
    padded = jnp.concatenate([edge, inner], 0).astype(jnp.float32)
    conv_pre = conv_bias + sum(
        (conv_kernel[tap] * padded[tap : tap + rows] * taps[tap] for tap in range(CONV))
    )
    alive = (seg_conv[CONV - 2 : CONV - 2 + rows] == own_seg)[:, None]
    mixed_in = jax.nn.silu(conv_pre)
    mixed_low = mixed_in.astype(jnp.bfloat16)
    selected = all_sum(matmul(mixed_low, select_weight), ("tp",), jnp.bfloat16)

    selected = after(selected, block_pairs, ffn_here)
    step_low = selected[:, :STEP_RANK]
    entry = selected[:, STEP_RANK : STEP_RANK + STATE]
    readout = selected[:, STEP_RANK + STATE :]
    step_low = step_low.astype(jnp.bfloat16)
    step_weight_low = step_weight.astype(jnp.bfloat16)
    step_pre = matmul(step_low, step_weight_low) + step_bias
    step_size = jax.nn.softplus(step_pre)
    decay = -jnp.exp(decay_log).T
    rate = decay * LOG2E
    size = jnp.where(alive, step_size, FAR)
    drive = step_size * mixed_in
    entry_wide = lanes_of(entry)
    readout_wide = lanes_of(readout)
    ends = block_end(False, size, after(drive, ssm_pair), entry_wide, rate)
    place = seq_index.astype(jnp.int32).reshape(1)
    block_ends = lax.all_gather(ends, "seq")
    grad_wide = jnp.pad(after(cotangent, selected), ((0, 0), (0, -D % LANES)))
    grad_wide = spread_later(grad_wide, block_ends)
    grad_rows = grad_wide[:, :D]
    scanned, states = scan_forward(
        place, block_ends, size, drive, entry_wide, rate, readout
    )
    zgate_in = matmul(after(block_in, ends), zproj)
    ssm = scanned + skip_scale * mixed_in
    zgate = jax.nn.silu(zgate_in)
    gated = (ssm * zgate).astype(jnp.bfloat16)
    gated = after(gated, grad_wide)
    mamba_part = matmul_nt(gated, mout).astype(jnp.bfloat16)
    mamba = token_sums(mamba_part)
    seg_ext = jnp.concatenate([jnp.full((hops * rows,), -1, jnp.int32), segments])
    query_seg = lax.dynamic_slice_in_dim(segments, first_row, quarter, 0)[:, None]
    key_seg = lax.dynamic_slice_in_dim(seg_ext, base, span, 0)[None]
    offset = (hops * rows + tp_index * quarter).astype(jnp.int32).reshape(1)

    def by_head(pieces):
        value = pieces.transpose(1, 0, 2).reshape(quarter, KV_HEADS, groups, HEAD_DIM)
        return value.transpose(1, 2, 0, 3).reshape(KV_HEADS, groups * quarter, HEAD_DIM)

    def by_column(value):
        value = value.reshape(KV_HEADS, groups, quarter, HEAD_DIM).transpose(2, 0, 1, 3)
        return value.reshape(quarter, tp_count, head_cols).transpose(1, 0, 2)

    sent_pairs = after(block_pairs, block_ends)
    pieces = [after(earlier(sent_pairs, hop), gated) for hop in range(hops, 0, -1)]
    pieces.append(block_pairs)
    queries = by_head(
        after(exchange(after(query_cols, ends).reshape(tp_count, quarter, head_cols), "tp"), mamba_part)
    )
    probs, heads_out = attend(pieces, offset, query_seg, key_seg, queries)
    heads_held = received(by_column(heads_out), "tp")
    heads_back = jnp.concatenate(heads_held, 0)
    attn_part = row_major(
        matmul_nt(after(heads_back, mamba), output_weight).astype(jnp.bfloat16)
    )
    mamba = after(mamba, attn_part, ffn_w)
    attn = attn_part[:quarter].astype(jnp.float32)
    for shift in range(1, tp_count):
        back = [(s, (s - shift) % tp_count) for s in range(tp_count)]
        part = row_major(attn_part[shift * quarter : (shift + 1) * quarter])
        attn = attn + lax.ppermute(part, "tp", back).astype(jnp.float32)
    heads_cols = by_source([after(held, attn_part) for held in heads_held], "tp")
    heads_cols = heads_cols.reshape(rows, head_cols)

    scale_attn = inverse_rms(attn)
    normed_attn = attn * scale_attn
    scale_mamba = inverse_rms(mamba)
    normed_mamba = mamba * scale_mamba
    resid = stream_f + 0.5 * (normed_attn * attn_gain + normed_mamba * mamba_gain)
    scale_two = inverse_rms(resid)
    normed_two = resid * scale_two
    ffn_in = (normed_two * ffn_gain).astype(jnp.bfloat16)
    grad_other = partner(grad_wide, "seq", 0, mamba)
    grad_two = jnp.concatenate([grad_wide, grad_other], 0)[:, :D]
    ffn_wide = jnp.pad(after(ffn_in, grad_other), ((0, 0), (0, -D % LANES)))
    ffn_rows = spread(ffn_wide)
    ffn_other = partner(ffn_rows, "seq", 0)
    ffn_two = jnp.concatenate([ffn_rows, ffn_other], 0)[:, :D]
    gate_up = matmul(ffn_two, gate_up_w)
    gate, up = gate_up[:, :wide], gate_up[:, wide:]
    activated = (jax.nn.silu(gate) * up).astype(jnp.bfloat16)

    grad_out = cotangent.astype(jnp.float32)
    grad_act_low = matmul(grad_two, down_w).astype(jnp.bfloat16)
    grad_gate = (grad_act_low * up * silu_slope(gate)).astype(jnp.bfloat16)
    grad_up = (grad_act_low * jax.nn.silu(gate)).astype(jnp.bfloat16)
    grad_gate_up = jnp.concatenate([grad_gate, grad_up], 1)

    def chip_tokens(value, weight):
        sent = matmul_nt(value[rows:], weight).astype(jnp.bfloat16)
        got = partner(jnp.pad(sent, ((0, 0), (0, -D % LANES))), "seq", 0)[:, :D]
        return (matmul_nt(value[:rows], weight) + got.astype(jnp.float32)).astype(jnp.bfloat16)

    grad_ffn_part = chip_tokens(grad_gate_up, gate_up_w)
    grad_ffn_in = token_sums(grad_ffn_part)
    gate_up_late, activated_late = lax.optimization_barrier(
        (grad_gate_up, activated, grad_ffn_part)
    )[:2]
    gate_up_grads = matmul_tn(ffn_two, gate_up_late).astype(jnp.bfloat16)
    down_grads = matmul_tn(grad_two, activated_late).astype(jnp.bfloat16)
    bits = chip_bits()
    gate_up_sum = over_chips(gate_up_grads)
    down_x = Halving(down_grads, bits[::-1])
    layer_part = chip_tokens(activated_late, down_w)
    grad_ffn_in = after(grad_ffn_in, gate_up_grads, down_x.sent, layer_part)
    grad_ffn_gain = jnp.sum(grad_ffn_in * normed_two, 0)
    grad_resid = grad_out + rms_back(grad_ffn_in * ffn_gain, normed_two, scale_two)
    grad_attn_gain = 0.5 * jnp.sum(grad_resid * normed_attn, 0)
    grad_mamba_gain = 0.5 * jnp.sum(grad_resid * normed_mamba, 0)
    grad_attn = rms_back(0.5 * grad_resid * attn_gain, normed_attn, scale_attn).astype(jnp.bfloat16)
    grad_mamba = rms_back(0.5 * grad_resid * mamba_gain, normed_mamba, scale_mamba).astype(
        jnp.bfloat16
    )
    grad_mrows = spread(grad_mamba)
    grad_arows = exchange(
        jnp.broadcast_to(after(grad_attn, grad_mrows), (tp_count,) + grad_attn.shape), "tp"
    ).reshape(rows, -1)
    grad_gated = matmul(grad_mrows, mout).astype(jnp.bfloat16)
    grad_ssm = grad_gated * zgate
    grad_zgate = (grad_gated * ssm * silu_slope(zgate_in)).astype(jnp.bfloat16)
    grad_skip = jnp.sum(grad_ssm * mixed_in, 0)
    down_x.step(grad_mrows)
    backlog = block_end(True, size, grad_ssm, readout_wide, rate)
    block_backlogs = lax.all_gather(backlog, "seq")

    grad_head_cols = matmul(grad_arows, output_weight).astype(jnp.bfloat16)
    grad_heads = by_head(
        exchange(grad_head_cols.reshape(tp_count, quarter, head_cols), "tp")
    )
    grad_heads = after(grad_heads, down_x.sent)
    mrows_own, mrows_sib = row_sides(after(grad_mrows, grad_ssm))
    block_own, block_sib = row_sides(block_in)
    mout_send = core_send(mrows_sib, gated)
    zgate_send = core_send(block_sib, grad_zgate)
    grad_query, grad_window = attend_back(pieces, queries, probs, grad_heads)
    mout_held = core_sum(mrows_own, gated, mout_send, backlog)
    zgate_held = core_sum(block_own, grad_zgate, zgate_send, backlog)
    window_grad = lax.psum_scatter(after(grad_window, gate_up_sum), "tp", scatter_dimension=0, tiled=False)
    grad_query_cols = exchange(by_column(grad_query), "tp").reshape(rows, head_cols)
    head_grads = jnp.concatenate(
        [matmul_tn(grad_query_cols, block_in), matmul_tn(heads_cols, grad_arows)], 0
    )
    head_grads = head_grads.astype(jnp.bfloat16)
    head_sums = lax.psum(head_grads, "seq")
    mout_x = Halving(mout_held, bits[::-1])
    zgate_x = Halving(zgate_held, bits)
    before_scan = after(
        grad_ssm, mout_x.sent, zgate_x.sent
    )
    grad_drive, grad_size, grad_entry, grad_read, grad_rates = scan_backward(
        place, block_backlogs, size, drive, before_scan, readout_wide, rate, entry, states
    )
    grad_step = grad_size + grad_drive * mixed_in
    grad_inputs = grad_drive * step_size + grad_ssm * skip_scale
    grad_pre = grad_step * jax.nn.sigmoid(step_pre)
    grad_pre_low = grad_pre.astype(jnp.bfloat16)
    grad_low = matmul_nt(grad_pre_low, step_weight_low)
    grad_low = jnp.concatenate(
        [grad_low, grad_entry.reshape(rows, STATE), grad_read.reshape(rows, STATE)], 1
    )
    grad_decay_log = grad_rates * decay
    grad_step_bias = jnp.sum(grad_pre, 0)
    grad_skip = jnp.sum(grad_ssm * mixed_in, 0)
    grad_step_weight = matmul_tn(step_low, grad_pre_low)
    grad_selected = all_sum(grad_low, ("tp",), jnp.bfloat16).astype(jnp.bfloat16)
    moved = [
        later(after(window_grad, grad_low)[:, (hops - hop) * rows : (hops - hop + 1) * rows], hop)
        for hop in range(1, hops + 1)
    ]
    grad_selected = after(grad_selected, window_grad)
    grad_inputs = grad_inputs + matmul_nt(grad_selected, select_weight)
    grad_conv = grad_inputs * silu_slope(conv_pre)
    grad_padded = sum(
        (
            jnp.pad(conv_kernel[tap] * grad_conv * taps[tap], ((tap, CONV - 1 - tap), (0, 0)))
            for tap in range(CONV)
        )
    )
    returned = later(grad_padded[: CONV - 1].astype(jnp.bfloat16), 1).astype(jnp.float32)
    grad_inner = (
        grad_padded[CONV - 1 :] + jnp.pad(returned, ((rows - (CONV - 1), 0), (0, 0)))
    ).astype(jnp.bfloat16)
    down_sum = down_x.finish(grad_selected)
    mout_x.step(grad_selected)
    zgate_x.step(grad_selected)
    layer_sums = token_sums(after(layer_part, grad_gated), grad_low)
    layer_out = (resid + layer_sums).astype(jnp.bfloat16)
    grad_pairs = window_grad[:, hops * rows :].astype(jnp.float32)
    for part in moved:
        grad_pairs = grad_pairs + after(part, grad_conv).astype(jnp.float32)
    grad_pair_low = grad_pairs.astype(jnp.bfloat16)
    pair_grads = matmul(grad_pair_low, block_in)
    grad_inner = after(grad_inner, mout_x.sent, zgate_x.sent, pair_grads)
    proj_send = core_send(block_sib, grad_inner)
    proj_x = Halving(core_sum(block_own, grad_inner, proj_send), bits[::-1])
    tail = proj_x.sent
    pair_grads = all_sum(pair_grads, ("seq",), jnp.bfloat16, [tail] * (len(bits) + 1))
    grad_block_rest = (
        matmul_nt(grad_zgate, zproj)
        + matmul_nt(grad_query_cols, query_weight)
        + lax.dot_general(
            grad_pair_low,
            pair_weight,
            (((0,), (1,)), ((), ())),
            preferred_element_type=jnp.float32,
        )
    )
    grad_block_in = matmul_nt(after(grad_inner, proj_send), proj) + grad_block_rest
    block_in_low = row_major(grad_block_in.astype(jnp.bfloat16))
    block_in_pieces = received(block_in_low.reshape(tp_count, quarter, -1), "tp")
    proj_sum = proj_x.finish()
    grad_mixer_in = sum(
        after(piece, tail).astype(jnp.float32) for piece in block_in_pieces
    )
    stream_grad = (grad_resid + rms_back(grad_mixer_in * mixer_gain, normed_one, scale_one)).astype(
        jnp.bfloat16
    )
    grad_mixer_gain = jnp.sum(after(grad_block_in, tail) * block_normed, 0)
    gain_parts = jnp.stack([grad_mixer_gain, grad_attn_gain, grad_mamba_gain, grad_ffn_gain])
    gain_parts = all_sum(gain_parts, ("tp",), jnp.float32)
    grad_select = matmul_tn(grad_selected, mixed_low)
    grad_conv_bias = jnp.sum(grad_conv, 0)
    lone_rows = [
        jnp.sum(grad_conv * padded[tap : tap + rows] * taps[tap], 0) for tap in range(CONV)
    ] + [grad_conv_bias, grad_step_bias, grad_skip, jnp.zeros_like(grad_skip)]
    width = grad_skip.shape[0]
    gain_rows = -(-gain_parts.size // width)
    gain_flat = jnp.pad(gain_parts.reshape(-1), (0, gain_rows * width - gain_parts.size))
    aligned = [
        gain_flat.reshape(gain_rows, width),
        jnp.stack(lone_rows),
        grad_decay_log,
        jnp.pad(grad_select, ((0, -grad_select.shape[0] % HALF), (0, 0))),
        jnp.pad(grad_step_weight, ((0, -STEP_RANK % HALF), (0, 0))),
    ]
    height = sum(part.shape[0] for part in aligned)
    small, above = 0.0, 0
    for part in aligned:
        below = height - above - part.shape[0]
        small = small + jnp.pad(part.astype(jnp.float32), ((above, below), (0, 0)))
        above += part.shape[0]
    small = small.astype(jnp.bfloat16)
    small = all_sum(after(small, tail), ("seq",), jnp.bfloat16)
    mout_sum = mout_x.finish(tail)
    zgate_sum = zgate_x.finish(tail)
    gate_grad, up_grad = core_rows_back(gate_up_sum, 2, half, tail)
    (down_grad,) = core_rows_back(down_sum, 1, half, tail)
    head_sums = after(head_sums, proj_sum)
    ranks = STEP_RANK + 2 * STATE
    starts = [0]
    for part in aligned:
        starts.append(starts[-1] + part.shape[0])
    gain_totals = small[: starts[1]].reshape(-1)[: gain_parts.size].reshape(gain_parts.shape)
    conv_at, decay_at, select_at, step_at = starts[1:5]
    lone_at = conv_at + CONV
    return (
        layer_out,
        stream_grad,
        gain_totals[0],
        head_sums[:head_cols].T.astype(jnp.float32),
        pair_grads[:pair_cols].T,
        pair_grads[pair_cols:].T,
        head_sums[head_cols:].T.astype(jnp.float32),
        gain_totals[1],
        gain_totals[2],
        proj_sum,
        zgate_sum,
        small[conv_at : conv_at + CONV],
        small[lone_at],
        small[select_at : select_at + ranks].T,
        small[step_at : step_at + STEP_RANK],
        small[lone_at + 1],
        small[decay_at : decay_at + STATE].T,
        small[lone_at + 2],
        mout_sum,
        gain_totals[3],
        gate_grad,
        up_grad,
        down_grad,
    )


def solution(mesh):
    return jax.shard_map(
        on_device,
        mesh=mesh,
        in_specs=(
            P(("seq", "tp"), None),
            P(("seq", "tp"), None),
            P(),
            P(),
            P(None, "tp"),
            P(None, "tp"),
            P(None, "tp"),
            P(None, "tp"),
            P(),
            P(),
            P("seq", "tp"),
            P("seq", "tp"),
            P(None, "tp"),
            P("tp"),
            P("tp", None),
            P(None, "tp"),
            P("tp"),
            P("tp", None),
            P("tp"),
            P("seq", "tp"),
            P(),
            P("seq", "tp"),
            P("seq", "tp"),
            P("seq", "tp"),
        ),
        out_specs=(
            P(("seq", "tp"), None),
            P(("seq", "tp"), None),
            P(),
            P(None, "tp"),
            P(None, "tp"),
            P(None, "tp"),
            P(None, "tp"),
            P(),
            P(),
            P("seq", "tp"),
            P("seq", "tp"),
            P(None, "tp"),
            P("tp"),
            P("tp", None),
            P(None, "tp"),
            P("tp"),
            P("tp", None),
            P("tp"),
            P("seq", "tp"),
            P(),
            P("seq", "tp"),
            P("seq", "tp"),
            P("seq", "tp"),
        ),
        check_vma=False,
    )
```

```python
import jax
import jax.numpy as jnp
from jax import lax
from jax.experimental import pallas as pl
from jax.experimental.layout import Layout, with_layout_constraint
from jax.experimental.pallas import tpu as pltpu
from jax.sharding import PartitionSpec as P
from functools import partial

D = 1600
HEADS = 25
KV_HEADS = 5
HEAD_DIM = 64
STATE = 16
CONV = 4
STEP_RANK = 100
WINDOW = 1024
TOK_DEV = 256
EPS = 1e-06
HIGH = lax.Precision.HIGHEST
NT = (((1,), (1,)), ((), ()))
LANES = 128
HALF = 8
CHUNK = 16
LOG2E = 1.4426950408889634
LN2 = 0.6931471805599453
FAR = 1e6
VMEM_LIMIT = 48 * 1024 * 1024


def lane_groups(width):
    return [(start, min(LANES, width - start)) for start in range(0, width, LANES)]


def tiles(width):
    return [(s, w, n) for s, w in lane_groups(width) for n in range(0, STATE, HALF)]


def spread_row(ref, row):
    return ref[pl.ds(row, 1), :]


def widened(width):
    return -(-width // LANES) * LANES


def end_kernel(reverse, size_in, drive_in, vec_ref, rate_ref, out_ref, size_ref, drive_ref):
    total, width = size_in.shape
    parts = tiles(width)
    size_ref[:, :width] = size_in[...]
    drive_ref[:, :width] = drive_in[...]

    def chunk_step(chunk, held):
        held = list(held)
        at = total // CHUNK - 1 - chunk if reverse else chunk
        for k in range(CHUNK - 1, -1, -1) if reverse else range(CHUNK):
            t = at * CHUNK + k
            sizes = spread_row(size_ref, t)
            drives = spread_row(drive_ref, t)
            for i, (s, w, n) in enumerate(parts):
                size, drive = sizes[:, s : s + w], drives[:, s : s + w]
                factor = jnp.exp2(size * rate_ref[n : n + HALF, s : s + w])
                push = drive * vec_ref[t, n : n + HALF, :w]
                held[i] = factor * (held[i] + push) if reverse else factor * held[i] + push
        return tuple(held)

    held = lax.fori_loop(
        0,
        total // CHUNK,
        chunk_step,
        tuple(jnp.zeros((HALF, w), jnp.float32) for _, w, _ in parts),
    )
    for i, (s, w, n) in enumerate(parts):
        out_ref[n : n + HALF, s : s + w] = held[i]
    out_ref[STATE:, :] = jnp.broadcast_to(
        jnp.sum(size_in[...], 0, keepdims=True), (out_ref.shape[0] - STATE, width)
    )


def entering(reverse, place_ref, ends_ref, rate_ref, into_ref):
    count = ends_ref.shape[0]
    into_ref[...] = jnp.zeros(into_ref.shape, jnp.float32)

    def one(step, carry):
        at = count - 1 - step if reverse else step
        decay = jnp.exp2(rate_ref[...] * ends_ref[at, STATE : STATE + 1, :])
        into_ref[...] = decay * into_ref[...] + ends_ref[at, 0:STATE, :]
        return carry

    lax.fori_loop(0, count - 1 - place_ref[0] if reverse else place_ref[0], one, 0)


def block_mask():
    span = CHUNK * STATE
    row = lax.broadcasted_iota(jnp.int32, (CHUNK, span), 0)
    col = lax.broadcasted_iota(jnp.int32, (CHUNK, span), 1)
    return (col >= row * STATE) & (col < (row + 1) * STATE)


def repeat_matrix():
    span = CHUNK * STATE
    row = lax.broadcasted_iota(jnp.int32, (STATE, span), 0)
    col = lax.broadcasted_iota(jnp.int32, (STATE, span), 1)
    return (lax.rem(col, STATE) == row).astype(jnp.bfloat16)


def picked(vec, mine, repeat):
    wide = jnp.dot(vec.astype(jnp.bfloat16), repeat, preferred_element_type=jnp.float32)
    return jnp.where(mine, wide, 0.0).astype(jnp.bfloat16)


def scan_kernel(
    place_ref, ends_ref, size_in, drive_in, vec_ref, rate_ref, pick_ref,
    y_ref, states_ref, into_ref, size_ref, drive_ref,
):
    total, width = size_in.shape
    parts = tiles(width)
    size_ref[:, :width] = size_in[...]
    drive_ref[:, :width] = drive_in[...]
    entering(False, place_ref, ends_ref, rate_ref, into_ref)
    states_ref[0:STATE, :] = into_ref[...].astype(jnp.bfloat16)
    mine = block_mask()
    repeat = repeat_matrix()

    def chunk_step(chunk, held):
        held = list(held)
        base = chunk * (CHUNK * STATE) + STATE
        for k in range(CHUNK):
            t = chunk * CHUNK + k
            sizes = spread_row(size_ref, t)
            drives = spread_row(drive_ref, t)
            for i, (s, w, n) in enumerate(parts):
                size, drive = sizes[:, s : s + w], drives[:, s : s + w]
                factor = jnp.exp2(size * rate_ref[n : n + HALF, s : s + w])
                held[i] = factor * held[i] + drive * vec_ref[t, n : n + HALF, :w]
                if n == HALF:
                    states_ref[pl.ds(pl.multiple_of(base + k * STATE, STATE), STATE), s : s + w] = (
                        jnp.concatenate([held[i - 1], held[i]], 0).astype(jnp.bfloat16)
                    )
        rows = pl.ds(pl.multiple_of(base, STATE), CHUNK * STATE)
        y_ref[pl.ds(pl.multiple_of(chunk * CHUNK, CHUNK), CHUNK), :] = jnp.dot(
            picked(pick_ref[pl.ds(pl.multiple_of(chunk * CHUNK, CHUNK), CHUNK), :], mine, repeat),
            states_ref[rows, :],
            preferred_element_type=jnp.float32,
        )
        return tuple(held)

    lax.fori_loop(
        0,
        total // CHUNK,
        chunk_step,
        tuple(into_ref[n : n + HALF, s : s + w] for s, w, n in parts),
    )


def back_kernel(
    place_ref, ends_ref, size_in, drive_ref, grad_in, vec_ref, rate_ref, pick_ref, states_ref,
    gdrive_ref, gsize_ref, gentry_ref, gread_ref, grate_ref,
    into_ref, adj_ref, slope_ref, size_ref, grad_ref,
):
    total, width = size_in.shape
    parts = tiles(width)
    size_ref[:, :width] = size_in[...]
    grad_ref[:, :width] = grad_in[...]
    span = CHUNK * STATE
    entering(True, place_ref, ends_ref, rate_ref, into_ref)
    own = block_mask()
    repeat = repeat_matrix()
    mine = own.astype(jnp.float32)
    ones = mine.astype(jnp.bfloat16)
    grate_ref[...] = jnp.zeros(grate_ref.shape, jnp.float32)

    def chunk_step(step, held):
        held = list(held)
        chunk = total // CHUNK - 1 - step
        rates = [jnp.zeros((HALF, w), jnp.float32) for _, w, _ in parts]
        for k in range(CHUNK - 1, -1, -1):
            t = chunk * CHUNK + k
            sizes = spread_row(size_ref, t)
            grads = spread_row(grad_ref, t)
            for i, (s, w, n) in enumerate(parts):
                if n != 0:
                    continue
                size, grad = sizes[:, s : s + w], grads[:, s : s + w]
                before = states_ref[pl.ds(pl.multiple_of(t * STATE, STATE), STATE), s : s + w].astype(
                    jnp.float32
                )
                adjs, slopes = [], []
                for j in range(2):
                    n0 = j * HALF
                    rate = rate_ref[n0 : n0 + HALF, s : s + w]
                    adj = grad * vec_ref[t, n0 : n0 + HALF, :w] + held[i + j]
                    held[i + j] = jnp.exp2(size * rate) * adj
                    moved = held[i + j] * before[n0 : n0 + HALF]
                    rates[i + j] = rates[i + j] + moved * size
                    adjs.append(adj)
                    slopes.append(moved * rate)
                at = slice(k * STATE, (k + 1) * STATE)
                adj_ref[at, s : s + w] = jnp.concatenate(adjs, 0).astype(jnp.bfloat16)
                slope_ref[at, s : s + w] = jnp.concatenate(slopes, 0).astype(jnp.bfloat16)
        for i, (s, w, n) in enumerate(parts):
            grate_ref[n : n + HALF, s : s + w] += rates[i]
        here = pl.ds(pl.multiple_of(chunk * CHUNK, CHUNK), CHUNK)
        gdrive_ref[here, :] = jnp.dot(
            picked(pick_ref[here, :], own, repeat), adj_ref[...], preferred_element_type=jnp.float32
        )
        gsize_ref[here, :] = (
            jnp.dot(ones, slope_ref[...], preferred_element_type=jnp.float32) * LN2
        )
        nt = (((1,), (1,)), ((), ()))
        gentry_ref[pl.ds(chunk, 1), :] = jnp.sum(
            mine
            * lax.dot_general(
                drive_ref[here, :].astype(jnp.bfloat16), adj_ref[...], nt,
                preferred_element_type=jnp.float32,
            ),
            0, keepdims=True,
        )
        rows = pl.ds(pl.multiple_of(chunk * span + STATE, STATE), span)
        gread_ref[pl.ds(chunk, 1), :] = jnp.sum(
            mine
            * lax.dot_general(
                grad_in[here, :].astype(jnp.bfloat16), states_ref[rows, :], nt,
                preferred_element_type=jnp.float32,
            ),
            0, keepdims=True,
        )
        return tuple(held)

    lax.fori_loop(
        0,
        total // CHUNK,
        chunk_step,
        tuple(into_ref[n : n + HALF, s : s + w] for s, w, n in parts),
    )


def cost(total, width, flops, exps, extra):
    cells = total * width * STATE
    return pl.CostEstimate(
        flops=cells * flops, transcendentals=cells * exps, bytes_accessed=total * width * 12 + extra
    )


def rows_scratch(total, width):
    return [pltpu.VMEM((total, widened(width)), jnp.float32)] * 2


def kernel_call(body, outs, scratch, smem, args, estimate):
    vmem = pl.BlockSpec(memory_space=pltpu.VMEM)
    return pl.pallas_call(
        body,
        out_shape=outs,
        in_specs=[pl.BlockSpec(memory_space=pltpu.SMEM)] * smem + [vmem] * (len(args) - smem),
        out_specs=jax.tree.map(lambda _: vmem, outs),
        scratch_shapes=scratch,
        compiler_params=pltpu.CompilerParams(vmem_limit_bytes=VMEM_LIMIT),
        cost_estimate=estimate,
    )(*args)


def block_end(reverse, size, drive, vec, rate):
    total, width = size.shape
    return kernel_call(
        partial(end_kernel, reverse),
        jax.ShapeDtypeStruct((STATE + HALF, width), jnp.float32),
        rows_scratch(total, width), 0, (size, drive, vec, rate),
        cost(total, width, 5, 1, 0),
    )


def scan_forward(place, ends, size, drive, vec, rate, pick):
    total, width = size.shape
    return kernel_call(
        scan_kernel,
        (
            jax.ShapeDtypeStruct((total, width), jnp.float32),
            jax.ShapeDtypeStruct(((total + 1) * STATE, width), jnp.bfloat16),
        ),
        [pltpu.VMEM((STATE, width), jnp.float32)] + rows_scratch(total, width),
        1, (place, ends, size, drive, vec, rate, pick),
        cost(total, width, 6, 1, total * width * 32),
    )


def scan_backward(place, ends, size, drive, grad, vec, rate, pick, states):
    total, width = size.shape
    span = CHUNK * STATE
    return kernel_call(
        back_kernel,
        (
            jax.ShapeDtypeStruct((total, width), jnp.float32),
            jax.ShapeDtypeStruct((total, width), jnp.float32),
            jax.ShapeDtypeStruct((total // CHUNK, span), jnp.float32),
            jax.ShapeDtypeStruct((total // CHUNK, span), jnp.float32),
            jax.ShapeDtypeStruct((STATE, width), jnp.float32),
        ),
        [
            pltpu.VMEM((STATE, width), jnp.float32),
            pltpu.VMEM((span, width), jnp.bfloat16),
            pltpu.VMEM((span, width), jnp.bfloat16),
        ]
        + rows_scratch(total, width),
        1, (place, ends, size, drive, grad, vec, rate, pick, states),
        cost(total, width, 12, 1, total * width * 32),
    )


def lanes_of(vec):
    return jnp.broadcast_to(vec[:, :, None], vec.shape + (LANES,))


def piece_of(head, cols):
    first = lax.div(head * HEAD_DIM, cols)
    last = lax.div(head * HEAD_DIM + HEAD_DIM - 1, cols)
    return first, last, jnp.where(last > first, 1.0, 0.0).astype(jnp.bfloat16)


def pick_head(head, piece, cols, start, width):
    row = lax.broadcasted_iota(jnp.int32, (2 * cols, width), 0)
    lane = lax.broadcasted_iota(jnp.int32, (2 * cols, width), 1)
    source = piece * cols + row
    key = (row < cols) & (lane < HEAD_DIM) & (source == head * HEAD_DIM + lane)
    value = (
        (row >= cols)
        & (lane >= HEAD_DIM)
        & (source - cols == head * HEAD_DIM + lane - HEAD_DIM)
    )
    return (key | value).astype(jnp.bfloat16)


def head_pairs(head, pieces, pair_ref):
    cols = pieces[0].shape[2] // 2
    rows = pieces[0].shape[1]
    first, last, two = piece_of(head, cols)
    pick_first = pick_head(head, first, cols, 0, 2 * HEAD_DIM)
    pick_last = pick_head(head, last, cols, 0, 2 * HEAD_DIM) * two
    for block, ref in enumerate(pieces):
        pair = jnp.dot(ref[first], pick_first, preferred_element_type=jnp.float32) + jnp.dot(
            ref[last], pick_last, preferred_element_type=jnp.float32
        )
        pair_ref[block * rows : (block + 1) * rows, :] = pair.astype(jnp.bfloat16)


def attend_kernel(count, *refs):
    pieces = refs[:count]
    offset_ref, query_seg_ref, key_seg_ref, query_ref, probs_ref, heads_ref = refs[count : count + 6]
    pair_ref, score_ref = refs[count + 6 :]
    head = pl.program_id(0)
    head_pairs(head, pieces, pair_ref)
    quarter = query_seg_ref.shape[0]
    span = key_seg_ref.shape[1]
    row = lax.broadcasted_iota(jnp.int32, (quarter, span), 0)
    col = lax.broadcasted_iota(jnp.int32, (quarter, span), 1)
    distance = row + offset_ref[0] - col
    allowed = (
        (distance >= 0) & (distance < WINDOW) & (query_seg_ref[...] == key_seg_ref[...])
    )
    score_ref[...] = lax.dot_general(
        query_ref[0], pair_ref[:, :HEAD_DIM], NT, preferred_element_type=jnp.float32
    )
    for group in range(query_ref.shape[1] // quarter):
        at = slice(group * quarter, (group + 1) * quarter)
        scores = jnp.where(allowed, score_ref[at, :] * HEAD_DIM ** (-0.5), -1e30)
        raised = jnp.exp(scores - jnp.max(scores, -1, keepdims=True))
        share = 1.0 / jnp.sum(raised, -1, keepdims=True)
        probs_ref[0, at, :] = (raised * share).astype(jnp.bfloat16)
    heads_ref[0] = jnp.dot(
        probs_ref[0], pair_ref[:, HEAD_DIM:], preferred_element_type=jnp.float32
    ).astype(jnp.bfloat16)


def attend_back_kernel(count, *refs):
    pieces = refs[:count]
    query_ref, probs_ref, grad_ref, gquery_ref, gwindow_ref = refs[count : count + 5]
    pair_ref, gprob_ref, gscore_ref = refs[count + 5 :]
    head = pl.program_id(0)
    cols = pieces[0].shape[2] // 2
    first, last, two = piece_of(head, cols)
    head_pairs(head, pieces, pair_ref)
    gprob_ref[...] = lax.dot_general(
        grad_ref[0], pair_ref[:, HEAD_DIM:], NT, preferred_element_type=jnp.float32
    )
    step = HEAD_DIM
    for at in range(0, gprob_ref.shape[0], step):
        probs = probs_ref[0, at : at + step, :].astype(jnp.float32)
        both = probs * gprob_ref[at : at + step, :]
        gscore_ref[at : at + step, :] = (
            both - probs * jnp.sum(both, -1, keepdims=True)
        ).astype(jnp.bfloat16)
    scale = HEAD_DIM ** (-0.5)
    gquery_ref[0] = (
        jnp.dot(gscore_ref[...], pair_ref[:, :HEAD_DIM], preferred_element_type=jnp.float32) * scale
    ).astype(jnp.bfloat16)
    row = lax.broadcasted_iota(jnp.int32, (HEAD_DIM, HEAD_DIM), 0)
    lane = lax.broadcasted_iota(jnp.int32, (HEAD_DIM, HEAD_DIM), 1)
    unit = (row == lane).astype(jnp.bfloat16)

    def turned(value):
        return lax.dot_general(unit, value, NT, preferred_element_type=jnp.float32).astype(
            jnp.bfloat16
        )

    gkey = jnp.dot(turned(query_ref[0]), gscore_ref[...], preferred_element_type=jnp.float32)
    gvalue = jnp.dot(turned(grad_ref[0]), probs_ref[0], preferred_element_type=jnp.float32)
    gpair = jnp.concatenate([gkey * scale, gvalue], 0).astype(jnp.bfloat16)

    @pl.when(head == 0)
    def _():
        gwindow_ref[...] = jnp.zeros(gwindow_ref.shape, jnp.bfloat16)

    def add(piece, weight):
        pick = pick_head(head, piece, cols, 0, 2 * HEAD_DIM) * weight
        part = jnp.dot(pick, gpair, preferred_element_type=jnp.float32)
        gwindow_ref[piece] = (gwindow_ref[piece].astype(jnp.float32) + part).astype(jnp.bfloat16)

    add(first, jnp.ones((), jnp.bfloat16))
    add(last, two)


def whole(shape):
    return pl.BlockSpec(shape, lambda head: (0,) * len(shape))


def of_head(shape):
    return pl.BlockSpec((1,) + shape[1:], lambda head: (head,) + (0,) * (len(shape) - 1))


def attend(pieces, offset, query_seg, key_seg, queries):
    heads, rows, dim = queries.shape
    span = key_seg.shape[1]
    outs = (
        jax.ShapeDtypeStruct((heads, rows, span), jnp.bfloat16),
        jax.ShapeDtypeStruct(queries.shape, jnp.bfloat16),
    )
    return pl.pallas_call(
        partial(attend_kernel, len(pieces)),
        grid=(heads,),
        out_shape=outs,
        in_specs=[whole(p.shape) for p in pieces]
        + [pl.BlockSpec(memory_space=pltpu.SMEM), whole(query_seg.shape), whole(key_seg.shape)]
        + [of_head(queries.shape)],
        out_specs=tuple(of_head(o.shape) for o in outs),
        scratch_shapes=[
            pltpu.VMEM((span, 2 * dim), jnp.bfloat16),
            pltpu.VMEM((rows, span), jnp.float32),
        ],
        compiler_params=pltpu.CompilerParams(vmem_limit_bytes=VMEM_LIMIT),
        cost_estimate=pl.CostEstimate(
            flops=4 * heads * rows * span * dim,
            transcendentals=heads * rows * span,
            bytes_accessed=2 * heads * rows * span + 4 * queries.size,
        ),
    )(*pieces, offset, query_seg, key_seg, queries)


def attend_back(pieces, queries, probs, grads):
    heads, rows, dim = queries.shape
    span = probs.shape[2]
    outs = (
        jax.ShapeDtypeStruct(queries.shape, jnp.bfloat16),
        jax.ShapeDtypeStruct((pieces[0].shape[0], pieces[0].shape[2], span), jnp.bfloat16),
    )
    return pl.pallas_call(
        partial(attend_back_kernel, len(pieces)),
        grid=(heads,),
        out_shape=outs,
        in_specs=[whole(p.shape) for p in pieces]
        + [of_head(queries.shape), of_head(probs.shape), of_head(grads.shape)],
        out_specs=(of_head(outs[0].shape), whole(outs[1].shape)),
        scratch_shapes=[
            pltpu.VMEM((span, 2 * dim), jnp.bfloat16),
            pltpu.VMEM((rows, span), jnp.float32),
            pltpu.VMEM((rows, span), jnp.bfloat16),
        ],
        compiler_params=pltpu.CompilerParams(vmem_limit_bytes=VMEM_LIMIT),
        cost_estimate=pl.CostEstimate(
            flops=8 * heads * rows * span * dim,
            transcendentals=0,
            bytes_accessed=4 * heads * rows * span,
        ),
    )(*pieces, queries, probs, grads)


def passed_along(value, axis, steps):
    count = lax.axis_size(axis)
    first, last = (max(0, -steps), min(count, count - steps))
    return lax.ppermute(value, axis, [(source, source + steps) for source in range(first, last)])


def after(value, *others):
    return lax.optimization_barrier((value, *others))[0]


def partner(value, axis, bit, when=None):
    count = lax.axis_size(axis)
    got = lax.ppermute(value, axis, [(s, s ^ (1 << bit)) for s in range(count)])
    return got if when is None else after(got, when)


def all_sum(value, axes, kind, whens=()):
    whens = list(whens)
    for axis in axes:
        count = lax.axis_size(axis)
        bits = count.bit_length() - 1
        if count != 1 << bits:
            value = lax.psum(value, axis)
            continue
        for bit in range(bits):
            low = value.astype(kind)
            got = partner(low, axis, bit, whens.pop(0) if whens else None)
            value = low.astype(jnp.float32) + got.astype(jnp.float32)
    return value


class Halving:
    def __init__(self, value, order):
        self.order = list(order)
        self.left = sorted(order, reverse=True)
        self.split(value.astype(jnp.bfloat16).reshape([2] * len(self.left) + [-1, value.shape[1]]))

    def split(self, held):
        self.bit = self.order.pop(0)
        axis = self.left.index(self.bit)
        self.left.remove(self.bit)
        mine = (lax.axis_index("seq") >> self.bit) & 1
        self.sent = lax.dynamic_index_in_dim(held, 1 - mine, axis, False)
        self.kept = lax.dynamic_index_in_dim(held, mine, axis, False)

    def step(self, when=None):
        got = partner(self.sent, "seq", self.bit, when)
        total = self.kept.astype(jnp.float32) + got.astype(jnp.float32)
        if self.order:
            self.split(total.astype(jnp.bfloat16))
        return total

    def finish(self, when=None):
        while self.order:
            self.step(when)
        return self.step(when)


def chip_bits():
    return list(range(1, lax.axis_size("seq").bit_length() - 1))


def row_sides(value):
    blocks = lax.axis_size("seq")
    turned = value.T.reshape(blocks // 2, 2, -1, value.shape[0])
    mine = lax.axis_index("seq") & 1
    return [
        lax.dynamic_index_in_dim(turned, side, 1, False).reshape(-1, value.shape[0])
        for side in (mine, 1 - mine)
    ]


def core_send(left_sib, right):
    return matmul(left_sib, right).astype(jnp.bfloat16)


def core_sum(left_own, right, send, when=None):
    got = partner(send, "seq", 0, when)
    return (matmul(left_own, right) + got.astype(jnp.float32)).astype(jnp.bfloat16)


def first_core():
    return (lax.axis_index("seq") & 1) == 0


def core_order(mine, other):
    first = first_core()
    return jnp.where(first, mine, other), jnp.where(first, other, mine)


def chip_groups():
    count = lax.axis_size("seq")
    return [[c for c in range(count) if c % 2 == p] for p in range(2)]


def core_columns(weights, padded_to):
    pad = [(0, 0), (0, padded_to - weights[0].shape[1] // 2)]
    low = jnp.concatenate([jnp.pad(w[:, : w.shape[1] // 2], pad) for w in weights], 1)
    high = jnp.concatenate([jnp.pad(w[:, w.shape[1] // 2 :], pad) for w in weights], 1)
    first = first_core()
    mine, other = jnp.where(first, low, high), jnp.where(first, high, low)
    return jnp.concatenate(core_order(mine, partner(other, "seq", 0)), 0)


def core_rows_back(held, count, width, when):
    mine = lax.axis_index("seq") & 1
    both = held.reshape(2, -1, held.shape[-1])
    kept = lax.dynamic_index_in_dim(both, mine, 0, False)
    sent = lax.dynamic_index_in_dim(both, 1 - mine, 0, False).astype(jnp.bfloat16)
    low, high = core_order(kept, partner(sent, "seq", 0, when).astype(kept.dtype))
    step = held.shape[-1] // count
    return [
        jnp.concatenate([low[:, at : at + width], high[:, at : at + width]], 1).astype(jnp.float32)
        for at in range(0, count * step, step)
    ]


def received(pieces, axis):
    count = lax.axis_size(axis)
    place = lax.axis_index(axis)
    held = []
    for shift in range(count):
        sent = row_major(lax.dynamic_index_in_dim(pieces, (place + shift) % count, 0, False))
        held.append(
            lax.ppermute(sent, axis, [(s, (s + shift) % count) for s in range(count)])
            if shift
            else sent
        )
    return held


def by_source(held, axis):
    count = lax.axis_size(axis)
    place = lax.axis_index(axis)
    held = jnp.stack(held)
    return jnp.stack(
        [
            lax.dynamic_index_in_dim(held, (place - source) % count, 0, False)
            for source in range(count)
        ]
    )


def exchange(pieces, axis):
    return lax.all_to_all(pieces, axis, 0, 0, tiled=True)


def spread_direct(value, axis, when):
    count = lax.axis_size(axis)
    value = row_major(value)
    held = [value]
    for shift in range(1, count):
        got = lax.ppermute(value, axis, [(s, (s + shift) % count) for s in range(count)])
        held.append(after(got, when))
    return by_source(held, axis)


def inverse_rms(value):
    return lax.rsqrt(jnp.mean(value * value, -1, keepdims=True) + EPS)


def rms_back(grad_normed, normed, scale):
    return scale * (grad_normed - normed * jnp.mean(grad_normed * normed, -1, keepdims=True))


def silu_slope(value):
    sigma = jax.nn.sigmoid(value)
    return sigma * (1.0 + value * (1.0 - sigma))


def matmul(left, right):
    return jnp.dot(left, right, preferred_element_type=jnp.float32)


def matmul_nt(left, right):
    return lax.dot_general(
        left, right, (((1,), (1,)), ((), ())), preferred_element_type=jnp.float32
    )


def row_major(value):
    order = tuple(range(value.ndim))
    return with_layout_constraint(value, Layout(major_to_minor=order))


def matmul_tn(left, right):
    return lax.dot_general(
        left, right, (((0,), (0,)), ((), ())), preferred_element_type=jnp.float32
    )


def on_device(
    stream,
    cotangent,
    segments,
    mixer_gain,
    query_weight,
    key_weight,
    value_weight,
    output_weight,
    attn_gain,
    mamba_gain,
    inner_proj,
    inner_gate,
    conv_kernel,
    conv_bias,
    select_weight,
    step_weight,
    step_bias,
    decay_log,
    skip_scale,
    mamba_out,
    ffn_gain,
    ffn_gate,
    ffn_up,
    ffn_down,
):
    seq_count = lax.axis_size("seq")
    tp_count = lax.axis_size("tp")
    seq_index = lax.axis_index("seq")
    tp_index = lax.axis_index("tp")
    quarter = stream.shape[0]
    rows = TOK_DEV
    hops = (WINDOW + TOK_DEV - 1) // TOK_DEV
    span = (hops + 1) * rows
    key_width = KV_HEADS * HEAD_DIM
    groups = HEADS // KV_HEADS
    head_cols = query_weight.shape[1]
    pair_cols = key_weight.shape[1]

    def spread(value):
        return lax.all_gather(value, "tp", axis=0, tiled=True)

    def spread_later(value, when):
        return spread_direct(value, "tp", when).reshape(rows, -1)

    def token_sums(value, when=None):
        value = row_major(value.astype(jnp.bfloat16))
        pieces = received(value.reshape(tp_count, quarter, -1), "tp")
        if when is not None:
            pieces = [after(piece, when) for piece in pieces]
        return sum(piece.astype(jnp.float32) for piece in pieces)

    def token_sums_late(value):
        pieces = exchange(value.astype(jnp.bfloat16).reshape(tp_count, quarter, -1), "tp")
        return jnp.sum(pieces.astype(jnp.float32), 0)

    def earlier(value, hop):
        return passed_along(value, "seq", hop)

    def later(value, hop):
        return passed_along(value, "seq", -hop)

    def whole_rows(weight):
        return lax.all_gather(weight, "seq", axis=0, tiled=True)

    def from_chips(value):
        return lax.all_gather(
            value, "seq", axis=0, tiled=True, axis_index_groups=chip_groups()
        )

    def over_chips(value):
        return lax.psum_scatter(
            value, "seq", scatter_dimension=0, tiled=True, axis_index_groups=chip_groups()
        )

    def own_cols(value):
        return value.reshape(quarter, tp_count, -1).transpose(1, 0, 2)

    proj = whole_rows(inner_proj)
    wide_cols = -(-inner_gate.shape[1] // LANES) * LANES
    pad_cols = ((0, 0), (0, wide_cols - inner_gate.shape[1]))
    ssm_pair = whole_rows(
        jnp.concatenate([jnp.pad(inner_gate, pad_cols), jnp.pad(mamba_out, pad_cols)], 1)
    )
    zproj = ssm_pair[:, : inner_gate.shape[1]]
    mout = ssm_pair[:, wide_cols : wide_cols + mamba_out.shape[1]]
    block_stream = spread(stream)
    (
        block_stream, stream, cotangent, segments, key_weight, value_weight, conv_kernel,
        conv_bias, decay_log, ffn_gate, ffn_up, ffn_down,
    ) = lax.optimization_barrier(
        (
            block_stream, stream, cotangent, segments, key_weight, value_weight, conv_kernel,
            conv_bias, decay_log, ffn_gate, ffn_up, ffn_down,
        )
    )
    block_stream = block_stream.astype(jnp.float32)
    base = seq_index * rows
    first_row = base + tp_index * quarter
    stream_f = stream.astype(jnp.float32)
    scale_one = inverse_rms(stream_f)
    normed_one = stream_f * scale_one
    block_normed = block_stream * inverse_rms(block_stream)
    block_in = (block_normed * mixer_gain).astype(jnp.bfloat16)
    pair_weight = jnp.concatenate([key_weight, value_weight], 1)
    query_cols = matmul(block_in, query_weight).astype(jnp.bfloat16)
    pair_part = matmul(block_in, pair_weight).astype(jnp.bfloat16)
    block_late = after(block_in, query_cols, pair_part)
    inner = matmul(block_late, proj).astype(jnp.bfloat16)
    half = ffn_gate.shape[1] // 2
    wide = -(-half // 256) * 256
    ffn_here = core_columns([after(ffn_gate, inner), ffn_up, ffn_down], wide)
    ffn_w = from_chips(ffn_here)
    gate_up_w, down_w = ffn_w[:, : 2 * wide], ffn_w[:, 2 * wide :]
    block_pairs = spread_direct(pair_part, "tp", inner)
    edge = earlier(inner[rows - (CONV - 1) :], 1)
    seg_conv = lax.dynamic_slice_in_dim(
        jnp.concatenate([jnp.full((CONV - 1,), -1, jnp.int32), segments]), base, rows + CONV - 1, 0
    )
    own_seg = seg_conv[CONV - 1 :]
    taps = [
        (seg_conv[tap : tap + rows] == own_seg).astype(jnp.float32)[:, None] for tap in range(CONV)
    ]
    padded = jnp.concatenate([edge, inner], 0).astype(jnp.float32)
    conv_pre = conv_bias + sum(
        (conv_kernel[tap] * padded[tap : tap + rows] * taps[tap] for tap in range(CONV))
    )
    alive = (seg_conv[CONV - 2 : CONV - 2 + rows] == own_seg)[:, None]
    mixed_in = jax.nn.silu(conv_pre)
    mixed_low = mixed_in.astype(jnp.bfloat16)
    selected = all_sum(matmul(mixed_low, select_weight), ("tp",), jnp.bfloat16)

    selected = after(selected, block_pairs, ffn_here)
    step_low = selected[:, :STEP_RANK]
    entry = selected[:, STEP_RANK : STEP_RANK + STATE]
    readout = selected[:, STEP_RANK + STATE :]
    step_low = step_low.astype(jnp.bfloat16)
    step_weight_low = step_weight.astype(jnp.bfloat16)
    step_pre = matmul(step_low, step_weight_low) + step_bias
    step_size = jax.nn.softplus(step_pre)
    decay = -jnp.exp(decay_log).T
    rate = decay * LOG2E
    size = jnp.where(alive, step_size, FAR)
    drive = step_size * mixed_in
    entry_wide = lanes_of(entry)
    readout_wide = lanes_of(readout)
    ends = block_end(False, size, after(drive, ssm_pair), entry_wide, rate)
    place = seq_index.astype(jnp.int32).reshape(1)
    block_ends = lax.all_gather(ends, "seq")
    grad_wide = jnp.pad(after(cotangent, selected), ((0, 0), (0, -D % LANES)))
    grad_wide = spread_later(grad_wide, block_ends)
    grad_rows = grad_wide[:, :D]
    scanned, states = scan_forward(
        place, block_ends, size, drive, entry_wide, rate, readout
    )
    zgate_in = matmul(after(block_in, ends), zproj)
    ssm = scanned + skip_scale * mixed_in
    zgate = jax.nn.silu(zgate_in)
    gated = (ssm * zgate).astype(jnp.bfloat16)
    gated = after(gated, grad_wide)
    mamba_part = matmul_nt(gated, mout).astype(jnp.bfloat16)
    mamba = token_sums(mamba_part)
    seg_ext = jnp.concatenate([jnp.full((hops * rows,), -1, jnp.int32), segments])
    query_seg = lax.dynamic_slice_in_dim(segments, first_row, quarter, 0)[:, None]
    key_seg = lax.dynamic_slice_in_dim(seg_ext, base, span, 0)[None]
    offset = (hops * rows + tp_index * quarter).astype(jnp.int32).reshape(1)

    def by_head(pieces):
        value = pieces.transpose(1, 0, 2).reshape(quarter, KV_HEADS, groups, HEAD_DIM)
        return value.transpose(1, 2, 0, 3).reshape(KV_HEADS, groups * quarter, HEAD_DIM)

    def by_column(value):
        value = value.reshape(KV_HEADS, groups, quarter, HEAD_DIM).transpose(2, 0, 1, 3)
        return value.reshape(quarter, tp_count, head_cols).transpose(1, 0, 2)

    sent_pairs = after(block_pairs, block_ends)
    pieces = [after(earlier(sent_pairs, hop), gated) for hop in range(hops, 0, -1)]
    pieces.append(block_pairs)
    queries = by_head(
        after(exchange(after(query_cols, ends).reshape(tp_count, quarter, head_cols), "tp"), mamba_part)
    )
    probs, heads_out = attend(pieces, offset, query_seg, key_seg, queries)
    heads_held = received(by_column(heads_out), "tp")
    heads_back = jnp.concatenate(heads_held, 0)
    attn_part = row_major(
        matmul_nt(after(heads_back, mamba), output_weight).astype(jnp.bfloat16)
    )
    mamba = after(mamba, attn_part, ffn_w)
    attn = attn_part[:quarter].astype(jnp.float32)
    for shift in range(1, tp_count):
        back = [(s, (s - shift) % tp_count) for s in range(tp_count)]
        part = row_major(attn_part[shift * quarter : (shift + 1) * quarter])
        attn = attn + lax.ppermute(part, "tp", back).astype(jnp.float32)
    heads_cols = by_source([after(held, attn_part) for held in heads_held], "tp")
    heads_cols = heads_cols.reshape(rows, head_cols)

    scale_attn = inverse_rms(attn)
    normed_attn = attn * scale_attn
    scale_mamba = inverse_rms(mamba)
    normed_mamba = mamba * scale_mamba
    resid = stream_f + 0.5 * (normed_attn * attn_gain + normed_mamba * mamba_gain)
    scale_two = inverse_rms(resid)
    normed_two = resid * scale_two
    ffn_in = (normed_two * ffn_gain).astype(jnp.bfloat16)
    grad_other = partner(grad_wide, "seq", 0, mamba)
    grad_two = jnp.concatenate([grad_wide, grad_other], 0)[:, :D]
    ffn_wide = jnp.pad(after(ffn_in, grad_other), ((0, 0), (0, -D % LANES)))
    ffn_rows = spread(ffn_wide)
    ffn_other = partner(ffn_rows, "seq", 0)
    ffn_two = jnp.concatenate([ffn_rows, ffn_other], 0)[:, :D]
    gate_up = matmul(ffn_two, gate_up_w)
    gate, up = gate_up[:, :wide], gate_up[:, wide:]
    activated = (jax.nn.silu(gate) * up).astype(jnp.bfloat16)

    grad_out = cotangent.astype(jnp.float32)
    grad_act_low = matmul(grad_two, down_w).astype(jnp.bfloat16)
    grad_gate = (grad_act_low * up * silu_slope(gate)).astype(jnp.bfloat16)
    grad_up = (grad_act_low * jax.nn.silu(gate)).astype(jnp.bfloat16)
    grad_gate_up = jnp.concatenate([grad_gate, grad_up], 1)

    def chip_tokens(value, weight):
        sent = matmul_nt(value[rows:], weight).astype(jnp.bfloat16)
        got = partner(jnp.pad(sent, ((0, 0), (0, -D % LANES))), "seq", 0)[:, :D]
        return (matmul_nt(value[:rows], weight) + got.astype(jnp.float32)).astype(jnp.bfloat16)

    grad_ffn_part = chip_tokens(grad_gate_up, gate_up_w)
    grad_ffn_in = token_sums(grad_ffn_part)
    gate_up_late, activated_late = lax.optimization_barrier(
        (grad_gate_up, activated, grad_ffn_part)
    )[:2]
    gate_up_grads = matmul_tn(ffn_two, gate_up_late).astype(jnp.bfloat16)
    down_grads = matmul_tn(grad_two, activated_late).astype(jnp.bfloat16)
    bits = chip_bits()
    gate_up_sum = over_chips(gate_up_grads)
    down_x = Halving(down_grads, bits[::-1])
    layer_part = chip_tokens(activated_late, down_w)
    grad_ffn_in = after(grad_ffn_in, gate_up_grads, down_x.sent, layer_part)
    grad_ffn_gain = jnp.sum(grad_ffn_in * normed_two, 0)
    grad_resid = grad_out + rms_back(grad_ffn_in * ffn_gain, normed_two, scale_two)
    grad_attn_gain = 0.5 * jnp.sum(grad_resid * normed_attn, 0)
    grad_mamba_gain = 0.5 * jnp.sum(grad_resid * normed_mamba, 0)
    grad_attn = rms_back(0.5 * grad_resid * attn_gain, normed_attn, scale_attn).astype(jnp.bfloat16)
    grad_mamba = rms_back(0.5 * grad_resid * mamba_gain, normed_mamba, scale_mamba).astype(
        jnp.bfloat16
    )
    grad_mrows = spread(grad_mamba)
    grad_arows = exchange(
        jnp.broadcast_to(after(grad_attn, grad_mrows), (tp_count,) + grad_attn.shape), "tp"
    ).reshape(rows, -1)
    grad_gated = matmul(grad_mrows, mout).astype(jnp.bfloat16)
    grad_ssm = grad_gated * zgate
    grad_zgate = (grad_gated * ssm * silu_slope(zgate_in)).astype(jnp.bfloat16)
    grad_skip = jnp.sum(grad_ssm * mixed_in, 0)
    down_x.step(grad_mrows)
    backlog = block_end(True, size, grad_ssm, readout_wide, rate)
    block_backlogs = lax.all_gather(backlog, "seq")

    grad_head_cols = matmul(grad_arows, output_weight).astype(jnp.bfloat16)
    grad_heads = by_head(
        exchange(grad_head_cols.reshape(tp_count, quarter, head_cols), "tp")
    )
    grad_heads = after(grad_heads, down_x.sent)
    mrows_own, mrows_sib = row_sides(after(grad_mrows, grad_ssm))
    block_own, block_sib = row_sides(block_in)
    mout_send = core_send(mrows_sib, gated)
    zgate_send = core_send(block_sib, grad_zgate)
    grad_query, grad_window = attend_back(pieces, queries, probs, grad_heads)
    mout_held = core_sum(mrows_own, gated, mout_send, backlog)
    zgate_held = core_sum(block_own, grad_zgate, zgate_send, backlog)
    window_grad = lax.psum_scatter(after(grad_window, gate_up_sum), "tp", scatter_dimension=0, tiled=False)
    grad_query_cols = exchange(by_column(grad_query), "tp").reshape(rows, head_cols)
    head_grads = jnp.concatenate(
        [matmul_tn(grad_query_cols, block_in), matmul_tn(heads_cols, grad_arows)], 0
    )
    head_grads = head_grads.astype(jnp.bfloat16)
    head_sums = lax.psum(head_grads, "seq")
    mout_x = Halving(mout_held, bits[::-1])
    zgate_x = Halving(zgate_held, bits)
    before_scan = after(
        grad_ssm, mout_x.sent, zgate_x.sent
    )
    grad_drive, grad_size, grad_entry, grad_read, grad_rates = scan_backward(
        place, block_backlogs, size, drive, before_scan, readout_wide, rate, entry, states
    )
    grad_step = grad_size + grad_drive * mixed_in
    grad_inputs = grad_drive * step_size + grad_ssm * skip_scale
    grad_pre = grad_step * jax.nn.sigmoid(step_pre)
    grad_pre_low = grad_pre.astype(jnp.bfloat16)
    grad_low = matmul_nt(grad_pre_low, step_weight_low)
    grad_low = jnp.concatenate(
        [grad_low, grad_entry.reshape(rows, STATE), grad_read.reshape(rows, STATE)], 1
    )
    grad_decay_log = grad_rates * decay
    grad_step_bias = jnp.sum(grad_pre, 0)
    grad_skip = jnp.sum(grad_ssm * mixed_in, 0)
    grad_step_weight = matmul_tn(step_low, grad_pre_low)
    grad_selected = all_sum(grad_low, ("tp",), jnp.bfloat16).astype(jnp.bfloat16)
    moved = [
        later(after(window_grad, grad_low)[:, (hops - hop) * rows : (hops - hop + 1) * rows], hop)
        for hop in range(1, hops + 1)
    ]
    grad_selected = after(grad_selected, window_grad)
    grad_inputs = grad_inputs + matmul_nt(grad_selected, select_weight)
    grad_conv = grad_inputs * silu_slope(conv_pre)
    grad_padded = sum(
        (
            jnp.pad(conv_kernel[tap] * grad_conv * taps[tap], ((tap, CONV - 1 - tap), (0, 0)))
            for tap in range(CONV)
        )
    )
    returned = later(grad_padded[: CONV - 1].astype(jnp.bfloat16), 1).astype(jnp.float32)
    grad_inner = (
        grad_padded[CONV - 1 :] + jnp.pad(returned, ((rows - (CONV - 1), 0), (0, 0)))
    ).astype(jnp.bfloat16)
    down_sum = down_x.finish(grad_selected)
    mout_x.step(grad_selected)
    zgate_x.step(grad_selected)
    layer_sums = token_sums(after(layer_part, grad_gated), grad_low)
    layer_out = (resid + layer_sums).astype(jnp.bfloat16)
    grad_pairs = window_grad[:, hops * rows :].astype(jnp.float32)
    for part in moved:
        grad_pairs = grad_pairs + after(part, grad_conv).astype(jnp.float32)
    grad_pair_low = grad_pairs.astype(jnp.bfloat16)
    pair_grads = matmul(grad_pair_low, block_in)
    grad_inner = after(grad_inner, mout_x.sent, zgate_x.sent, pair_grads)
    proj_send = core_send(block_sib, grad_inner)
    proj_x = Halving(core_sum(block_own, grad_inner, proj_send), bits[::-1])
    tail = proj_x.sent
    pair_grads = all_sum(pair_grads, ("seq",), jnp.bfloat16, [tail] * (len(bits) + 1))
    grad_block_rest = (
        matmul_nt(grad_zgate, zproj)
        + matmul_nt(grad_query_cols, query_weight)
        + lax.dot_general(
            grad_pair_low,
            pair_weight,
            (((0,), (1,)), ((), ())),
            preferred_element_type=jnp.float32,
        )
    )
    grad_block_in = matmul_nt(after(grad_inner, proj_send), proj) + grad_block_rest
    block_in_low = row_major(grad_block_in.astype(jnp.bfloat16))
    block_in_pieces = received(block_in_low.reshape(tp_count, quarter, -1), "tp")
    proj_sum = proj_x.finish()
    grad_mixer_gain = jnp.sum(after(grad_block_in, tail) * block_normed, 0)
    gain_parts = jnp.stack([grad_mixer_gain, grad_attn_gain, grad_mamba_gain, grad_ffn_gain])
    gain_parts = all_sum(gain_parts, ("tp",), jnp.float32)
    grad_select = matmul_tn(after(grad_selected, tail), mixed_low)
    grad_conv_bias = jnp.sum(grad_conv, 0)
    lone_rows = [
        jnp.sum(grad_conv * padded[tap : tap + rows] * taps[tap], 0) for tap in range(CONV)
    ] + [grad_conv_bias, grad_step_bias, grad_skip, jnp.zeros_like(grad_skip)]
    width = grad_skip.shape[0]
    gain_rows = -(-gain_parts.size // width)
    gain_flat = jnp.pad(gain_parts.reshape(-1), (0, gain_rows * width - gain_parts.size))
    aligned = [
        gain_flat.reshape(gain_rows, width),
        jnp.stack(lone_rows),
        grad_decay_log,
        jnp.pad(grad_select, ((0, -grad_select.shape[0] % HALF), (0, 0))),
        jnp.pad(grad_step_weight, ((0, -STEP_RANK % HALF), (0, 0))),
    ]
    height = sum(part.shape[0] for part in aligned)
    small, above = 0.0, 0
    for part in aligned:
        below = height - above - part.shape[0]
        small = small + jnp.pad(part.astype(jnp.float32), ((above, below), (0, 0)))
        above += part.shape[0]
    small = small.astype(jnp.bfloat16)
    small = all_sum(after(small, tail), ("seq",), jnp.bfloat16)
    mout_sum = mout_x.finish(tail)
    zgate_sum = zgate_x.finish(tail)
    gate_grad, up_grad = core_rows_back(gate_up_sum, 2, half, tail)
    (down_grad,) = core_rows_back(down_sum, 1, half, tail)
    grad_mixer_in = sum(
        after(piece, gate_grad, up_grad, down_grad, mout_sum, zgate_sum).astype(jnp.float32) for piece in block_in_pieces
    )
    stream_grad = (grad_resid + rms_back(grad_mixer_in * mixer_gain, normed_one, scale_one)).astype(
        jnp.bfloat16
    )
    head_sums = after(head_sums, proj_sum)
    ranks = STEP_RANK + 2 * STATE
    starts = [0]
    for part in aligned:
        starts.append(starts[-1] + part.shape[0])
    gain_totals = small[: starts[1]].reshape(-1)[: gain_parts.size].reshape(gain_parts.shape)
    conv_at, decay_at, select_at, step_at = starts[1:5]
    lone_at = conv_at + CONV
    return (
        layer_out,
        stream_grad,
        gain_totals[0],
        head_sums[:head_cols].T.astype(jnp.float32),
        pair_grads[:pair_cols].T,
        pair_grads[pair_cols:].T,
        head_sums[head_cols:].T.astype(jnp.float32),
        gain_totals[1],
        gain_totals[2],
        proj_sum,
        zgate_sum,
        small[conv_at : conv_at + CONV],
        small[lone_at],
        small[select_at : select_at + ranks].T,
        small[step_at : step_at + STEP_RANK],
        small[lone_at + 1],
        small[decay_at : decay_at + STATE].T,
        small[lone_at + 2],
        mout_sum,
        gain_totals[3],
        gate_grad,
        up_grad,
        down_grad,
    )


def solution(mesh):
    return jax.shard_map(
        on_device,
        mesh=mesh,
        in_specs=(
            P(("seq", "tp"), None),
            P(("seq", "tp"), None),
            P(),
            P(),
            P(None, "tp"),
            P(None, "tp"),
            P(None, "tp"),
            P(None, "tp"),
            P(),
            P(),
            P("seq", "tp"),
            P("seq", "tp"),
            P(None, "tp"),
            P("tp"),
            P("tp", None),
            P(None, "tp"),
            P("tp"),
            P("tp", None),
            P("tp"),
            P("seq", "tp"),
            P(),
            P("seq", "tp"),
            P("seq", "tp"),
            P("seq", "tp"),
        ),
        out_specs=(
            P(("seq", "tp"), None),
            P(("seq", "tp"), None),
            P(),
            P(None, "tp"),
            P(None, "tp"),
            P(None, "tp"),
            P(None, "tp"),
            P(),
            P(),
            P("seq", "tp"),
            P("seq", "tp"),
            P(None, "tp"),
            P("tp"),
            P("tp", None),
            P(None, "tp"),
            P("tp"),
            P("tp", None),
            P("tp"),
            P("seq", "tp"),
            P(),
            P("seq", "tp"),
            P("seq", "tp"),
            P("seq", "tp"),
        ),
        check_vma=False,
    )
```
